32 devices in a mesh: grp: 4 (over z), node: 8 (over y, x, core).
Axes of the slice: x: 2, y: 2, z: 4, core: 2. Of those that a mesh axis runs over, the one named last changes fastest.
Arguments:
- features: bfloat16 [8, 4096, 100], P('grp', 'node')
- adjacency: bfloat16 [8, 4096, 4096], P('grp', 'node'), as said below
- labels: int32 [8, 4096], P('grp', 'node'), may hold values from 0 to 46
- train_mask: int32 [8, 4096], P('grp', 'node'), may hold values from 0 to 1, as said below
- input_weight: float32 [100, 256], P(None, 'grp'), may hold values from -0.625 to 0.625
- input_moment: float32 [100, 256], P(None, 'grp'), may hold values from -0.125 to 0.125
- conv_weight: float32 [2, 512, 256], P(None, None, 'grp'), may hold values from -0.25 to 0.25
- conv_moment: float32 [2, 512, 256], P(None, None, 'grp'), may hold values from -0.125 to 0.125
- head_weight: float32 [256, 47], replicated, may hold values from -0.375 to 0.375
- head_first: float32 [256, 47], replicated, may hold values from -0.013671875 to 0.013671875
- head_second: float32 [256, 47], replicated, may hold values from 3.2348632e-06 to 1.2817382e-05
- head_bias: float32 [47], replicated, may hold values from -3 to 3
- bias_first: float32 [47], replicated, may hold values from -0.013671875 to 0.013671875
- bias_second: float32 [47], replicated, may hold values from 3.2348632e-06 to 1.2817382e-05
- norm_params: float32 [2, 2, 256], replicated
- norm_first: float32 [2, 2, 256], replicated, may hold values from -0.013671875 to 0.013671875
- norm_second: float32 [2, 2, 256], replicated, may hold values from 3.2348632e-06 to 1.2817382e-05
Outputs:
- loss_parts: float32 [2], replicated
- input_new: float32 [100, 256], P(None, 'grp')
- input_moment_new: float32 [100, 256], P(None, 'grp')
- conv_new: float32 [2, 512, 256], P(None, None, 'grp')
- conv_moment_new: float32 [2, 512, 256], P(None, None, 'grp')
- head_new: float32 [256, 47], replicated
- head_first_new: float32 [256, 47], replicated
- head_second_new: float32 [256, 47], replicated
- bias_new: float32 [47], replicated
- bias_first_new: float32 [47], replicated
- bias_second_new: float32 [47], replicated
- norm_new: float32 [2, 2, 256], replicated
- norm_first_new: float32 [2, 2, 256], replicated
- norm_second_new: float32 [2, 2, 256], replicated
The draws below stay inside these ranges and needn't reach their ends.
Inputs may be any that keep to these rules, and one draw needn't show every extreme that they name: adjacency[s] equals its own transpose for every subgraph s; entries are zero or positive. `train_mask`: 0 or 1; the first node of every subgraph is a training node.
All inputs are finite; a program needn't handle non-finite values.
Results may differ from the reference program's by a relative error of at most 0.003.
Values may be sent and summed in bfloat16 or wider, within the bound.
A program may use at most 192 MiB of HBM per device.

```python
import math
import jax
import jax.numpy as jnp
from jax import lax

F_IN = 100
HID = 256
CLS = 47
LAYERS = 2
NODE_DEV = 512
DEG = 64
NS_STEPS = 5
STEP = 10
N_SUB = 4096
SUBS_ALL = 8
N_GRP = 4


def draw_features(key, part):
    key = jax.random.fold_in(key, 11)
    position = jnp.arange(N_SUB, dtype=jnp.float32) / N_SUB
    base = jax.random.normal(key, (SUBS_ALL, N_SUB, F_IN), jnp.float32)
    factor = 1.0 + 2.0 * position
    return (base * factor[None, :, None]).astype(jnp.bfloat16)


def draw_adjacency(key, part):
    key = jax.random.fold_in(key, 12)
    key_tile, key_pick, key_value = jax.random.split(key, 3)
    blocks = N_SUB // NODE_DEV
    tiles = jax.random.uniform(key_tile, (SUBS_ALL, blocks, blocks), jnp.float32, 0.25, 1.75)
    tiles = jnp.triu(tiles) + jnp.swapaxes(jnp.triu(tiles, 1), 1, 2)
    tiles = jnp.repeat(jnp.repeat(tiles, NODE_DEV, 1), NODE_DEV, 2)
    chance = jnp.minimum(1.0, DEG * tiles / N_SUB)
    picks = jax.random.uniform(key_pick, (SUBS_ALL, N_SUB, N_SUB), jnp.float32)
    values = jnp.exp(jax.random.uniform(key_value, (SUBS_ALL, N_SUB, N_SUB), jnp.float32, -0.69, 0.69))
    raw = jnp.where(picks < chance, values, 0.0) / DEG
    whole = jnp.triu(raw) + jnp.swapaxes(jnp.triu(raw, 1), 1, 2)
    return whole.astype(jnp.bfloat16)


def draw_train_mask(key, part):
    key = jax.random.fold_in(key, 13)
    votes = jax.random.randint(key, (SUBS_ALL, N_SUB), 0, 100)
    rows = jnp.arange(N_SUB, dtype=jnp.int32)
    groups = jnp.arange(SUBS_ALL, dtype=jnp.int32)
    limit = 15 + 35 * rows[None, :] // N_SUB + 35 * groups[:, None] // SUBS_ALL
    chosen = (votes < limit) | (rows[None, :] == 0)
    return chosen.astype(jnp.int32)


def draw_norm_params(key, part):
    key = jax.random.fold_in(key, 14)
    key_gain, key_shift = jax.random.split(key)
    gains = jnp.exp(jax.random.uniform(key_gain, (LAYERS, HID), jnp.float32, -0.35, 0.35))
    shifts = 0.2 * jax.random.normal(key_shift, (LAYERS, HID), jnp.float32)
    return jnp.stack([gains, shifts], 1)


def plant(drawn, rng, least, largest):
    longest = drawn.shape.index(max(drawn.shape))
    spots = []
    for shift in (0, 1):
        where = [jax.random.randint(jax.random.fold_in(rng, axis), (), 0, length) for axis, length in enumerate(drawn.shape)]
        where[longest] = (where[longest] + shift) % drawn.shape[longest]
        spots.append(tuple(where))
    return drawn.at[spots[0]].set(least).at[spots[1]].set(largest)


def steps_of(rng, dims, shards, low, high):
    def one(dim, blocks):
        draws = jax.random.uniform(jax.random.fold_in(jax.random.fold_in(rng, 6), dim), (blocks,), jnp.float32, low / len(shards), high / len(shards))
        return jnp.repeat(jnp.exp(draws), dims[dim] // blocks).reshape((-1,) + (1,) * (len(dims) - dim - 1))

    loudness = one(*shards[0])
    for cut in shards[1:]:
        loudness = loudness * one(*cut)
    return loudness


def centred(own_key, dims, scale, most, pieces=(), kind=jnp.bfloat16):
    factor_of = steps_of(own_key, dims, pieces, -0.22, 0.18) if pieces else 1.0
    values = jax.random.normal(own_key, dims, jnp.float32) * scale * factor_of
    return jnp.minimum(jnp.maximum(values, -most), most).astype(kind)


def setup_inputs(seed: int = 0) -> dict:
    key_of = jax.random.split(jax.random.key(seed), 18)
    features = draw_features(jax.random.fold_in(key_of[17], 71), 0)
    adjacency = draw_adjacency(jax.random.fold_in(key_of[17], 71), 0)
    labels = plant(jax.random.randint(key_of[2], (SUBS_ALL, N_SUB), 0, CLS), jax.random.fold_in(key_of[2], 1), 0, CLS - 1).astype(jnp.int32)
    train_mask = draw_train_mask(jax.random.fold_in(key_of[17], 71), 0)
    input_weight = centred(key_of[4], (F_IN, HID), F_IN ** -0.5, 0.625, ((1, 4),), jnp.float32)
    input_moment = centred(key_of[5], (F_IN, HID), (1.0 / (N_GRP * N_SUB) ** 0.5), 0.125, ((1, 4),), jnp.float32)
    conv_weight = centred(key_of[6], (LAYERS, 2 * HID, HID), (2 * HID) ** -0.5, 0.25, ((2, 4),), jnp.float32)
    conv_moment = centred(key_of[7], (LAYERS, 2 * HID, HID), (1.0 / (N_GRP * N_SUB) ** 0.5), 0.125, ((2, 4),), jnp.float32)
    head_weight = centred(key_of[8], (HID, CLS), HID ** -0.5, 0.375, (), jnp.float32)
    head_first = centred(key_of[9], (HID, CLS), (0.11 / (N_GRP * N_SUB) ** 0.5), 0.013671875, (), jnp.float32)
    head_second = jnp.clip(jnp.exp(jax.random.uniform(key_of[10], (HID, CLS), jnp.float32, math.log(3.2348632430512225e-06), math.log(1.2817382412322331e-05))), 3.2348632430512225e-06, 1.2817382412322331e-05)
    head_bias = centred(key_of[11], (CLS,), 0.3, 3.0, (), jnp.float32)
    bias_first = centred(key_of[12], (CLS,), (0.11 / (N_GRP * N_SUB) ** 0.5), 0.013671875, (), jnp.float32)
    bias_second = jnp.clip(jnp.exp(jax.random.uniform(key_of[13], (CLS,), jnp.float32, math.log(3.2348632430512225e-06), math.log(1.2817382412322331e-05))), 3.2348632430512225e-06, 1.2817382412322331e-05)
    norm_params = draw_norm_params(jax.random.fold_in(key_of[17], 71), 0)
    norm_first = centred(key_of[15], (LAYERS, 2, HID), (0.11 / (N_GRP * N_SUB) ** 0.5), 0.013671875, (), jnp.float32)
    norm_second = jnp.clip(jnp.exp(jax.random.uniform(key_of[16], (LAYERS, 2, HID), jnp.float32, math.log(3.2348632430512225e-06), math.log(1.2817382412322331e-05))), 3.2348632430512225e-06, 1.2817382412322331e-05)
    return dict(features=features, adjacency=adjacency, labels=labels, train_mask=train_mask, input_weight=input_weight, input_moment=input_moment, conv_weight=conv_weight, conv_moment=conv_moment, head_weight=head_weight, head_first=head_first, head_second=head_second, head_bias=head_bias, bias_first=bias_first, bias_second=bias_second, norm_params=norm_params, norm_first=norm_first, norm_second=norm_second)


norm_eps = 1e-05
smoothing = 0.1
poly_first = 3.4445
poly_second = -4.775
poly_third = 2.0315
muon_beta = 0.95
muon_rate = 0.2
decay_rate = 0.01
adam_rate = 0.05
beta_first = 0.9
beta_second = 0.95
adam_eps = 1e-08

@jax.custom_vjp
def low(v):
    return lax.optimization_barrier(v.astype(jnp.bfloat16)).astype(jnp.float32)

@jax.custom_vjp
def low_back(v):
    return v

def low_keep(v):
    return (low(v), None)

def low_pass(kept, grad):
    return (grad,)

def back_keep(v):
    return (v, None)

def back_low(kept, grad):
    return (low(grad),)
low.defvjp(low_keep, low_pass)
low_back.defvjp(back_keep, back_low)

def matmul_hi(left, right):
    return jnp.dot(left, right, precision=lax.Precision.HIGHEST)

def sub_loss(params, inputs, adj, label_row, mask_row):
    input_w, conv_w, head_w, head_b, norms = params
    state = matmul_hi(inputs, low(input_w))
    for layer in range(LAYERS):
        rounded = low(low_back(state))
        agg_low = low(low_back(matmul_hi(adj, rounded)))
        weight = low(conv_w[layer])
        pre = low_back(matmul_hi(rounded, weight[:HID]) + matmul_hi(agg_low, weight[HID:]))
        act = jax.nn.gelu(pre)
        mean = lax.optimization_barrier(jnp.mean(act, 0))
        var = lax.optimization_barrier(jnp.mean(act * act, 0)) - mean * mean
        state = (act - mean) * lax.rsqrt(var + norm_eps) * norms[layer, 0] + norms[layer, 1]
    rounded = low(low_back(state))
    logits = low_back(matmul_hi(rounded, low(head_w)) + head_b)
    logp = jax.nn.log_softmax(logits, -1)
    onehot = (label_row[:, None] == jnp.arange(CLS, dtype=jnp.int32)[None, :]).astype(jnp.float32)
    target = (1.0 - smoothing) * onehot + smoothing / CLS
    return -jnp.sum(mask_row.astype(jnp.float32) * lax.optimization_barrier(jnp.sum(target * logp, -1)))

def orthogonal(moment):
    gram = matmul_hi(moment, moment.T)
    scale = jnp.sqrt(jnp.trace(gram)) + 1e-07
    iterate = moment / scale
    square = gram / (scale * scale)
    for step in range(NS_STEPS):
        if step > 0:
            square = matmul_hi(iterate, iterate.T)
        poly = poly_second * square + poly_third * matmul_hi(square, square)
        iterate = poly_first * iterate + matmul_hi(poly, iterate)
    return iterate

def muon(weight, grad, moment):
    moment_new = muon_beta * moment + grad
    ortho = orthogonal(moment_new)
    factor = 0.2 * float(max(weight.shape)) ** 0.5
    return (weight - muon_rate * (factor * ortho + decay_rate * weight), moment_new)

def adamw(weight, grad, first, second):
    first_new = beta_first * first + (1.0 - beta_first) * grad
    second_new = beta_second * second + (1.0 - beta_second) * grad * grad
    fixed_first = first_new / (1.0 - beta_first ** STEP)
    fixed_second = second_new / (1.0 - beta_second ** STEP)
    update = fixed_first / (jnp.sqrt(fixed_second) + adam_eps) + decay_rate * weight
    return (weight - adam_rate * update, first_new, second_new)

def reference(features, adjacency, labels, train_mask, input_weight, input_moment, conv_weight, conv_moment, head_weight, head_first, head_second, head_bias, bias_first, bias_second, norm_params, norm_first, norm_second):
    count = jnp.sum(train_mask).astype(jnp.float32)
    data = (features.astype(jnp.float32), adjacency.astype(jnp.float32), labels, train_mask)

    def objective(params):

        def one_sub(items):
            return jax.checkpoint(sub_loss)(params, items[0], items[1], items[2], items[3])
        total = jnp.sum(lax.map(one_sub, data))
        return (total / count, total)
    params = (input_weight, conv_weight, head_weight, head_bias, norm_params)
    _, pull, loss_sum = jax.vjp(objective, params, has_aux=True)
    grads = pull(jnp.float32(1.0))[0]
    grad_in, grad_conv, grad_head, grad_bias, grad_norm = grads
    input_new, input_moment_new = muon(input_weight, grad_in, input_moment)
    conv_list = []
    moment_list = []
    for layer in range(LAYERS):
        new_w, new_m = muon(conv_weight[layer], grad_conv[layer], conv_moment[layer])
        conv_list.append(new_w)
        moment_list.append(new_m)
    head_new, head_first_new, head_second_new = adamw(head_weight, grad_head, head_first, head_second)
    bias_new, bias_first_new, bias_second_new = adamw(head_bias, grad_bias, bias_first, bias_second)
    norm_new, norm_first_new, norm_second_new = adamw(norm_params, grad_norm, norm_first, norm_second)
    loss_parts = jnp.stack([loss_sum, count])
    return (loss_parts, input_new, input_moment_new, jnp.stack(conv_list), jnp.stack(moment_list), head_new, head_first_new, head_second_new, bias_new, bias_first_new, bias_second_new, norm_new, norm_first_new, norm_second_new)
```

```python
import functools

import jax
import jax.numpy as jnp
from jax import lax
from jax.experimental import pallas as pl
from jax.experimental.pallas import tpu as pltpu
from jax.sharding import PartitionSpec as P

NS_STEPS = 5
STEP = 10


norm_eps = 1e-05
smoothing = 0.1
poly_first = 3.4445
poly_second = -4.775
poly_third = 2.0315
muon_beta = 0.95
muon_rate = 0.2
decay_rate = 0.01
adam_rate = 0.05
beta_first = 0.9
beta_second = 0.95
adam_eps = 1e-08


def lowered(value):
    return value.astype(jnp.bfloat16)


def matmul_hi(left, right):
    return jnp.dot(left, right, precision=lax.Precision.HIGHEST)


def column_dot(left, right):
    return lax.dot_general(
        left, right, (((0,), (0,)), ((), ())), preferred_element_type=jnp.float32
    )


def row_dot(left, right):
    return lax.dot_general(
        left, right, (((1,), (1,)), ((), ())), preferred_element_type=jnp.float32
    )


def neighbour_sum(adj, values):
    return jnp.dot(
        adj, lax.all_gather(values, "node", axis=0, tiled=True), preferred_element_type=jnp.float32
    )


def neighbour_back(adj, grads):
    return lax.psum_scatter(column_dot(adj, grads), "node", scatter_dimension=0, tiled=True)


def layer_forward(adj, inputs_low, weight_low, gain, shift, total_rows):
    hidden = weight_low.shape[1]
    agg_low = lowered(neighbour_sum(adj, inputs_low))
    pre = jnp.dot(inputs_low, weight_low[:hidden], preferred_element_type=jnp.float32)
    pre = pre + jnp.dot(agg_low, weight_low[hidden:], preferred_element_type=jnp.float32)
    act = jax.nn.gelu(pre)
    sums, squares = lax.psum((jnp.sum(act, 0), jnp.sum(act * act, 0)), "node")
    mean = sums / total_rows
    var = squares / total_rows - mean * mean
    inv_std = lax.rsqrt(var + norm_eps)
    normed = (act - mean) * inv_std
    return (normed * gain + shift, (inputs_low, agg_low, pre, normed, inv_std))


def layer_backward(adj, weight_low, gain, kept, grad_out, total_rows):
    inputs_low, agg_low, pre, normed, inv_std = kept
    hidden = weight_low.shape[1]
    grad_gain = jnp.sum(grad_out * normed, 0)
    grad_shift = jnp.sum(grad_out, 0)
    grad_normed = grad_out * gain
    first, second = lax.psum((jnp.sum(grad_normed, 0), jnp.sum(grad_normed * normed, 0)), "node")
    grad_act = (grad_normed - first / total_rows - normed * (second / total_rows)) * inv_std
    grad_pre = jax.vjp(jax.nn.gelu, pre)[1](grad_act)[0]
    pre_low = lowered(grad_pre)
    grad_weight = jnp.concatenate(
        [column_dot(inputs_low, pre_low), column_dot(agg_low, pre_low)], 0
    )
    grad_agg = lowered(row_dot(pre_low, weight_low[hidden:]))
    grad_inputs = row_dot(pre_low, weight_low[:hidden]) + neighbour_back(adj, grad_agg)
    return (grad_inputs, grad_weight, jnp.stack([grad_gain, grad_shift]))


def gram_of(block):
    return matmul_hi(block, block.T)


def orthogonal_blocks(first_block, second_block, third_block):
    blocks = [first_block, second_block, third_block]
    for step in range(NS_STEPS):
        grams = lax.psum((gram_of(blocks[0]), gram_of(blocks[1]), gram_of(blocks[2])), "grp")
        grams = list(grams)
        if step == 0:
            scales = [jnp.sqrt(jnp.trace(gram)) + 1e-07 for gram in grams]
            blocks = [block / scale for block, scale in zip(blocks, scales)]
            grams = [gram / (scale * scale) for gram, scale in zip(grams, scales)]
        polys = [poly_second * gram + poly_third * matmul_hi(gram, gram) for gram in grams]
        blocks = [poly_first * block + matmul_hi(poly, block) for block, poly in zip(blocks, polys)]
    return blocks


def adamw(weight, grad, first, second):
    first_new = beta_first * first + (1.0 - beta_first) * grad
    second_new = beta_second * second + (1.0 - beta_second) * grad * grad
    fixed_first = first_new / (1.0 - beta_first**STEP)
    fixed_second = second_new / (1.0 - beta_second**STEP)
    update = fixed_first / (jnp.sqrt(fixed_second) + adam_eps) + decay_rate * weight
    return (weight - adam_rate * update, first_new, second_new)


def per_device(
    features,
    adjacency,
    labels,
    train_mask,
    input_weight,
    input_moment,
    conv_weight,
    conv_moment,
    head_weight,
    head_first,
    head_second,
    head_bias,
    bias_first,
    bias_second,
    norm_params,
    norm_first,
    norm_second,
):
    layers = conv_weight.shape[0]
    hidden = head_weight.shape[0]
    classes = head_weight.shape[1]
    f_width = input_weight.shape[0]
    total_rows = features.shape[1] * lax.axis_size("node")
    input_full, conv_full = (
        lax.all_gather(lowered(input_weight), "grp", axis=1, tiled=True),
        lax.all_gather(lowered(conv_weight), "grp", axis=2, tiled=True),
    )
    head_low = lowered(head_weight)
    count = lax.psum(jnp.sum(train_mask).astype(jnp.float32), ("grp", "node"))
    grad_input = jnp.zeros((f_width, hidden), jnp.float32)
    grad_conv = [jnp.zeros((2 * hidden, hidden), jnp.float32) for layer in range(layers)]
    grad_norm = [jnp.zeros((2, hidden), jnp.float32) for layer in range(layers)]
    grad_head = jnp.zeros((hidden, classes), jnp.float32)
    grad_bias = jnp.zeros((classes,), jnp.float32)
    loss_sum = jnp.float32(0.0)
    for graph in range(features.shape[0]):
        inputs = features[graph]
        adj = adjacency[graph]
        current_low = lowered(jnp.dot(inputs, input_full, preferred_element_type=jnp.float32))
        kept_list = []
        for layer in range(layers):
            output, kept = layer_forward(
                adj,
                current_low,
                conv_full[layer],
                norm_params[layer, 0],
                norm_params[layer, 1],
                total_rows,
            )
            kept_list.append(kept)
            current_low = lowered(output)
        logits = jnp.dot(current_low, head_low, preferred_element_type=jnp.float32) + head_bias
        logp = jax.nn.log_softmax(logits, -1)
        onehot = (labels[graph][:, None] == jnp.arange(classes, dtype=jnp.int32)[None, :]).astype(
            jnp.float32
        )
        target = (1.0 - smoothing) * onehot + smoothing / classes
        weights = train_mask[graph].astype(jnp.float32)
        loss_sum = loss_sum - jnp.sum(weights * jnp.sum(target * logp, -1))
        logits_low = lowered((weights / count)[:, None] * (jnp.exp(logp) - target))
        grad_head = grad_head + column_dot(current_low, logits_low)
        grad_bias = grad_bias + jnp.sum(logits_low.astype(jnp.float32), 0)
        grad_low = lowered(row_dot(logits_low, head_low))
        for layer in reversed(range(layers)):
            grad_inputs, grad_weight, grad_pair = layer_backward(
                adj,
                conv_full[layer],
                norm_params[layer, 0],
                kept_list[layer],
                grad_low.astype(jnp.float32),
                total_rows,
            )
            grad_conv[layer] = grad_conv[layer] + grad_weight
            grad_norm[layer] = grad_norm[layer] + grad_pair
            grad_low = lowered(grad_inputs)
        grad_input = grad_input + column_dot(inputs, grad_low)
    grad_conv_all = jnp.stack(grad_conv)
    grad_norm_all = jnp.stack(grad_norm)
    grad_input, grad_conv_all, grad_head, grad_bias, grad_norm_all, loss_sum = lax.psum(
        (grad_input, grad_conv_all, grad_head, grad_bias, grad_norm_all, loss_sum), "node"
    )
    grad_input, grad_conv_all = (
        lax.psum_scatter(grad_input, "grp", scatter_dimension=1, tiled=True),
        lax.psum_scatter(grad_conv_all, "grp", scatter_dimension=2, tiled=True),
    )
    grad_head, grad_bias, grad_norm_all, loss_sum = lax.psum(
        (grad_head, grad_bias, grad_norm_all, loss_sum), "grp"
    )
    moment_in = muon_beta * input_moment + grad_input
    moment_conv = muon_beta * conv_moment + grad_conv_all
    ortho_in, ortho_first, ortho_second = orthogonal_blocks(
        moment_in, moment_conv[0], moment_conv[1]
    )
    factor_in = 0.2 * float(max(f_width, hidden)) ** 0.5
    factor_conv = 0.2 * float(2 * hidden) ** 0.5
    input_new = input_weight - muon_rate * (factor_in * ortho_in + decay_rate * input_weight)
    ortho_conv = jnp.stack([ortho_first, ortho_second])
    conv_new = conv_weight - muon_rate * (factor_conv * ortho_conv + decay_rate * conv_weight)
    head_new, head_first_new, head_second_new = adamw(
        head_weight, grad_head, head_first, head_second
    )
    bias_new, bias_first_new, bias_second_new = adamw(head_bias, grad_bias, bias_first, bias_second)
    norm_new, norm_first_new, norm_second_new = adamw(
        norm_params, grad_norm_all, norm_first, norm_second
    )
    loss_parts = jnp.stack([loss_sum, count])
    return (
        loss_parts,
        input_new,
        moment_in,
        conv_new,
        moment_conv,
        head_new,
        head_first_new,
        head_second_new,
        bias_new,
        bias_first_new,
        bias_second_new,
        norm_new,
        norm_first_new,
        norm_second_new,
    )

MESH = pl.DeviceIdType.MESH
NT = (((1,), (1,)), ((), ()))
NN = (((1,), (0,)), ((), ()))
VMEM_BYTES = 56 * 1024 * 1024
ROUNDS = 8


def flip(index, bit):
    return index + bit - 2 * bit * lax.rem(lax.div(index, bit), 2)


def dot(left, right, dims=NN):
    return lax.dot_general(left, right, dims, preferred_element_type=jnp.float32)


def split(value):
    high = lowered(value)
    return high, lowered(value - high.astype(jnp.float32))


def dot_three(left, right, dims=NN):
    left_high, left_rest = left
    right_high, right_rest = right
    return (
        dot(left_high, right_high, dims)
        + dot(left_high, right_rest, dims)
        + dot(left_rest, right_high, dims)
    )


def step_kernel(
    groups,
    classes,
    feat,
    adj,
    labels,
    train,
    w_in,
    m_in,
    w_conv,
    m_conv,
    w_head,
    f_head,
    s_head,
    w_bias,
    f_bias,
    s_bias,
    w_norm,
    f_norm,
    s_norm,
    o_small,
    o_in,
    o_in_m,
    o_conv,
    o_conv_m,
    o_head,
    o_head_f,
    o_head_s,
    o_norm,
    o_norm_f,
    o_norm_s,
    av,
    xg,
    hg,
    dg,
    pad,
    wt,
    wt_in,
    wn,
    wt_head,
    h0,
    agg,
    act,
    slope,
    ms,
    axh,
    accx,
    acc,
    h2,
    dh,
    dp,
    gt,
    q1,
    q2,
    ght,
    st,
    zs,
    sums,
    mpc,
    mpi,
    gbc,
    gbi,
    gbh,
    rsc,
    rsi,
    rsh,
    zc,
    zi,
    zh,
    mf,
    mfi,
    hf,
    y_conv,
    y_in,
    loc,
    ga_s,
    ga_r,
    st_s,
    st_r,
    z_s,
    z_r,
    rs_s,
    rs_r,
    ag_s,
    ag_r,
):
    f32 = jnp.float32
    bf16 = jnp.bfloat16
    graphs, rows, width = feat.shape
    total = adj.shape[2]
    hidden = w_head.shape[0]
    wide = 2 * hidden
    shard = hidden // groups
    part = shard // 4
    half = rows // 2
    chunk = min(rows, 128)
    chunks = rows // chunk
    g = lax.axis_index("grp")
    me = lax.axis_index("node")
    core = lax.rem(me, 2)
    chip = lax.div(me, 2)
    n_sib, n_x, n_y, n_d = flip(me, 1), flip(me, 2), flip(me, 4), flip(flip(me, 2), 4)
    peers = [
        flip(flip(flip(me, 1) if b & 1 else me, 2) if b & 2 else (flip(me, 1) if b & 1 else me), 4)
        if b & 4
        else (flip(flip(me, 1) if b & 1 else me, 2) if b & 2 else flip(me, 1))
        for b in range(1, 8)
    ]
    z_peers = [lax.rem(g + d, groups) for d in range(1, groups)]
    z_from = [lax.rem(g + groups - d, groups) for d in range(1, groups)]
    started = []

    def send(src, dst, s_sem, r_sem, group, node):
        copy = pltpu.make_async_remote_copy(
            src_ref=src,
            dst_ref=dst,
            send_sem=s_sem,
            recv_sem=r_sem,
            device_id=(group, node),
            device_id_type=MESH,
        )
        copy.start()
        started.append(copy)
        return copy

    def lanes_of_core(span):
        return pl.ds(pl.multiple_of(core * span, span), span)

    barrier = pltpu.get_barrier_semaphore()
    for node in peers:
        pl.semaphore_signal(barrier, inc=1, device_id=(g, node), device_id_type=MESH)
    for group in z_peers:
        pl.semaphore_signal(barrier, inc=1, device_id=(group, me), device_id_type=MESH)

    own_x = [pltpu.make_async_copy(feat.at[s], xg.at[s, me], loc.at[s]) for s in range(graphs)]
    own_a = [pltpu.make_async_copy(adj.at[s], av.at[s], loc.at[graphs + s]) for s in range(graphs)]
    for copy in own_x + own_a:
        copy.start()

    pad[...] = jnp.zeros_like(pad)

    def transposed(value):
        depth, span = value.shape
        pad[pl.ds(0, depth), pl.ds(0, span)] = value
        return pad[...].T

    for l in range(2):
        wt[l, pl.ds(pl.multiple_of(g * shard, shard), shard), :] = lowered(
            transposed(w_conv[l])[:shard]
        )
    wt_in[pl.ds(pl.multiple_of(g * shard, shard), shard), :] = lowered(
        transposed(w_in[...])[:shard, :width]
    )
    for copy in own_x:
        copy.wait()
    pl.semaphore_wait(barrier, 7 + groups - 1)

    def gather_of(index, ref):
        low, high = pl.ds(0, half), pl.ds(half, half)

        def go(j, node, block, span=None):
            view = ref.at[block] if span is None else ref.at[block, span]
            return send(view, view, ga_s.at[index, j], ga_r.at[index, j], g, node)

        kept = {}

        def own():
            kept[0] = go(0, n_x, me, low)
            kept[1] = go(1, n_y, me, high)
            kept[6] = go(6, n_sib, me)
            kept[2] = go(2, n_x, me, high)
            kept[3] = go(3, n_y, me, low)

        def relay():
            kept[0].wait_recv()
            kept[4] = go(4, n_y, n_x, low)
            kept[1].wait_recv()
            kept[5] = go(5, n_x, n_y, high)

        def near():
            kept[2].wait_recv()
            kept[7] = go(7, n_sib, n_x)
            kept[3].wait_recv()
            kept[8] = go(8, n_sib, n_y)

        def far():
            kept[4].wait_recv()
            kept[5].wait_recv()
            kept[9] = go(9, n_sib, n_d)

        def near_ready():
            for j in (6, 7, 8):
                kept[j].wait_recv()

        def far_ready():
            kept[9].wait_recv()

        return own, relay, near, far, near_ready, far_ready

    def chip_at(i):
        cx = lax.rem(lax.rem(chip, 2) + lax.rem(i, 2), 2)
        cy = lax.rem(lax.div(chip, 2) + lax.div(i, 2), 2)
        return cx + 2 * cy

    def product(s, ref, out, first, last):
        if first == 0:
            out[...] = jnp.zeros_like(out)

        def body(i, carry):
            c = chip_at(i)
            block = ref[pl.ds(2 * c, 2)].reshape(2 * rows, ref.shape[2])
            left = av[s, :, pl.ds(pl.multiple_of(c * 2 * rows, 2 * rows), 2 * rows)]
            out[...] += dot(left, block)
            return carry

        lax.fori_loop(first, last, body, 0)

    def over_rows(body, carry):
        def one(i, value):
            return body(pl.ds(pl.multiple_of(i * chunk, chunk), chunk), value)

        return lax.fori_loop(0, chunks, one, carry)

    def fold(value):
        return jnp.sum(value.reshape(chunk // 8, 8, hidden), 0)

    st_copies = {}

    def plane_send(k):
        view = st.at[k, me]
        st_copies[k] = [
            send(view, view, st_s.at[k, i], st_r.at[k, i], g, node) for i, node in enumerate(peers)
        ]

    def plane_sum(k):
        for copy in st_copies[k]:
            copy.wait_recv()
        value = st[k, 0]
        for i in range(1, 8):
            value = value + st[k, i]
        return value

    z_copies = {}

    def z_send(k, view):
        z_copies[k] = [
            send(view, view, z_s.at[k, i], z_r.at[k, i], group, me)
            for i, group in enumerate(z_peers)
        ]

    def z_wait(k):
        for copy in z_copies[k]:
            copy.wait_recv()

    x_g = [gather_of(s, xg.at[s]) for s in range(2)]
    h_g = [gather_of(2 + s, hg.at[s]) for s in range(2)]
    d_g = [gather_of(4 + s, dg.at[s]) for s in range(2)]

    x_g[0][0]()
    own_rows = pl.ds(pl.multiple_of(g * shard, shard), shard)
    z_send(0, wt_in.at[own_rows])
    z_send(1, wt.at[0, own_rows])
    z_send(2, wt.at[1, own_rows])
    x_g[0][1]()
    x_g[1][0]()
    wt_head[...] = lowered(transposed(w_head[...])[:, :hidden])
    bias_col = jnp.broadcast_to(w_bias[...], (8, classes))
    pad[pl.ds(0, 8), pl.ds(0, classes)] = bias_col
    bias_col = pad[pl.ds(0, 128), :].T[:64, :1]
    for l in range(2):
        piece = transposed(m_conv[l])[:shard].reshape(4, part, wide)
        gt[0, pl.ds(0, shard), :] = piece.reshape(shard, wide)
        rows_q = pl.ds(pl.multiple_of(chip * part, part), part)
        mpc[l, g] = gt[0, rows_q, lanes_of_core(hidden)]
    pad_in = transposed(m_in[...])[:shard, :width]
    accx[pl.ds(0, shard), :] = pad_in
    mpi[g] = accx[pl.ds(pl.multiple_of(chip * part, part), part), :]
    z_send(6, mpc.at[0, g])
    z_send(7, mpc.at[1, g])
    z_send(8, mpi.at[g])
    count_own = jnp.sum(train[...].astype(f32), axis=1, keepdims=True)
    count_own = count_own[0:1] + count_own[1:2]

    x_g[0][2]()
    for copy in own_a:
        copy.wait()

    def forward_act(s, l, k, first, second, w_first, w_second):
        acc[...] = dot(first, w_first) + dot(second, w_second)

        def body(span, carry):
            pre = acc[span, :]
            square = pre * pre
            inner = 0.7978845608028654 * pre * (1.0 + 0.044715 * square)
            t = jnp.tanh(inner)
            value = 0.5 * pre * (1.0 + t)
            act[l, s, span, :] = value
            slope[l, s, span, :] = 0.5 * (1.0 + t) + 0.5 * pre * (1.0 - t * t) * (
                0.7978845608028654 * (1.0 + 3.0 * 0.044715 * square)
            )
            return carry[0] + fold(value), carry[1] + fold(value * value)

        zero = jnp.zeros((8, hidden), f32)
        one, two = over_rows(body, (zero, zero))
        st[k, me] = jnp.zeros((8, hidden), f32)
        st[k, me, 0:1, :] = jnp.sum(one, 0, keepdims=True)
        st[k, me, 1:2, :] = jnp.sum(two, 0, keepdims=True)
        if k == 0:
            st[k, me, 2:3, :] = jnp.broadcast_to(count_own, (1, hidden))
        plane_send(k)

    def normalise(s, l, k, out):
        sums_all = plane_sum(k)
        mean = sums_all[0:1] / total
        var = sums_all[1:2] / total - mean * mean
        inv = lax.rsqrt(var + norm_eps)
        ms[l, s, 0:1, :] = inv
        gain, shift = w_norm[l, 0:1, :], w_norm[l, 1:2, :]

        def body(span, carry):
            normed = (act[l, s, span, :] - mean) * inv
            act[l, s, span, :] = normed
            out[span, :] = lowered(normed * gain + shift)
            return carry

        over_rows(body, 0)
        return sums_all

    def layer_zero(s):
        high, rest = split(accx[...])
        axh[s] = high
        w = wt_in[...]
        agg[0, s] = lowered(dot(high, w, NT) + dot(rest, w, NT))
        h0[s] = lowered(dot(xg[s, me], w, NT))
        forward_act(s, 0, s, h0[s], agg[0, s], wn[0, :hidden, :], wn[0, hidden:, :])

    def layer_one(s):
        agg[1, s] = lowered(acc[...])
        forward_act(s, 1, 2 + s, hg[s, me], agg[1, s], wn[1, :hidden, :], wn[1, hidden:, :])

    def head(s, count):
        value = h2[s]
        logits = dot(wt_head[pl.ds(0, 64), :], value, NT) + bias_col
        at = lax.broadcasted_iota(jnp.int32, (64, rows), 0)
        valid = at < classes
        logits = jnp.where(valid, logits, -1e30)
        shifted = logits - jnp.max(logits, 0, keepdims=True)
        logp = shifted - jnp.log(jnp.sum(jnp.exp(shifted), 0, keepdims=True))
        onehot = jnp.where(at == labels[s : s + 1, :], 1.0, 0.0)
        target = jnp.where(valid, (1.0 - smoothing) * onehot + smoothing / classes, 0.0)
        weights = train[s : s + 1, :].astype(f32)
        node_loss = jnp.sum(target * logp, 0, keepdims=True)
        loss = -jnp.sum(weights * node_loss, axis=1, keepdims=True)
        delta = (weights / count) * (jnp.exp(logp) - target)
        delta_low = lowered(delta)
        value_t = dot(delta_low, value)
        ght[...] = value_t if s == 0 else ght[...] + value_t
        column = dot(jnp.ones((8, rows), bf16), delta_low, NT)
        tall = jnp.concatenate([delta_low.astype(f32), jnp.zeros((64, rows), f32)], 0).T
        dh[s] = lowered(dot(lowered(tall), wt_head[...])).astype(f32)
        return loss, column

    def backward_sums(s, l, k, extra=None):
        def body(span, carry):
            grad = dh[s, span, :]
            return carry[0] + fold(grad), carry[1] + fold(grad * act[l, s, span, :])

        zero = jnp.zeros((8, hidden), f32)
        one, two = over_rows(body, (zero, zero))
        st[k, me] = jnp.zeros((8, hidden), f32)
        st[k, me, 0:1, :] = jnp.sum(one, 0, keepdims=True)
        st[k, me, 1:2, :] = jnp.sum(two, 0, keepdims=True)
        if extra is not None:
            st[k, me, 2:3, 0:64] = extra[1][0:1]
            st[k, me, 3:4, :] = jnp.broadcast_to(extra[0], (1, hidden))
        plane_send(k)

    def backward_pre(s, l, k):
        sums_all = plane_sum(k)
        sums[1 - l] = sums_all if s == 0 else sums[1 - l] + sums_all
        gain = w_norm[l, 0:1, :]
        inv = ms[l, s, 0:1, :]
        first = gain * sums_all[0:1] / total
        second = gain * sums_all[1:2] / total

        def body(span, carry):
            grad = dh[s, span, :] * gain - first - act[l, s, span, :] * second
            dp[l, s, span, :] = lowered(grad * inv * slope[l, s, span, :])
            return carry

        over_rows(body, 0)

    def conv_grads(s, l, left, right):
        turned = dp[l, s].T
        one, two = dot(turned, left), dot(turned, right)
        if s == 0:
            gt[l, :, :hidden] = one
            gt[l, :, hidden:] = two
        else:
            gt[l, :, :hidden] += one
            gt[l, :, hidden:] += two
        return turned

    rs_copies = {}

    def pieces_send(k, src, dst, where):
        rs_copies[k] = []
        for i, node in enumerate(peers):
            rs_copies[k].append(
                send(where(src, node), dst.at[me], rs_s.at[k, i], rs_r.at[k, i], g, node)
            )

    def pieces_sum(k, src, dst, own):
        dst[me] = own
        for copy in rs_copies[k]:
            copy.wait_recv()
        value = dst[0].astype(f32)
        for i in range(1, 8):
            value = value + dst[i].astype(f32)
        return value

    def conv_piece(ref, node):
        n_core, n_chip = lax.rem(node, 2), lax.div(node, 2)
        return ref.at[:, n_chip, :, pl.ds(pl.multiple_of(n_core * hidden, hidden), hidden)]

    def in_piece(ref, node):
        return ref.at[:, lax.div(node, 2)]

    def head_piece(ref, node):
        n_core, n_chip = lax.rem(node, 2), lax.div(node, 2)
        return ref.at[n_chip, :, pl.ds(pl.multiple_of(n_core * (hidden // 2), hidden // 2), hidden // 2)]

    def over_z(k, buf):
        z_wait(k)
        value = buf[0].astype(f32)
        for i in range(1, groups):
            value = value + buf[i].astype(f32)
        return value

    ag_copies = {}

    def spread(k, view, nodes):
        ag_copies[k] = [
            send(view, view, ag_s.at[k, i], ag_r.at[k, i], g, node) for i, node in nodes
        ]

    def spread_wait(k):
        for copy in ag_copies[k]:
            copy.wait_recv()

    all_nodes = list(enumerate(peers))
    same_core = [(i, peers[i]) for i in (1, 3, 5)]
    core_lanes = lanes_of_core(hidden)
    head_lanes = lanes_of_core(hidden // 2)

    x_g[0][4]()
    product(0, xg.at[0], accx, 0, 3)
    x_g[1][1]()
    x_g[0][3]()
    x_g[0][5]()
    product(0, xg.at[0], accx, 3, 4)
    z_wait(0)
    z_wait(1)
    wn[0] = wt[0].T
    layer_zero(0)
    x_g[1][2]()
    x_g[1][4]()
    product(1, xg.at[1], accx, 0, 3)
    x_g[1][3]()
    x_g[1][5]()
    product(1, xg.at[1], accx, 3, 4)
    layer_zero(1)
    count_plane = normalise(0, 0, 0, hg.at[0, me])
    h_g[0][0]()
    zs[0, g] = count_plane
    z_send(3, zs.at[0, g])
    z_wait(2)
    wn[1] = wt[1].T
    normalise(1, 0, 1, hg.at[1, me])
    h_g[0][1]()
    h_g[1][0]()
    h_g[0][2]()
    h_g[0][4]()
    product(0, hg.at[0], acc, 0, 3)
    h_g[0][3]()
    h_g[1][1]()
    h_g[0][5]()
    product(0, hg.at[0], acc, 3, 4)
    layer_one(0)
    z_wait(3)
    count = zs[0, 0]
    for i in range(1, groups):
        count = count + zs[0, i]
    count = count[2:3, 0:1]
    normalise(0, 1, 2, h2.at[0])
    loss_row = head(0, count)
    backward_sums(0, 1, 4, loss_row)
    h_g[1][2]()
    h_g[1][3]()
    backward_pre(0, 1, 4)
    dg[0, me] = lowered(dot(dp[1, 0], wt[1, :, hidden:]))
    d_g[0][0]()
    h_g[1][4]()
    product(1, hg.at[1], acc, 0, 3)
    h_g[1][5]()
    product(1, hg.at[1], acc, 3, 4)
    layer_one(1)
    conv_grads(0, 1, hg[0, me], agg[1, 0])
    dh[0] = dot(dp[1, 0], wt[1, :, :hidden])
    normalise(1, 1, 3, h2.at[1])
    loss_row = head(1, count)
    backward_sums(1, 1, 5, loss_row)
    d_g[0][1]()
    backward_pre(1, 1, 5)
    dg[1, me] = lowered(dot(dp[1, 1], wt[1, :, hidden:]))
    d_g[1][0]()
    conv_grads(1, 1, hg[1, me], agg[1, 1])
    dh[1] = dot(dp[1, 1], wt[1, :, :hidden])
    gbc[1] = lowered(gt[1]).reshape(groups, 4, part, wide)
    gbh[...] = lowered(ght[...]).reshape(4, 16, hidden)
    zs[1, g] = sums[0]
    z_send(4, zs.at[1, g])
    d_g[0][2]()
    d_g[0][4]()
    product(0, dg.at[0], acc, 0, 3)
    d_g[0][3]()
    d_g[1][1]()
    d_g[0][5]()
    product(0, dg.at[0], acc, 3, 4)
    dh[0] = lowered(dh[0] + acc[...]).astype(f32)
    backward_sums(0, 0, 6)
    pieces_send(0, gbc.at[1], rsc.at[1], conv_piece)
    pieces_send(1, gbh, rsh, head_piece)
    d_g[1][2]()
    d_g[1][4]()
    product(1, dg.at[1], acc, 0, 3)
    d_g[1][3]()
    backward_pre(0, 0, 6)
    turned = conv_grads(0, 0, h0[0], agg[0, 0])
    q1[...] = dot(turned, xg[0, me])
    q2[...] = dot(turned, axh[0])
    d_g[1][5]()
    product(1, dg.at[1], acc, 3, 4)
    dh[1] = lowered(dh[1] + acc[...]).astype(f32)
    backward_sums(1, 0, 7)
    zc[1, g] = lowered(pieces_sum(0, None, rsc.at[1], conv_piece(gbc.at[1], me)[...]))
    z_send(9, zc.at[1, g])
    zh[g] = lowered(pieces_sum(1, None, rsh, head_piece(gbh, me)[...]))
    z_send(10, zh.at[g])
    backward_pre(1, 0, 7)
    turned = conv_grads(1, 0, h0[1], agg[0, 1])
    q1[...] += dot(turned, xg[1, me])
    q2[...] += dot(turned, axh[1])
    gbc[0] = lowered(gt[0]).reshape(groups, 4, part, wide)
    pieces_send(2, gbc.at[0], rsc.at[0], conv_piece)
    one, two = split(q1[...]), split(q2[...])
    w_self, w_near = wn[0, :hidden, :], wn[0, hidden:, :]
    g_in = dot(w_self, one[0]) + dot(w_self, one[1]) + dot(w_near, two[0]) + dot(w_near, two[1])
    gbi[...] = lowered(g_in).reshape(groups, 4, part, width)
    pieces_send(3, gbi, rsi, in_piece)
    zs[2, g] = sums[1]
    z_send(5, zs.at[2, g])

    z_wait(7)
    mf[1, :, chip, :, core_lanes] = muon_beta * mpc[1] + over_z(9, zc.at[1])
    spread(0, mf.at[1, :, chip, :, core_lanes], all_nodes)
    hf[chip, :, head_lanes] = over_z(10, zh)
    spread(1, hf.at[chip, :, head_lanes], all_nodes)
    zc[0, g] = lowered(pieces_sum(2, None, rsc.at[0], conv_piece(gbc.at[0], me)[...]))
    z_send(11, zc.at[0, g])
    zi[g] = lowered(pieces_sum(3, None, rsi, in_piece(gbi, me)[...]))
    z_send(12, zi.at[g])
    z_wait(6)
    z_wait(8)
    mf[0, :, chip, :, core_lanes] = muon_beta * mpc[0] + over_z(11, zc.at[0])
    spread(2, mf.at[0, :, chip, :, core_lanes], all_nodes)
    mfi[:, chip] = muon_beta * mpi[...] + over_z(12, zi)
    spread(3, mfi.at[:, chip], same_core)

    def scaled(value):
        norm = jnp.sqrt(jnp.sum(jnp.sum(value * value, 0, keepdims=True), 1, keepdims=True))
        return value / (norm + 1e-07)

    def iterate(refs):
        def body(i, carry):
            for ref in refs:
                value = ref[...]
                pair = split(value)
                gram = dot_three(pair, pair, NT)
                gram_pair = split(gram)
                poly = split(poly_second * gram + poly_third * dot_three(gram_pair, gram_pair))
                ref[...] = poly_first * value + dot_three(poly, pair)
            return carry

        lax.fori_loop(0, NS_STEPS, body, 0)

    def back(value):
        depth, span = value.shape
        flat = jnp.concatenate([value, jnp.zeros((128 - depth, span), f32)], 0)
        return flat.T[:, :depth]

    factor_conv = 0.2 * float(wide) ** 0.5
    factor_in = 0.2 * float(max(width, hidden)) ** 0.5

    def conv_out(l):
        o_conv_m[l] = back(mf[l, g].reshape(shard, wide))
        ortho = back(y_conv[l, own_rows, :])
        weight = w_conv[l]
        o_conv[l] = weight - muon_rate * (factor_conv * ortho + decay_rate * weight)

    spread_wait(0)
    y_conv[1] = scaled(mf[1].reshape(hidden, wide))
    iterate([y_conv.at[1]])
    conv_out(1)

    def adam(weight, grad, first, second):
        return adamw(weight, grad, first, second)

    spread_wait(1)
    grad = jnp.concatenate([hf[...].reshape(64, hidden), jnp.zeros((64, hidden), f32)], 0)
    grad = grad.T[:, :classes]
    o_head[...], o_head_f[...], o_head_s[...] = adam(w_head[...], grad, f_head[...], s_head[...])
    z_wait(4)
    z_wait(5)
    late = zs[1, 0]
    early = zs[2, 0]
    for i in range(1, groups):
        late = late + zs[1, i]
        early = early + zs[2, i]
    for l, rows_l in ((0, early), (1, late)):
        grad = jnp.concatenate([rows_l[1:2], rows_l[0:1]], 0)
        o_norm[l], o_norm_f[l], o_norm_s[l] = adam(w_norm[l], grad, f_norm[l], s_norm[l])
    one, two, three = adam(w_bias[...], late[2:3, :classes], f_bias[...], s_bias[...])
    o_small[...] = jnp.zeros_like(o_small)
    o_small[0:1, 0:classes] = one
    o_small[1:2, 0:classes] = two
    o_small[2:3, 0:classes] = three
    o_small[3:4, 0:1] = late[3:4, 0:1]
    o_small[3:4, 1:2] = count

    spread_wait(2)
    spread_wait(3)
    y_conv[0] = scaled(mf[0].reshape(hidden, wide))
    y_in[...] = scaled(mfi[...].reshape(hidden, width))
    iterate([y_conv.at[0], y_in])
    conv_out(0)
    pad[pl.ds(0, shard), pl.ds(0, width)] = mfi[g].reshape(shard, width)
    o_in_m[...] = pad[pl.ds(0, 128), :].T[:width, :shard]
    pad[pl.ds(0, shard), pl.ds(0, width)] = y_in[own_rows, :]
    ortho = pad[pl.ds(0, 128), :].T[:width, :shard]
    weight = w_in[...]
    o_in[...] = weight - muon_rate * (factor_in * ortho + decay_rate * weight)
    for copy in started:
        copy.wait_send()


def planned(mesh):
    groups = mesh.shape["grp"]

    def call(
        features,
        adjacency,
        labels,
        train_mask,
        input_weight,
        input_moment,
        conv_weight,
        conv_moment,
        head_weight,
        head_first,
        head_second,
        head_bias,
        bias_first,
        bias_second,
        norm_params,
        norm_first,
        norm_second,
    ):
        f32, bf16 = jnp.float32, jnp.bfloat16
        graphs, rows, width = features.shape
        total = adjacency.shape[2]
        hidden, classes = head_weight.shape
        wide = 2 * hidden
        shard = hidden // groups
        part = shard // 4
        vm = pltpu.VMEM
        sem = pltpu.SemaphoreType.DMA
        shape = jax.ShapeDtypeStruct
        near = pl.BlockSpec(memory_space=pltpu.VMEM)
        anywhere = pl.BlockSpec(memory_space=pl.ANY)
        outs = pl.pallas_call(
            functools.partial(step_kernel, groups, classes),
            out_shape=[
                shape((8, 128), f32),
                shape(input_weight.shape, f32),
                shape(input_weight.shape, f32),
                shape(conv_weight.shape, f32),
                shape(conv_weight.shape, f32),
                shape(head_weight.shape, f32),
                shape(head_weight.shape, f32),
                shape(head_weight.shape, f32),
                shape(norm_params.shape, f32),
                shape(norm_params.shape, f32),
                shape(norm_params.shape, f32),
            ],
            in_specs=[anywhere] * 2 + [near] * 15,
            out_specs=[near] * 11,
            scratch_shapes=[
                vm((graphs, rows, total), bf16),
                vm((graphs, 8, rows, width), bf16),
                vm((graphs, 8, rows, hidden), bf16),
                vm((graphs, 8, rows, hidden), bf16),
                vm((wide, 128), f32),
                vm((2, hidden, wide), bf16),
                vm((hidden, width), bf16),
                vm((2, wide, hidden), bf16),
                vm((128, hidden), bf16),
                vm((graphs, rows, hidden), bf16),
                vm((2, graphs, rows, hidden), bf16),
                vm((2, graphs, rows, hidden), f32),
                vm((2, graphs, rows, hidden), f32),
                vm((2, graphs, 8, hidden), f32),
                vm((graphs, rows, width), bf16),
                vm((rows, width), f32),
                vm((rows, hidden), f32),
                vm((graphs, rows, hidden), bf16),
                vm((graphs, rows, hidden), f32),
                vm((2, graphs, rows, hidden), bf16),
                vm((2, hidden, wide), f32),
                vm((hidden, width), f32),
                vm((hidden, width), f32),
                vm((64, hidden), f32),
                vm((ROUNDS, 8, 8, hidden), f32),
                vm((3, groups, 8, hidden), f32),
                vm((2, 8, hidden), f32),
                vm((2, groups, part, hidden), f32),
                vm((groups, part, width), f32),
                vm((2, groups, 4, part, wide), bf16),
                vm((groups, 4, part, width), bf16),
                vm((4, 16, hidden), bf16),
                vm((2, 8, groups, part, hidden), bf16),
                vm((8, groups, part, width), bf16),
                vm((8, 16, hidden // 2), bf16),
                vm((2, groups, groups, part, hidden), bf16),
                vm((groups, groups, part, width), bf16),
                vm((groups, 16, hidden // 2), bf16),
                vm((2, groups, 4, part, wide), f32),
                vm((groups, 4, part, width), f32),
                vm((4, 16, hidden), f32),
                vm((2, hidden, wide), f32),
                vm((hidden, width), f32),
                sem((2 * graphs,)),
                sem((6, 10)),
                sem((6, 10)),
                sem((ROUNDS, 7)),
                sem((ROUNDS, 7)),
                sem((13, groups - 1)),
                sem((13, groups - 1)),
                sem((4, 7)),
                sem((4, 7)),
                sem((4, 7)),
                sem((4, 7)),
            ],
            compiler_params=pltpu.CompilerParams(
                collective_id=0, has_side_effects=True, vmem_limit_bytes=VMEM_BYTES
            ),
            name="train_step",
        )(
            features,
            adjacency,
            labels,
            train_mask,
            input_weight,
            input_moment,
            conv_weight,
            conv_moment,
            head_weight,
            head_first,
            head_second,
            head_bias[None, :],
            bias_first[None, :],
            bias_second[None, :],
            norm_params,
            norm_first,
            norm_second,
        )
        small, in_new, in_m, conv_new, conv_m, h_new, h_f, h_s, n_new, n_f, n_s = outs
        return (
            small[3, :2],
            in_new,
            in_m,
            conv_new,
            conv_m,
            h_new,
            h_f,
            h_s,
            small[0, :classes],
            small[1, :classes],
            small[2, :classes],
            n_new,
            n_f,
            n_s,
        )

    return call


def solution(mesh):
    placed = (
        P("grp", "node", None),
        P("grp", "node", None),
        P("grp", "node"),
        P("grp", "node"),
        P(None, "grp"),
        P(None, "grp"),
        P(None, None, "grp"),
        P(None, None, "grp"),
        P(),
        P(),
        P(),
        P(),
        P(),
        P(),
        P(),
        P(),
        P(),
    )
    small = mesh.shape["node"] == 8 and mesh.shape["grp"] == 4
    return jax.shard_map(
        planned(mesh) if small else per_device,
        mesh=mesh,
        in_specs=placed,
        out_specs=(
            P(),
            P(None, "grp"),
            P(None, "grp"),
            P(None, None, "grp"),
            P(None, None, "grp"),
            P(),
            P(),
            P(),
            P(),
            P(),
            P(),
            P(),
            P(),
            P(),
        ),
        check_vma=False,
    )
```

```python
import functools

import jax
import jax.numpy as jnp
from jax import lax
from jax.experimental import pallas as pl
from jax.experimental.pallas import tpu as pltpu
from jax.sharding import PartitionSpec as P

NS_STEPS = 5
STEP = 10


norm_eps = 1e-05
smoothing = 0.1
poly_first = 3.4445
poly_second = -4.775
poly_third = 2.0315
muon_beta = 0.95
muon_rate = 0.2
decay_rate = 0.01
adam_rate = 0.05
beta_first = 0.9
beta_second = 0.95
adam_eps = 1e-08


def lowered(value):
    return value.astype(jnp.bfloat16)


def matmul_hi(left, right):
    return jnp.dot(left, right, precision=lax.Precision.HIGHEST)


def column_dot(left, right):
    return lax.dot_general(
        left, right, (((0,), (0,)), ((), ())), preferred_element_type=jnp.float32
    )


def row_dot(left, right):
    return lax.dot_general(
        left, right, (((1,), (1,)), ((), ())), preferred_element_type=jnp.float32
    )


def neighbour_sum(adj, values):
    return jnp.dot(
        adj, lax.all_gather(values, "node", axis=0, tiled=True), preferred_element_type=jnp.float32
    )


def neighbour_back(adj, grads):
    return lax.psum_scatter(column_dot(adj, grads), "node", scatter_dimension=0, tiled=True)


def layer_forward(adj, inputs_low, weight_low, gain, shift, total_rows):
    hidden = weight_low.shape[1]
    agg_low = lowered(neighbour_sum(adj, inputs_low))
    pre = jnp.dot(inputs_low, weight_low[:hidden], preferred_element_type=jnp.float32)
    pre = pre + jnp.dot(agg_low, weight_low[hidden:], preferred_element_type=jnp.float32)
    act = jax.nn.gelu(pre)
    sums, squares = lax.psum((jnp.sum(act, 0), jnp.sum(act * act, 0)), "node")
    mean = sums / total_rows
    var = squares / total_rows - mean * mean
    inv_std = lax.rsqrt(var + norm_eps)
    normed = (act - mean) * inv_std
    return (normed * gain + shift, (inputs_low, agg_low, pre, normed, inv_std))


def layer_backward(adj, weight_low, gain, kept, grad_out, total_rows):
    inputs_low, agg_low, pre, normed, inv_std = kept
    hidden = weight_low.shape[1]
    grad_gain = jnp.sum(grad_out * normed, 0)
    grad_shift = jnp.sum(grad_out, 0)
    grad_normed = grad_out * gain
    first, second = lax.psum((jnp.sum(grad_normed, 0), jnp.sum(grad_normed * normed, 0)), "node")
    grad_act = (grad_normed - first / total_rows - normed * (second / total_rows)) * inv_std
    grad_pre = jax.vjp(jax.nn.gelu, pre)[1](grad_act)[0]
    pre_low = lowered(grad_pre)
    grad_weight = jnp.concatenate(
        [column_dot(inputs_low, pre_low), column_dot(agg_low, pre_low)], 0
    )
    grad_agg = lowered(row_dot(pre_low, weight_low[hidden:]))
    grad_inputs = row_dot(pre_low, weight_low[:hidden]) + neighbour_back(adj, grad_agg)
    return (grad_inputs, grad_weight, jnp.stack([grad_gain, grad_shift]))


def gram_of(block):
    return matmul_hi(block, block.T)


def orthogonal_blocks(first_block, second_block, third_block):
    blocks = [first_block, second_block, third_block]
    for step in range(NS_STEPS):
        grams = lax.psum((gram_of(blocks[0]), gram_of(blocks[1]), gram_of(blocks[2])), "grp")
        grams = list(grams)
        if step == 0:
            scales = [jnp.sqrt(jnp.trace(gram)) + 1e-07 for gram in grams]
            blocks = [block / scale for block, scale in zip(blocks, scales)]
            grams = [gram / (scale * scale) for gram, scale in zip(grams, scales)]
        polys = [poly_second * gram + poly_third * matmul_hi(gram, gram) for gram in grams]
        blocks = [poly_first * block + matmul_hi(poly, block) for block, poly in zip(blocks, polys)]
    return blocks


def adamw(weight, grad, first, second):
    first_new = beta_first * first + (1.0 - beta_first) * grad
    second_new = beta_second * second + (1.0 - beta_second) * grad * grad
    fixed_first = first_new / (1.0 - beta_first**STEP)
    fixed_second = second_new / (1.0 - beta_second**STEP)
    update = fixed_first / (jnp.sqrt(fixed_second) + adam_eps) + decay_rate * weight
    return (weight - adam_rate * update, first_new, second_new)


def per_device(
    features,
    adjacency,
    labels,
    train_mask,
    input_weight,
    input_moment,
    conv_weight,
    conv_moment,
    head_weight,
    head_first,
    head_second,
    head_bias,
    bias_first,
    bias_second,
    norm_params,
    norm_first,
    norm_second,
):
    layers = conv_weight.shape[0]
    hidden = head_weight.shape[0]
    classes = head_weight.shape[1]
    f_width = input_weight.shape[0]
    total_rows = features.shape[1] * lax.axis_size("node")
    input_full, conv_full = (
        lax.all_gather(lowered(input_weight), "grp", axis=1, tiled=True),
        lax.all_gather(lowered(conv_weight), "grp", axis=2, tiled=True),
    )
    head_low = lowered(head_weight)
    count = lax.psum(jnp.sum(train_mask).astype(jnp.float32), ("grp", "node"))
    grad_input = jnp.zeros((f_width, hidden), jnp.float32)
    grad_conv = [jnp.zeros((2 * hidden, hidden), jnp.float32) for layer in range(layers)]
    grad_norm = [jnp.zeros((2, hidden), jnp.float32) for layer in range(layers)]
    grad_head = jnp.zeros((hidden, classes), jnp.float32)
    grad_bias = jnp.zeros((classes,), jnp.float32)
    loss_sum = jnp.float32(0.0)
    for graph in range(features.shape[0]):
        inputs = features[graph]
        adj = adjacency[graph]
        current_low = lowered(jnp.dot(inputs, input_full, preferred_element_type=jnp.float32))
        kept_list = []
        for layer in range(layers):
            output, kept = layer_forward(
                adj,
                current_low,
                conv_full[layer],
                norm_params[layer, 0],
                norm_params[layer, 1],
                total_rows,
            )
            kept_list.append(kept)
            current_low = lowered(output)
        logits = jnp.dot(current_low, head_low, preferred_element_type=jnp.float32) + head_bias
        logp = jax.nn.log_softmax(logits, -1)
        onehot = (labels[graph][:, None] == jnp.arange(classes, dtype=jnp.int32)[None, :]).astype(
            jnp.float32
        )
        target = (1.0 - smoothing) * onehot + smoothing / classes
        weights = train_mask[graph].astype(jnp.float32)
        loss_sum = loss_sum - jnp.sum(weights * jnp.sum(target * logp, -1))
        logits_low = lowered((weights / count)[:, None] * (jnp.exp(logp) - target))
        grad_head = grad_head + column_dot(current_low, logits_low)
        grad_bias = grad_bias + jnp.sum(logits_low.astype(jnp.float32), 0)
        grad_low = lowered(row_dot(logits_low, head_low))
        for layer in reversed(range(layers)):
            grad_inputs, grad_weight, grad_pair = layer_backward(
                adj,
                conv_full[layer],
                norm_params[layer, 0],
                kept_list[layer],
                grad_low.astype(jnp.float32),
                total_rows,
            )
            grad_conv[layer] = grad_conv[layer] + grad_weight
            grad_norm[layer] = grad_norm[layer] + grad_pair
            grad_low = lowered(grad_inputs)
        grad_input = grad_input + column_dot(inputs, grad_low)
    grad_conv_all = jnp.stack(grad_conv)
    grad_norm_all = jnp.stack(grad_norm)
    grad_input, grad_conv_all, grad_head, grad_bias, grad_norm_all, loss_sum = lax.psum(
        (grad_input, grad_conv_all, grad_head, grad_bias, grad_norm_all, loss_sum), "node"
    )
    grad_input, grad_conv_all = (
        lax.psum_scatter(grad_input, "grp", scatter_dimension=1, tiled=True),
        lax.psum_scatter(grad_conv_all, "grp", scatter_dimension=2, tiled=True),
    )
    grad_head, grad_bias, grad_norm_all, loss_sum = lax.psum(
        (grad_head, grad_bias, grad_norm_all, loss_sum), "grp"
    )
    moment_in = muon_beta * input_moment + grad_input
    moment_conv = muon_beta * conv_moment + grad_conv_all
    ortho_in, ortho_first, ortho_second = orthogonal_blocks(
        moment_in, moment_conv[0], moment_conv[1]
    )
    factor_in = 0.2 * float(max(f_width, hidden)) ** 0.5
    factor_conv = 0.2 * float(2 * hidden) ** 0.5
    input_new = input_weight - muon_rate * (factor_in * ortho_in + decay_rate * input_weight)
    ortho_conv = jnp.stack([ortho_first, ortho_second])
    conv_new = conv_weight - muon_rate * (factor_conv * ortho_conv + decay_rate * conv_weight)
    head_new, head_first_new, head_second_new = adamw(
        head_weight, grad_head, head_first, head_second
    )
    bias_new, bias_first_new, bias_second_new = adamw(head_bias, grad_bias, bias_first, bias_second)
    norm_new, norm_first_new, norm_second_new = adamw(
        norm_params, grad_norm_all, norm_first, norm_second
    )
    loss_parts = jnp.stack([loss_sum, count])
    return (
        loss_parts,
        input_new,
        moment_in,
        conv_new,
        moment_conv,
        head_new,
        head_first_new,
        head_second_new,
        bias_new,
        bias_first_new,
        bias_second_new,
        norm_new,
        norm_first_new,
        norm_second_new,
    )

MESH = pl.DeviceIdType.MESH
NT = (((1,), (1,)), ((), ()))
NN = (((1,), (0,)), ((), ()))
VMEM_BYTES = 56 * 1024 * 1024
ROUNDS = 8


def flip(index, bit):
    return index + bit - 2 * bit * lax.rem(lax.div(index, bit), 2)


def dot(left, right, dims=NN):
    return lax.dot_general(left, right, dims, preferred_element_type=jnp.float32)


def split(value):
    high = lowered(value)
    return high, lowered(value - high.astype(jnp.float32))


def dot_three(left, right, dims=NN):
    left_high, left_rest = left
    right_high, right_rest = right
    axis = dims[0][1][0]
    return dot(
        jnp.concatenate([left_high, left_high, left_rest], 1),
        jnp.concatenate([right_high, right_rest, right_high], axis),
        dims,
    )


def step_kernel(
    groups,
    classes,
    feat,
    adj,
    labels,
    train,
    w_in,
    m_in,
    w_conv,
    m_conv,
    w_head,
    f_head,
    s_head,
    w_bias,
    f_bias,
    s_bias,
    w_norm,
    f_norm,
    s_norm,
    o_loss,
    o_in,
    o_in_m,
    o_conv,
    o_conv_m,
    o_head,
    o_head_f,
    o_head_s,
    o_bias,
    o_bias_f,
    o_bias_s,
    o_norm,
    o_norm_f,
    o_norm_s,
    av,
    xg,
    hg,
    dg,
    pad,
    padh,
    wa,
    wb,
    wn,
    wt_head,
    h0,
    agg,
    act,
    slope,
    ms,
    axh,
    accx,
    acc,
    h2,
    dh,
    dp,
    gt,
    q1,
    q2,
    tall_in,
    ght,
    st,
    zs,
    sums,
    mpc,
    mit,
    mi,
    gbc,
    gbi,
    gbh,
    rsc,
    rsi,
    rsh,
    zc,
    zi,
    zh,
    mf,
    mfi,
    hf,
    y_conv,
    y_in,
    loc,
    ga_s,
    ga_r,
    st_s,
    st_r,
    z_s,
    z_r,
    zf_s,
    zf_r,
    rs_s,
    rs_r,
    ag_s,
    ag_r,
):
    f32 = jnp.float32
    bf16 = jnp.bfloat16
    width, graphs, rows = feat.shape
    total = adj.shape[2]
    hidden = w_head.shape[1]
    wide = 2 * hidden
    shard = hidden // groups
    part = shard // 4
    half = rows // 2
    span_in = 16 * ((width + 15) // 16)
    chunk = min(rows, 128)
    chunks = rows // chunk
    g = lax.axis_index("grp")
    me = lax.axis_index("node")
    core = lax.rem(me, 2)
    chip = lax.div(me, 2)
    n_sib, n_x, n_y, n_d = flip(me, 1), flip(me, 2), flip(me, 4), flip(flip(me, 2), 4)
    peers = [n_d, flip(n_d, 1), n_x, n_y, flip(n_x, 1), flip(n_y, 1), n_sib]
    z_peers = [lax.rem(g + d, groups) for d in range(1, groups)]
    z_from = [lax.rem(g + groups - d, groups) for d in range(1, groups)]
    started = []

    def send(src, dst, s_sem, r_sem, group, node):
        copy = pltpu.make_async_remote_copy(
            src_ref=src,
            dst_ref=dst,
            send_sem=s_sem,
            recv_sem=r_sem,
            device_id=(group, node),
            device_id_type=MESH,
        )
        copy.start()
        started.append(copy)
        return copy

    def lanes_of_core(span):
        return pl.ds(pl.multiple_of(core * span, span), span)

    barrier = pltpu.get_barrier_semaphore()
    for node in peers:
        pl.semaphore_signal(barrier, inc=1, device_id=(g, node), device_id_type=MESH)
    for group in z_peers:
        pl.semaphore_signal(barrier, inc=1, device_id=(group, me), device_id_type=MESH)

    own_a = [pltpu.make_async_copy(adj.at[s], av.at[s], loc.at[s]) for s in range(graphs)]
    part_rows = pl.ds(pl.multiple_of(chip * part, part), part)
    core_lanes = lanes_of_core(hidden)
    own_m = [
        pltpu.make_async_copy(m_conv.at[l, part_rows, core_lanes], mpc.at[l, g], loc.at[graphs + l])
        for l in range(2)
    ]
    for copy in own_a + own_m:
        copy.start()

    high_rows = pl.ds(pl.multiple_of(g * shard, shard), shard)
    padh[...] = jnp.zeros_like(padh)
    for s in range(graphs):
        padh[pl.ds(0, width), :] = feat[:, s, :].astype(f32)
        xg[s, me] = lowered(padh[pl.ds(0, span_in), :])
    mit[...] = jnp.zeros_like(mit)
    mit[high_rows, pl.ds(0, width)] = w_in[...]
    wa[high_rows, pl.ds(0, wide)] = lowered(w_conv[0])
    wa[high_rows, pl.ds(wide, 128)] = lowered(mit[high_rows, :])
    wb[high_rows, :] = lowered(w_conv[1])
    pl.semaphore_wait(barrier, 7 + groups - 1)

    def gather_of(index, ref, by_lane=False):
        low, high = pl.ds(0, half), pl.ds(half, half)

        def go(j, node, block, span=None):
            view = ref.at[block]
            if span is not None:
                view = ref.at[block, :, span] if by_lane else ref.at[block, span]
            return send(view, view, ga_s.at[index, j], ga_r.at[index, j], g, node)

        kept = {}

        def own():
            kept[0] = go(0, n_x, me, low)
            kept[1] = go(1, n_y, me, high)
            kept[6] = go(6, n_sib, me)
            kept[2] = go(2, n_x, me, high)
            kept[3] = go(3, n_y, me, low)

        def relay():
            kept[0].wait_recv()
            kept[4] = go(4, n_y, n_x, low)
            kept[1].wait_recv()
            kept[5] = go(5, n_x, n_y, high)

        def near():
            kept[2].wait_recv()
            kept[7] = go(7, n_sib, n_x)
            kept[3].wait_recv()
            kept[8] = go(8, n_sib, n_y)

        def far():
            kept[4].wait_recv()
            kept[5].wait_recv()
            kept[9] = go(9, n_sib, n_d)

        def near_ready():
            for j in (6, 7, 8):
                kept[j].wait_recv()

        def far_ready():
            kept[9].wait_recv()

        return own, relay, near, far, near_ready, far_ready

    def chip_at(i):
        cx = lax.rem(lax.rem(chip, 2) + lax.rem(i, 2), 2)
        cy = lax.rem(lax.div(chip, 2) + lax.div(i, 2), 2)
        return cx + 2 * cy

    def product(s, ref, out, first, last):
        if first == 0:
            out[...] = jnp.zeros_like(out)

        def body(i, carry):
            c = chip_at(i)
            block = ref[pl.ds(2 * c, 2)].reshape(2 * rows, ref.shape[2])
            left = av[s, :, pl.ds(pl.multiple_of(c * 2 * rows, 2 * rows), 2 * rows)]
            out[...] += dot(left, block)
            return carry

        lax.fori_loop(first, last, body, 0)

    def product_x(s, first, last):
        if first == 0:
            accx[...] = jnp.zeros_like(accx)

        def body(i, carry):
            block = 2 * chip_at(lax.div(i, 2)) + lax.rem(i, 2)
            left = av[s, :, pl.ds(pl.multiple_of(block * rows, rows), rows)]
            accx[...] += dot(left, xg[s, block], NT)
            return carry

        lax.fori_loop(2 * first, 2 * last, body, 0)

    def over_rows(body, carry):
        def one(i, value):
            return body(pl.ds(pl.multiple_of(i * chunk, chunk), chunk), value)

        return lax.fori_loop(0, chunks, one, carry)

    def fold(value):
        return jnp.sum(value.reshape(chunk // 8, 8, hidden), 0)

    st_copies = {}

    def plane_send(k):
        view = st.at[k, me]
        st_copies[k] = [
            send(view, view, st_s.at[k, i], st_r.at[k, i], g, node) for i, node in enumerate(peers)
        ]

    def plane_sum(k):
        for copy in st_copies[k]:
            copy.wait_recv()
        value = st[k, 0]
        for i in range(1, 8):
            value = value + st[k, i]
        return value

    z_copies = {}

    def z_send(k, view):
        z_copies[k] = [
            send(view, view, z_s.at[k, i], z_r.at[k, i], group, me)
            for i, group in enumerate(z_peers)
        ]

    def z_wait(k):
        for copy in z_copies[k]:
            copy.wait_recv()

    x_g = [gather_of(s, xg.at[s], True) for s in range(2)]
    h_g = [gather_of(2 + s, hg.at[s]) for s in range(2)]
    d_g = [gather_of(4 + s, dg.at[s]) for s in range(2)]

    own_rows = pl.ds(pl.multiple_of(g * shard, shard), shard)
    strip = shard // 2

    def strip_of(group):
        return pl.ds(pl.multiple_of(group * shard + core * strip, strip), strip)

    forwards = {}

    def z_forward(k, ref):
        forwards[k] = []
        for i, group in enumerate(z_from):
            z_copies[k][i].wait_recv()
            view = ref.at[strip_of(group)]
            forwards[k].append(send(view, view, zf_s.at[k, i], zf_r.at[k, i], g, n_sib))

    def z_forwarded(k):
        for copy in forwards[k]:
            copy.wait_recv()

    x_g[0][0]()
    z_send(0, wa.at[strip_of(g)])
    mit[high_rows, pl.ds(0, width)] = m_in[...]
    x_g[0][1]()
    x_g[1][0]()
    z_send(1, wb.at[strip_of(g)])
    padh[...] = jnp.zeros_like(padh)
    padh[pl.ds(0, classes), pl.ds(0, hidden)] = w_head[...]
    wt_head[...] = lowered(padh[:, :hidden])
    pad[...] = jnp.zeros_like(pad)
    pad[pl.ds(0, 8), pl.ds(0, classes)] = jnp.broadcast_to(w_bias[...], (8, classes))
    bias_col = pad[...].T[:64, :1]
    count_own = jnp.sum(train[...].astype(f32), axis=1, keepdims=True)
    count_own = count_own[0:1] + count_own[1:2]
    x_g[0][2]()
    for copy in own_m:
        copy.wait()
    for copy in own_a:
        copy.wait()

    def forward_act(s, l, k, first, second, w_first, w_second):
        acc[...] = dot(first, w_first) + dot(second, w_second)

        def body(span, carry):
            pre = acc[span, :]
            square = pre * pre
            inner = 0.7978845608028654 * pre * (1.0 + 0.044715 * square)
            t = jnp.tanh(inner)
            value = 0.5 * pre * (1.0 + t)
            act[l, s, span, :] = value
            slope[l, s, span, :] = 0.5 * (1.0 + t) + 0.5 * pre * (1.0 - t * t) * (
                0.7978845608028654 * (1.0 + 3.0 * 0.044715 * square)
            )
            return carry[0] + fold(value), carry[1] + fold(value * value)

        zero = jnp.zeros((8, hidden), f32)
        one, two = over_rows(body, (zero, zero))
        st[k, me] = jnp.zeros((8, hidden), f32)
        st[k, me, 0:1, :] = jnp.sum(one, 0, keepdims=True)
        st[k, me, 1:2, :] = jnp.sum(two, 0, keepdims=True)
        if k == 0:
            st[k, me, 2:3, :] = jnp.broadcast_to(count_own, (1, hidden))
        plane_send(k)

    def normalise(s, l, k, out):
        sums_all = plane_sum(k)
        mean = sums_all[0:1] / total
        var = sums_all[1:2] / total - mean * mean
        inv = lax.rsqrt(var + norm_eps)
        ms[l, s, 0:1, :] = inv
        gain, shift = w_norm[l, 0:1, :], w_norm[l, 1:2, :]

        def body(span, carry):
            normed = (act[l, s, span, :] - mean) * inv
            act[l, s, span, :] = normed
            out[span, :] = lowered(normed * gain + shift)
            return carry

        over_rows(body, 0)
        return sums_all

    def layer_zero(s):
        high, rest = split(accx[...])
        axh[s] = high
        w = wa[:, wide : wide + span_in]
        agg[0, s] = lowered(dot(high, w, NT) + dot(rest, w, NT))
        h0[s] = lowered(dot(xg[s, me].T, w, NT))
        forward_act(s, 0, s, h0[s], agg[0, s], wn[0, :hidden, :], wn[0, hidden:, :])

    def layer_one(s):
        agg[1, s] = lowered(acc[...])
        forward_act(s, 1, 2 + s, hg[s, me], agg[1, s], wn[1, :hidden, :], wn[1, hidden:, :])

    def head(s, count):
        value = h2[s]
        logits = dot(wt_head[pl.ds(0, 64), :], value, NT) + bias_col
        at = lax.broadcasted_iota(jnp.int32, (64, rows), 0)
        valid = at < classes
        logits = jnp.where(valid, logits, -1e30)
        shifted = logits - jnp.max(logits, 0, keepdims=True)
        logp = shifted - jnp.log(jnp.sum(jnp.exp(shifted), 0, keepdims=True))
        onehot = jnp.where(at == labels[s : s + 1, :], 1.0, 0.0)
        target = jnp.where(valid, (1.0 - smoothing) * onehot + smoothing / classes, 0.0)
        weights = train[s : s + 1, :].astype(f32)
        node_loss = jnp.sum(target * logp, 0, keepdims=True)
        loss = -jnp.sum(weights * node_loss, axis=1, keepdims=True)
        delta = (weights / count) * (jnp.exp(logp) - target)
        delta_low = lowered(delta)
        value_t = dot(delta_low, value)
        ght[...] = value_t if s == 0 else ght[...] + value_t
        column = dot(jnp.ones((8, rows), bf16), delta_low, NT)
        tall = jnp.concatenate([delta_low.astype(f32), jnp.zeros((64, rows), f32)], 0).T
        dh[s] = lowered(dot(lowered(tall), wt_head[...])).astype(f32)
        return loss, column

    def backward_sums(s, l, k, extra=None):
        def body(span, carry):
            grad = dh[s, span, :]
            return carry[0] + fold(grad), carry[1] + fold(grad * act[l, s, span, :])

        zero = jnp.zeros((8, hidden), f32)
        one, two = over_rows(body, (zero, zero))
        st[k, me] = jnp.zeros((8, hidden), f32)
        st[k, me, 0:1, :] = jnp.sum(one, 0, keepdims=True)
        st[k, me, 1:2, :] = jnp.sum(two, 0, keepdims=True)
        if extra is not None:
            st[k, me, 2:3, 0:64] = extra[1][0:1]
            st[k, me, 3:4, :] = jnp.broadcast_to(extra[0], (1, hidden))
        plane_send(k)

    def backward_pre(s, l, k):
        sums_all = plane_sum(k)
        sums[1 - l] = sums_all if s == 0 else sums[1 - l] + sums_all
        gain = w_norm[l, 0:1, :]
        inv = ms[l, s, 0:1, :]
        first = gain * sums_all[0:1] / total
        second = gain * sums_all[1:2] / total

        def body(span, carry):
            grad = dh[s, span, :] * gain - first - act[l, s, span, :] * second
            dp[l, s, span, :] = lowered(grad * inv * slope[l, s, span, :])
            return carry

        over_rows(body, 0)

    def conv_grads(s, l, left, right):
        turned = dp[l, s].T
        one, two = dot(turned, left), dot(turned, right)
        if s == 0:
            gt[l, :, :hidden] = one
            gt[l, :, hidden:] = two
        else:
            gt[l, :, :hidden] += one
            gt[l, :, hidden:] += two
        return turned

    rs_copies = {}

    def pieces_send(k, src, dst, where):
        rs_copies[k] = []
        for i, node in enumerate(peers):
            rs_copies[k].append(
                send(where(src, node), dst.at[me], rs_s.at[k, i], rs_r.at[k, i], g, node)
            )

    def pieces_sum(k, src, dst, own):
        dst[me] = own
        for copy in rs_copies[k]:
            copy.wait_recv()
        value = dst[0].astype(f32)
        for i in range(1, 8):
            value = value + dst[i].astype(f32)
        return value

    def conv_piece(ref, node):
        n_core, n_chip = lax.rem(node, 2), lax.div(node, 2)
        return ref.at[:, n_chip, :, pl.ds(pl.multiple_of(n_core * hidden, hidden), hidden)]

    def in_piece(ref, node):
        return ref.at[node]

    def head_piece(ref, node):
        n_core, n_chip = lax.rem(node, 2), lax.div(node, 2)
        return ref.at[n_chip, :, pl.ds(pl.multiple_of(n_core * (hidden // 2), hidden // 2), hidden // 2)]

    def over_z(k, buf):
        z_wait(k)
        value = buf[0].astype(f32)
        for i in range(1, groups):
            value = value + buf[i].astype(f32)
        return value

    ag_copies = {}

    def spread(k, view_of):
        view = view_of(me)
        ag_copies[k] = [
            send(view, view, ag_s.at[k, i], ag_r.at[k, i], g, node)
            for i, node in enumerate((n_d, n_x, n_y, n_sib))
        ]

    def spread_forward(k, view_of):
        for i, node in ((1, n_x), (2, n_y), (0, n_d)):
            ag_copies[k][i].wait_recv()
            view = view_of(node)
            ag_copies[k].append(
                send(view, view, ag_s.at[k, 4 + i], ag_r.at[k, 4 + i], g, n_sib)
            )

    def spread_wait(k):
        for copy in ag_copies[k][3:]:
            copy.wait_recv()

    head_lanes = lanes_of_core(hidden // 2)

    x_g[0][4]()
    product_x(0, 0, 3)
    x_g[1][1]()
    x_g[0][3]()
    z_forward(0, wa)
    x_g[0][5]()
    product_x(0, 3, 4)
    z_forwarded(0)
    wn[0] = wa[:, :wide].T
    layer_zero(0)
    x_g[1][2]()
    x_g[1][4]()
    product_x(1, 0, 3)
    x_g[1][3]()
    x_g[1][5]()
    product_x(1, 3, 4)
    layer_zero(1)
    count_plane = normalise(0, 0, 0, hg.at[0, me])
    h_g[0][0]()
    zs[0, g] = count_plane
    z_send(3, zs.at[0, g])
    z_forward(1, wb)
    normalise(1, 0, 1, hg.at[1, me])
    h_g[0][1]()
    h_g[1][0]()
    z_send(6, mpc.at[0, g])
    z_send(7, mpc.at[1, g])
    z_send(8, mit.at[own_rows])
    z_forwarded(1)
    wn[1] = wb[...].T
    h_g[0][2]()
    h_g[0][4]()
    product(0, hg.at[0], acc, 0, 3)
    h_g[0][3]()
    h_g[1][1]()
    h_g[0][5]()
    product(0, hg.at[0], acc, 3, 4)
    layer_one(0)
    z_wait(3)
    count = zs[0, 0]
    for i in range(1, groups):
        count = count + zs[0, i]
    count = count[2:3, 0:1]
    normalise(0, 1, 2, h2.at[0])
    loss_row = head(0, count)
    backward_sums(0, 1, 4, loss_row)
    h_g[1][2]()
    h_g[1][3]()
    backward_pre(0, 1, 4)
    dg[0, me] = lowered(dot(dp[1, 0], wb[:, hidden:]))
    d_g[0][0]()
    h_g[1][4]()
    product(1, hg.at[1], acc, 0, 3)
    h_g[1][5]()
    product(1, hg.at[1], acc, 3, 4)
    layer_one(1)
    conv_grads(0, 1, hg[0, me], agg[1, 0])
    dh[0] = dot(dp[1, 0], wb[:, :hidden])
    normalise(1, 1, 3, h2.at[1])
    loss_row = head(1, count)
    backward_sums(1, 1, 5, loss_row)
    d_g[0][1]()
    backward_pre(1, 1, 5)
    dg[1, me] = lowered(dot(dp[1, 1], wb[:, hidden:]))
    d_g[1][0]()
    conv_grads(1, 1, hg[1, me], agg[1, 1])
    dh[1] = dot(dp[1, 1], wb[:, :hidden])
    gbc[1] = lowered(gt[1]).reshape(groups, 4, part, wide)
    gbh[...] = lowered(ght[...]).reshape(4, 16, hidden)
    zs[1, g] = sums[0]
    z_send(4, zs.at[1, g])
    d_g[0][2]()
    d_g[0][4]()
    product(0, dg.at[0], acc, 0, 3)
    d_g[0][3]()
    d_g[1][1]()
    d_g[0][5]()
    product(0, dg.at[0], acc, 3, 4)
    dh[0] = lowered(dh[0] + acc[...]).astype(f32)
    backward_sums(0, 0, 6)
    pieces_send(0, gbc.at[1], rsc.at[1], conv_piece)
    pieces_send(1, gbh, rsh, head_piece)
    d_g[1][2]()
    d_g[1][4]()
    product(1, dg.at[1], acc, 0, 3)
    d_g[1][3]()
    backward_pre(0, 0, 6)
    turned = conv_grads(0, 0, h0[0], agg[0, 0])
    q1[...] = dot(turned, xg[0, me], NT)
    q2[...] = dot(turned, axh[0])
    d_g[1][5]()
    product(1, dg.at[1], acc, 3, 4)
    dh[1] = lowered(dh[1] + acc[...]).astype(f32)
    backward_sums(1, 0, 7)
    zc[1, g] = lowered(pieces_sum(0, None, rsc.at[1], conv_piece(gbc.at[1], me)[...]))
    z_send(9, zc.at[1, g])
    zh[g] = lowered(pieces_sum(1, None, rsh, head_piece(gbh, me)[...]))
    z_send(10, zh.at[g])
    backward_pre(1, 0, 7)
    turned = conv_grads(1, 0, h0[1], agg[0, 1])
    q1[...] += dot(turned, xg[1, me], NT)
    q2[...] += dot(turned, axh[1])
    gbc[0] = lowered(gt[0]).reshape(groups, 4, part, wide)
    pieces_send(2, gbc.at[0], rsc.at[0], conv_piece)
    one, two = split(q1[...]), split(q2[...])
    w_self, w_near = wn[0, :hidden, :], wn[0, hidden:, :]
    g_in = dot(w_self, one[0]) + dot(w_self, one[1]) + dot(w_near, two[0]) + dot(w_near, two[1])
    tall_in[:, pl.ds(0, span_in)] = g_in
    gbi[...] = lowered(tall_in[...].T).reshape(8, 16, hidden)
    pieces_send(3, gbi, rsi, in_piece)
    zs[2, g] = sums[1]
    z_send(5, zs.at[2, g])

    def conv_view(l):
        return lambda node: conv_piece(mf.at[l], node)

    def head_view(node):
        return head_piece(hf, node)

    def in_view(node):
        return mfi.at[node]

    z_wait(7)
    mf[1, :, chip, :, core_lanes] = muon_beta * mpc[1] + over_z(9, zc.at[1])
    spread(0, conv_view(1))
    hf[chip, :, head_lanes] = over_z(10, zh)
    spread(1, head_view)
    z_wait(6)
    z_wait(8)
    tall_in[...] = mit[...]
    mi[...] = tall_in[...].T.reshape(8, 16, hidden)
    zc[0, g] = lowered(pieces_sum(2, None, rsc.at[0], conv_piece(gbc.at[0], me)[...]))
    z_send(11, zc.at[0, g])
    zi[g] = lowered(pieces_sum(3, None, rsi, gbi[me]))
    z_send(12, zi.at[g])
    spread_forward(0, conv_view(1))
    spread_forward(1, head_view)
    mf[0, :, chip, :, core_lanes] = muon_beta * mpc[0] + over_z(11, zc.at[0])
    spread(2, conv_view(0))
    mfi[me] = muon_beta * mi[me] + over_z(12, zi)
    spread(3, in_view)

    def scaled(value):
        norm = jnp.sqrt(jnp.sum(jnp.sum(value * value, 0, keepdims=True), 1, keepdims=True))
        return value / (norm + 1e-07)

    def iterate(refs):
        def body(i, carry):
            for ref in refs:
                value = ref[...]
                pair = split(value)
                gram = dot_three(pair, pair, NT)
                gram_pair = split(gram)
                poly = split(poly_second * gram + poly_third * dot_three(gram_pair, gram_pair))
                ref[...] = poly_first * value + dot_three(poly, pair)
            return carry

        lax.fori_loop(0, NS_STEPS, body, 0)

    factor_conv = 0.2 * float(wide) ** 0.5
    factor_in = 0.2 * float(max(width, hidden)) ** 0.5

    def conv_out(l):
        o_conv_m[l] = mf[l, g].reshape(shard, wide)
        ortho = y_conv[l, own_rows, :]
        weight = w_conv[l]
        o_conv[l] = weight - muon_rate * (factor_conv * ortho + decay_rate * weight)

    spread_wait(0)
    y_conv[1] = scaled(mf[1].reshape(hidden, wide))
    iterate([y_conv.at[1]])
    spread_forward(2, conv_view(0))
    spread_forward(3, in_view)
    conv_out(1)

    def adam(weight, grad, first, second):
        return adamw(weight, grad, first, second)

    spread_wait(1)
    grad = hf[...].reshape(64, hidden)[:classes]
    o_head[...], o_head_f[...], o_head_s[...] = adam(w_head[...], grad, f_head[...], s_head[...])
    z_wait(4)
    z_wait(5)
    late = zs[1, 0]
    early = zs[2, 0]
    for i in range(1, groups):
        late = late + zs[1, i]
        early = early + zs[2, i]
    for l, rows_l in ((0, early), (1, late)):
        grad = jnp.concatenate([rows_l[1:2], rows_l[0:1]], 0)
        o_norm[l], o_norm_f[l], o_norm_s[l] = adam(w_norm[l], grad, f_norm[l], s_norm[l])
    o_bias[...], o_bias_f[...], o_bias_s[...] = adam(
        w_bias[...], late[2:3, :classes], f_bias[...], s_bias[...]
    )
    o_loss[...] = jnp.concatenate([late[3:4, 0:1], count], 1)

    spread_wait(2)
    spread_wait(3)
    y_conv[0] = scaled(mf[0].reshape(hidden, wide))
    y_in[...] = scaled(mfi[...].reshape(128, hidden))
    iterate([y_conv.at[0], y_in])
    conv_out(0)
    tall_in[...] = mfi[...].reshape(128, hidden).T
    o_in_m[...] = tall_in[own_rows, :][:, :width]
    tall_in[...] = y_in[...].T
    ortho = tall_in[own_rows, :][:, :width]
    weight = w_in[...]
    o_in[...] = weight - muon_rate * (factor_in * ortho + decay_rate * weight)
    for copy in started:
        copy.wait_send()


def planned(mesh):
    groups = mesh.shape["grp"]

    def call(
        features,
        adjacency,
        labels,
        train_mask,
        input_weight,
        input_moment,
        conv_weight,
        conv_moment,
        head_weight,
        head_first,
        head_second,
        head_bias,
        bias_first,
        bias_second,
        norm_params,
        norm_first,
        norm_second,
    ):
        f32, bf16 = jnp.float32, jnp.bfloat16
        graphs, rows, width = features.shape
        total = adjacency.shape[2]
        hidden, classes = head_weight.shape
        wide = 2 * hidden
        shard = hidden // groups
        part = shard // 4
        span_in = 16 * ((width + 15) // 16)
        vm = pltpu.VMEM
        sem = pltpu.SemaphoreType.DMA
        shape = jax.ShapeDtypeStruct
        near = pl.BlockSpec(memory_space=pltpu.VMEM)
        anywhere = pl.BlockSpec(memory_space=pl.ANY)
        results = [
            shape((1, 2), f32),
            shape((shard, width), f32),
            shape((shard, width), f32),
            shape((2, shard, wide), f32),
            shape((2, shard, wide), f32),
            shape((classes, hidden), f32),
            shape((classes, hidden), f32),
            shape((classes, hidden), f32),
            shape((1, classes), f32),
            shape((1, classes), f32),
            shape((1, classes), f32),
            shape(norm_params.shape, f32),
            shape(norm_params.shape, f32),
            shape(norm_params.shape, f32),
        ]
        outs = pl.pallas_call(
            functools.partial(step_kernel, groups, classes),
            out_shape=results,
            in_specs=[near, anywhere, near, near, near, near, near, anywhere] + [near] * 9,
            out_specs=[near] * 14,
            scratch_shapes=[
                vm((graphs, rows, total), bf16),
                vm((graphs, 8, span_in, rows), bf16),
                vm((graphs, 8, rows, hidden), bf16),
                vm((graphs, 8, rows, hidden), bf16),
                vm((128, 128), f32),
                vm((128, rows), f32),
                vm((hidden, wide + 128), bf16),
                vm((hidden, wide), bf16),
                vm((2, wide, hidden), bf16),
                vm((128, hidden), bf16),
                vm((graphs, rows, hidden), bf16),
                vm((2, graphs, rows, hidden), bf16),
                vm((2, graphs, rows, hidden), f32),
                vm((2, graphs, rows, hidden), f32),
                vm((2, graphs, 8, hidden), f32),
                vm((graphs, rows, span_in), bf16),
                vm((rows, span_in), f32),
                vm((rows, hidden), f32),
                vm((graphs, rows, hidden), bf16),
                vm((graphs, rows, hidden), f32),
                vm((2, graphs, rows, hidden), bf16),
                vm((2, hidden, wide), f32),
                vm((hidden, span_in), f32),
                vm((hidden, span_in), f32),
                vm((hidden, 128), f32),
                vm((64, hidden), f32),
                vm((ROUNDS, 8, 8, hidden), f32),
                vm((3, groups, 8, hidden), f32),
                vm((2, 8, hidden), f32),
                vm((2, groups, part, hidden), f32),
                vm((hidden, 128), f32),
                vm((8, 16, hidden), f32),
                vm((2, groups, 4, part, wide), bf16),
                vm((8, 16, hidden), bf16),
                vm((4, 16, hidden), bf16),
                vm((2, 8, groups, part, hidden), bf16),
                vm((8, 16, hidden), bf16),
                vm((8, 16, hidden // 2), bf16),
                vm((2, groups, groups, part, hidden), bf16),
                vm((groups, 16, hidden), bf16),
                vm((groups, 16, hidden // 2), bf16),
                vm((2, groups, 4, part, wide), f32),
                vm((8, 16, hidden), f32),
                vm((4, 16, hidden), f32),
                vm((2, hidden, wide), f32),
                vm((128, hidden), f32),
                sem((graphs + 2,)),
                sem((6, 10)),
                sem((6, 10)),
                sem((ROUNDS, 7)),
                sem((ROUNDS, 7)),
                sem((13, groups - 1)),
                sem((13, groups - 1)),
                sem((2, groups - 1)),
                sem((2, groups - 1)),
                sem((4, 7)),
                sem((4, 7)),
                sem((4, 7)),
                sem((4, 7)),
            ],
            compiler_params=pltpu.CompilerParams(
                collective_id=0, has_side_effects=True, vmem_limit_bytes=VMEM_BYTES
            ),
            name="train_step",
        )(
            jnp.transpose(features, (2, 0, 1)),
            adjacency,
            labels,
            train_mask,
            input_weight.T,
            input_moment.T,
            jnp.swapaxes(conv_weight, 1, 2),
            jnp.swapaxes(conv_moment, 1, 2),
            head_weight.T,
            head_first.T,
            head_second.T,
            head_bias[None, :],
            bias_first[None, :],
            bias_second[None, :],
            norm_params,
            norm_first,
            norm_second,
        )
        outs = pl.pallas_call(
            hand_over,
            out_shape=results,
            in_specs=[near] * 14,
            out_specs=[near] * 14,
            name="hand_over",
        )(*outs)
        loss, in_new, in_m, conv_new, conv_m, h_new, h_f, h_s, b_new, b_f, b_s, *norms = outs
        return (
            loss[0],
            in_new.T,
            in_m.T,
            jnp.swapaxes(conv_new, 1, 2),
            jnp.swapaxes(conv_m, 1, 2),
            h_new.T,
            h_f.T,
            h_s.T,
            b_new[0],
            b_f[0],
            b_s[0],
            *norms,
        )

    return call


def hand_over(*refs):
    for source, target in zip(refs[:14], refs[14:]):
        target[...] = source[...]


def solution(mesh):
    placed = (
        P("grp", "node", None),
        P("grp", "node", None),
        P("grp", "node"),
        P("grp", "node"),
        P(None, "grp"),
        P(None, "grp"),
        P(None, None, "grp"),
        P(None, None, "grp"),
        P(),
        P(),
        P(),
        P(),
        P(),
        P(),
        P(),
        P(),
        P(),
    )
    small = mesh.shape["node"] == 8 and mesh.shape["grp"] == 4
    return jax.shard_map(
        planned(mesh) if small else per_device,
        mesh=mesh,
        in_specs=placed,
        out_specs=(
            P(),
            P(None, "grp"),
            P(None, "grp"),
            P(None, None, "grp"),
            P(None, None, "grp"),
            P(),
            P(),
            P(),
            P(),
            P(),
            P(),
            P(),
            P(),
            P(),
        ),
        check_vma=False,
    )
```

```python
import functools

import jax
import jax.numpy as jnp
from jax import lax
from jax.experimental import pallas as pl
from jax.experimental.pallas import tpu as pltpu
from jax.sharding import PartitionSpec as P

NS_STEPS = 5
STEP = 10


norm_eps = 1e-05
smoothing = 0.1
poly_first = 3.4445
poly_second = -4.775
poly_third = 2.0315
muon_beta = 0.95
muon_rate = 0.2
decay_rate = 0.01
adam_rate = 0.05
beta_first = 0.9
beta_second = 0.95
adam_eps = 1e-08


def lowered(value):
    return value.astype(jnp.bfloat16)


def matmul_hi(left, right):
    return jnp.dot(left, right, precision=lax.Precision.HIGHEST)


def column_dot(left, right):
    return lax.dot_general(
        left, right, (((0,), (0,)), ((), ())), preferred_element_type=jnp.float32
    )


def row_dot(left, right):
    return lax.dot_general(
        left, right, (((1,), (1,)), ((), ())), preferred_element_type=jnp.float32
    )


def neighbour_sum(adj, values):
    return jnp.dot(
        adj, lax.all_gather(values, "node", axis=0, tiled=True), preferred_element_type=jnp.float32
    )


def neighbour_back(adj, grads):
    return lax.psum_scatter(column_dot(adj, grads), "node", scatter_dimension=0, tiled=True)


def layer_forward(adj, inputs_low, weight_low, gain, shift, total_rows):
    hidden = weight_low.shape[1]
    agg_low = lowered(neighbour_sum(adj, inputs_low))
    pre = jnp.dot(inputs_low, weight_low[:hidden], preferred_element_type=jnp.float32)
    pre = pre + jnp.dot(agg_low, weight_low[hidden:], preferred_element_type=jnp.float32)
    act = jax.nn.gelu(pre)
    sums, squares = lax.psum((jnp.sum(act, 0), jnp.sum(act * act, 0)), "node")
    mean = sums / total_rows
    var = squares / total_rows - mean * mean
    inv_std = lax.rsqrt(var + norm_eps)
    normed = (act - mean) * inv_std
    return (normed * gain + shift, (inputs_low, agg_low, pre, normed, inv_std))


def layer_backward(adj, weight_low, gain, kept, grad_out, total_rows):
    inputs_low, agg_low, pre, normed, inv_std = kept
    hidden = weight_low.shape[1]
    grad_gain = jnp.sum(grad_out * normed, 0)
    grad_shift = jnp.sum(grad_out, 0)
    grad_normed = grad_out * gain
    first, second = lax.psum((jnp.sum(grad_normed, 0), jnp.sum(grad_normed * normed, 0)), "node")
    grad_act = (grad_normed - first / total_rows - normed * (second / total_rows)) * inv_std
    grad_pre = jax.vjp(jax.nn.gelu, pre)[1](grad_act)[0]
    pre_low = lowered(grad_pre)
    grad_weight = jnp.concatenate(
        [column_dot(inputs_low, pre_low), column_dot(agg_low, pre_low)], 0
    )
    grad_agg = lowered(row_dot(pre_low, weight_low[hidden:]))
    grad_inputs = row_dot(pre_low, weight_low[:hidden]) + neighbour_back(adj, grad_agg)
    return (grad_inputs, grad_weight, jnp.stack([grad_gain, grad_shift]))


def gram_of(block):
    return matmul_hi(block, block.T)


def orthogonal_blocks(first_block, second_block, third_block):
    blocks = [first_block, second_block, third_block]
    for step in range(NS_STEPS):
        grams = lax.psum((gram_of(blocks[0]), gram_of(blocks[1]), gram_of(blocks[2])), "grp")
        grams = list(grams)
        if step == 0:
            scales = [jnp.sqrt(jnp.trace(gram)) + 1e-07 for gram in grams]
            blocks = [block / scale for block, scale in zip(blocks, scales)]
            grams = [gram / (scale * scale) for gram, scale in zip(grams, scales)]
        polys = [poly_second * gram + poly_third * matmul_hi(gram, gram) for gram in grams]
        blocks = [poly_first * block + matmul_hi(poly, block) for block, poly in zip(blocks, polys)]
    return blocks


def adamw(weight, grad, first, second):
    first_new = beta_first * first + (1.0 - beta_first) * grad
    second_new = beta_second * second + (1.0 - beta_second) * grad * grad
    fixed_first = first_new / (1.0 - beta_first**STEP)
    fixed_second = second_new / (1.0 - beta_second**STEP)
    update = fixed_first / (jnp.sqrt(fixed_second) + adam_eps) + decay_rate * weight
    return (weight - adam_rate * update, first_new, second_new)


def per_device(
    features,
    adjacency,
    labels,
    train_mask,
    input_weight,
    input_moment,
    conv_weight,
    conv_moment,
    head_weight,
    head_first,
    head_second,
    head_bias,
    bias_first,
    bias_second,
    norm_params,
    norm_first,
    norm_second,
):
    layers = conv_weight.shape[0]
    hidden = head_weight.shape[0]
    classes = head_weight.shape[1]
    f_width = input_weight.shape[0]
    total_rows = features.shape[1] * lax.axis_size("node")
    input_full, conv_full = (
        lax.all_gather(lowered(input_weight), "grp", axis=1, tiled=True),
        lax.all_gather(lowered(conv_weight), "grp", axis=2, tiled=True),
    )
    head_low = lowered(head_weight)
    count = lax.psum(jnp.sum(train_mask).astype(jnp.float32), ("grp", "node"))
    grad_input = jnp.zeros((f_width, hidden), jnp.float32)
    grad_conv = [jnp.zeros((2 * hidden, hidden), jnp.float32) for layer in range(layers)]
    grad_norm = [jnp.zeros((2, hidden), jnp.float32) for layer in range(layers)]
    grad_head = jnp.zeros((hidden, classes), jnp.float32)
    grad_bias = jnp.zeros((classes,), jnp.float32)
    loss_sum = jnp.float32(0.0)
    for graph in range(features.shape[0]):
        inputs = features[graph]
        adj = adjacency[graph]
        current_low = lowered(jnp.dot(inputs, input_full, preferred_element_type=jnp.float32))
        kept_list = []
        for layer in range(layers):
            output, kept = layer_forward(
                adj,
                current_low,
                conv_full[layer],
                norm_params[layer, 0],
                norm_params[layer, 1],
                total_rows,
            )
            kept_list.append(kept)
            current_low = lowered(output)
        logits = jnp.dot(current_low, head_low, preferred_element_type=jnp.float32) + head_bias
        logp = jax.nn.log_softmax(logits, -1)
        onehot = (labels[graph][:, None] == jnp.arange(classes, dtype=jnp.int32)[None, :]).astype(
            jnp.float32
        )
        target = (1.0 - smoothing) * onehot + smoothing / classes
        weights = train_mask[graph].astype(jnp.float32)
        loss_sum = loss_sum - jnp.sum(weights * jnp.sum(target * logp, -1))
        logits_low = lowered((weights / count)[:, None] * (jnp.exp(logp) - target))
        grad_head = grad_head + column_dot(current_low, logits_low)
        grad_bias = grad_bias + jnp.sum(logits_low.astype(jnp.float32), 0)
        grad_low = lowered(row_dot(logits_low, head_low))
        for layer in reversed(range(layers)):
            grad_inputs, grad_weight, grad_pair = layer_backward(
                adj,
                conv_full[layer],
                norm_params[layer, 0],
                kept_list[layer],
                grad_low.astype(jnp.float32),
                total_rows,
            )
            grad_conv[layer] = grad_conv[layer] + grad_weight
            grad_norm[layer] = grad_norm[layer] + grad_pair
            grad_low = lowered(grad_inputs)
        grad_input = grad_input + column_dot(inputs, grad_low)
    grad_conv_all = jnp.stack(grad_conv)
    grad_norm_all = jnp.stack(grad_norm)
    grad_input, grad_conv_all, grad_head, grad_bias, grad_norm_all, loss_sum = lax.psum(
        (grad_input, grad_conv_all, grad_head, grad_bias, grad_norm_all, loss_sum), "node"
    )
    grad_input, grad_conv_all = (
        lax.psum_scatter(grad_input, "grp", scatter_dimension=1, tiled=True),
        lax.psum_scatter(grad_conv_all, "grp", scatter_dimension=2, tiled=True),
    )
    grad_head, grad_bias, grad_norm_all, loss_sum = lax.psum(
        (grad_head, grad_bias, grad_norm_all, loss_sum), "grp"
    )
    moment_in = muon_beta * input_moment + grad_input
    moment_conv = muon_beta * conv_moment + grad_conv_all
    ortho_in, ortho_first, ortho_second = orthogonal_blocks(
        moment_in, moment_conv[0], moment_conv[1]
    )
    factor_in = 0.2 * float(max(f_width, hidden)) ** 0.5
    factor_conv = 0.2 * float(2 * hidden) ** 0.5
    input_new = input_weight - muon_rate * (factor_in * ortho_in + decay_rate * input_weight)
    ortho_conv = jnp.stack([ortho_first, ortho_second])
    conv_new = conv_weight - muon_rate * (factor_conv * ortho_conv + decay_rate * conv_weight)
    head_new, head_first_new, head_second_new = adamw(
        head_weight, grad_head, head_first, head_second
    )
    bias_new, bias_first_new, bias_second_new = adamw(head_bias, grad_bias, bias_first, bias_second)
    norm_new, norm_first_new, norm_second_new = adamw(
        norm_params, grad_norm_all, norm_first, norm_second
    )
    loss_parts = jnp.stack([loss_sum, count])
    return (
        loss_parts,
        input_new,
        moment_in,
        conv_new,
        moment_conv,
        head_new,
        head_first_new,
        head_second_new,
        bias_new,
        bias_first_new,
        bias_second_new,
        norm_new,
        norm_first_new,
        norm_second_new,
    )

MESH = pl.DeviceIdType.MESH
NT = (((1,), (1,)), ((), ()))
NN = (((1,), (0,)), ((), ()))
VMEM_BYTES = 56 * 1024 * 1024
ROUNDS = 8
EARLY_STEPS = 0


def flip(index, bit):
    return index + bit - 2 * bit * lax.rem(lax.div(index, bit), 2)


def dot(left, right, dims=NN):
    return lax.dot_general(left, right, dims, preferred_element_type=jnp.float32)


def split(value):
    high = lowered(value)
    return high, lowered(value - high.astype(jnp.float32))


def dot_three(left, right, dims=NN):
    left_high, left_rest = left
    right_high, right_rest = right
    axis = dims[0][1][0]
    return dot(
        jnp.concatenate([left_high, left_high, left_rest], 1),
        jnp.concatenate([right_high, right_rest, right_high], axis),
        dims,
    )


def step_kernel(
    groups,
    classes,
    feat,
    adj,
    labels,
    train,
    w_in,
    m_in,
    w_conv,
    m_conv,
    w_head,
    f_head,
    s_head,
    w_bias,
    f_bias,
    s_bias,
    w_norm,
    f_norm,
    s_norm,
    o_loss,
    o_in,
    o_in_m,
    o_conv,
    o_conv_m,
    o_head,
    o_head_f,
    o_head_s,
    o_bias,
    o_bias_f,
    o_bias_s,
    o_norm,
    o_norm_f,
    o_norm_s,
    av,
    xg,
    hg,
    dg,
    pad,
    padh,
    wa,
    wb,
    wn,
    wt_head,
    h0,
    agg,
    act,
    slope,
    ms,
    axh,
    accx,
    acc,
    h2,
    dh,
    dp,
    gt,
    q1,
    q2,
    tall_in,
    ght,
    st,
    zs,
    sums,
    mpc,
    mit,
    mi,
    gbc,
    gbi,
    gbh,
    rsc,
    rsi,
    rsh,
    zc,
    zi,
    zh,
    mf,
    mfi,
    hf,
    y_conv,
    y_in,
    loc,
    ga_s,
    ga_r,
    st_s,
    st_r,
    z_s,
    z_r,
    zf_s,
    zf_r,
    rs_s,
    rs_r,
    ag_s,
    ag_r,
):
    f32 = jnp.float32
    bf16 = jnp.bfloat16
    width, graphs, rows = feat.shape
    total = adj.shape[2]
    hidden = w_head.shape[1]
    wide = 2 * hidden
    shard = hidden // groups
    part = shard // 4
    half = rows // 2
    span_in = 16 * ((width + 15) // 16)
    chunk = min(rows, 128)
    chunks = rows // chunk
    g = lax.axis_index("grp")
    me = lax.axis_index("node")
    core = lax.rem(me, 2)
    chip = lax.div(me, 2)
    n_sib, n_x, n_y, n_d = flip(me, 1), flip(me, 2), flip(me, 4), flip(flip(me, 2), 4)
    peers = [n_d, flip(n_d, 1), n_x, n_y, flip(n_x, 1), flip(n_y, 1), n_sib]
    z_peers = [lax.rem(g + d, groups) for d in range(1, groups)]
    z_from = [lax.rem(g + groups - d, groups) for d in range(1, groups)]
    started = []

    def send(src, dst, s_sem, r_sem, group, node):
        copy = pltpu.make_async_remote_copy(
            src_ref=src,
            dst_ref=dst,
            send_sem=s_sem,
            recv_sem=r_sem,
            device_id=(group, node),
            device_id_type=MESH,
        )
        copy.start()
        started.append(copy)
        return copy

    def lanes_of_core(span):
        return pl.ds(pl.multiple_of(core * span, span), span)

    barrier = pltpu.get_barrier_semaphore()
    for node in peers:
        pl.semaphore_signal(barrier, inc=1, device_id=(g, node), device_id_type=MESH)
    for group in z_peers:
        pl.semaphore_signal(barrier, inc=1, device_id=(group, me), device_id_type=MESH)

    own_a = [pltpu.make_async_copy(adj.at[s], av.at[s], loc.at[s]) for s in range(graphs)]
    part_rows = pl.ds(pl.multiple_of(chip * part, part), part)
    core_lanes = lanes_of_core(hidden)
    own_m = [
        pltpu.make_async_copy(m_conv.at[l, part_rows, core_lanes], mpc.at[l, g], loc.at[graphs + l])
        for l in range(2)
    ]
    for copy in own_a + own_m:
        copy.start()

    high_rows = pl.ds(pl.multiple_of(g * shard, shard), shard)
    padh[...] = jnp.zeros_like(padh)
    for s in range(graphs):
        padh[pl.ds(0, width), :] = feat[:, s, :].astype(f32)
        xg[s, me] = lowered(padh[pl.ds(0, span_in), :])
    mit[...] = jnp.zeros_like(mit)
    mit[high_rows, pl.ds(0, width)] = w_in[...]
    wa[high_rows, pl.ds(0, wide)] = lowered(w_conv[0])
    wa[high_rows, pl.ds(wide, 128)] = lowered(mit[high_rows, :])
    wb[high_rows, :] = lowered(w_conv[1])
    pl.semaphore_wait(barrier, 7 + groups - 1)

    def gather_of(index, ref, by_lane=False):
        low, high = pl.ds(0, half), pl.ds(half, half)

        def go(j, node, block, span=None):
            view = ref.at[block]
            if span is not None:
                view = ref.at[block, :, span] if by_lane else ref.at[block, span]
            return send(view, view, ga_s.at[index, j], ga_r.at[index, j], g, node)

        kept = {}

        def own_first():
            kept[0] = go(0, n_x, me, low)
            kept[1] = go(1, n_y, me, high)
            kept[6] = go(6, n_sib, me)

        def own_second():
            kept[2] = go(2, n_x, me, high)
            kept[3] = go(3, n_y, me, low)

        def own():
            own_first()
            own_second()

        def relay():
            kept[0].wait_recv()
            kept[4] = go(4, n_y, n_x, low)
            kept[1].wait_recv()
            kept[5] = go(5, n_x, n_y, high)

        def near():
            kept[2].wait_recv()
            kept[7] = go(7, n_sib, n_x)
            kept[3].wait_recv()
            kept[8] = go(8, n_sib, n_y)

        def far():
            kept[4].wait_recv()
            kept[5].wait_recv()
            kept[9] = go(9, n_sib, n_d)

        def near_ready():
            for j in (6, 7, 8):
                kept[j].wait_recv()

        def far_ready():
            kept[9].wait_recv()

        return own, relay, near, far, near_ready, far_ready, own_first, own_second

    def chip_at(i):
        cx = lax.rem(lax.rem(chip, 2) + lax.rem(i, 2), 2)
        cy = lax.rem(lax.div(chip, 2) + lax.div(i, 2), 2)
        return cx + 2 * cy

    def product(s, ref, out, first, last):
        if first == 0:
            out[...] = jnp.zeros_like(out)

        def body(i, carry):
            c = chip_at(i)
            block = ref[pl.ds(2 * c, 2)].reshape(2 * rows, ref.shape[2])
            left = av[s, :, pl.ds(pl.multiple_of(c * 2 * rows, 2 * rows), 2 * rows)]
            out[...] += dot(left, block)
            return carry

        lax.fori_loop(first, last, body, 0)

    def product_x(s, first, last):
        if first == 0:
            accx[...] = jnp.zeros_like(accx)

        def body(i, carry):
            block = 2 * chip_at(lax.div(i, 2)) + lax.rem(i, 2)
            left = av[s, :, pl.ds(pl.multiple_of(block * rows, rows), rows)]
            accx[...] += dot(left, xg[s, block], NT)
            return carry

        lax.fori_loop(2 * first, 2 * last, body, 0)

    def over_rows(body, carry):
        def one(i, value):
            return body(pl.ds(pl.multiple_of(i * chunk, chunk), chunk), value)

        return lax.fori_loop(0, chunks, one, carry)

    def fold(value):
        return jnp.sum(value.reshape(chunk // 8, 8, hidden), 0)

    st_copies = {}

    def plane_send(k):
        view = st.at[k, me]
        st_copies[k] = [
            send(view, view, st_s.at[k, i], st_r.at[k, i], g, node) for i, node in enumerate(peers)
        ]

    def plane_sum(k):
        for copy in st_copies[k]:
            copy.wait_recv()
        value = st[k, 0]
        for i in range(1, 8):
            value = value + st[k, i]
        return value

    z_copies = {}

    def z_send(k, view):
        z_copies[k] = [
            send(view, view, z_s.at[k, i], z_r.at[k, i], group, me)
            for i, group in enumerate(z_peers)
        ]

    def z_wait(k):
        for copy in z_copies[k]:
            copy.wait_recv()

    x_g = [gather_of(s, xg.at[s], True) for s in range(2)]
    h_g = [gather_of(2 + s, hg.at[s]) for s in range(2)]
    d_g = [gather_of(4 + s, dg.at[s]) for s in range(2)]

    own_rows = pl.ds(pl.multiple_of(g * shard, shard), shard)
    strip = shard // 2

    def strip_of(group):
        return pl.ds(pl.multiple_of(group * shard + core * strip, strip), strip)

    forwards = {}

    def z_forward(k, ref):
        forwards[k] = []
        for i, group in enumerate(z_from):
            z_copies[k][i].wait_recv()
            view = ref.at[strip_of(group)]
            forwards[k].append(send(view, view, zf_s.at[k, i], zf_r.at[k, i], g, n_sib))

    def z_forwarded(k):
        for copy in forwards[k]:
            copy.wait_recv()

    x_g[0][0]()
    z_send(0, wa.at[strip_of(g)])
    mit[high_rows, pl.ds(0, width)] = m_in[...]
    x_g[0][1]()
    x_g[1][0]()
    z_send(1, wb.at[strip_of(g)])
    padh[...] = jnp.zeros_like(padh)
    padh[pl.ds(0, classes), pl.ds(0, hidden)] = w_head[...]
    wt_head[...] = lowered(padh[:, :hidden])
    pad[...] = jnp.zeros_like(pad)
    pad[pl.ds(0, 8), pl.ds(0, classes)] = jnp.broadcast_to(w_bias[...], (8, classes))
    bias_col = pad[...].T[:64, :1]
    count_own = jnp.sum(train[...].astype(f32), axis=1, keepdims=True)
    count_own = count_own[0:1] + count_own[1:2]
    x_g[0][2]()
    for copy in own_m:
        copy.wait()
    for copy in own_a:
        copy.wait()

    def forward_act(s, l, k, first, second, w_first, w_second):
        acc[...] = dot(first, w_first) + dot(second, w_second)

        def body(span, carry):
            pre = acc[span, :]
            square = pre * pre
            inner = 0.7978845608028654 * pre * (1.0 + 0.044715 * square)
            t = jnp.tanh(inner)
            value = 0.5 * pre * (1.0 + t)
            act[l, s, span, :] = value
            slope[l, s, span, :] = 0.5 * (1.0 + t) + 0.5 * pre * (1.0 - t * t) * (
                0.7978845608028654 * (1.0 + 3.0 * 0.044715 * square)
            )
            return carry[0] + fold(value), carry[1] + fold(value * value)

        zero = jnp.zeros((8, hidden), f32)
        one, two = over_rows(body, (zero, zero))
        st[k, me] = jnp.zeros((8, hidden), f32)
        st[k, me, 0:1, :] = jnp.sum(one, 0, keepdims=True)
        st[k, me, 1:2, :] = jnp.sum(two, 0, keepdims=True)
        if k == 0:
            st[k, me, 2:3, :] = jnp.broadcast_to(count_own, (1, hidden))
        plane_send(k)

    def normalise(s, l, k, out):
        sums_all = plane_sum(k)
        mean = sums_all[0:1] / total
        var = sums_all[1:2] / total - mean * mean
        inv = lax.rsqrt(var + norm_eps)
        ms[l, s, 0:1, :] = inv
        gain, shift = w_norm[l, 0:1, :], w_norm[l, 1:2, :]

        def body(span, carry):
            normed = (act[l, s, span, :] - mean) * inv
            act[l, s, span, :] = normed
            out[span, :] = lowered(normed * gain + shift)
            return carry

        over_rows(body, 0)
        return sums_all

    def layer_zero(s):
        high, rest = split(accx[...])
        axh[s] = high
        w = wa[:, wide : wide + span_in]
        agg[0, s] = lowered(dot(high, w, NT) + dot(rest, w, NT))
        h0[s] = lowered(dot(xg[s, me].T, w, NT))
        forward_act(s, 0, s, h0[s], agg[0, s], wn[0, :hidden, :], wn[0, hidden:, :])

    def layer_one(s):
        agg[1, s] = lowered(acc[...])
        forward_act(s, 1, 2 + s, hg[s, me], agg[1, s], wn[1, :hidden, :], wn[1, hidden:, :])

    def head(s, count):
        value = h2[s]
        logits = dot(wt_head[pl.ds(0, 64), :], value, NT) + bias_col
        at = lax.broadcasted_iota(jnp.int32, (64, rows), 0)
        valid = at < classes
        logits = jnp.where(valid, logits, -1e30)
        shifted = logits - jnp.max(logits, 0, keepdims=True)
        logp = shifted - jnp.log(jnp.sum(jnp.exp(shifted), 0, keepdims=True))
        onehot = jnp.where(at == labels[s : s + 1, :], 1.0, 0.0)
        target = jnp.where(valid, (1.0 - smoothing) * onehot + smoothing / classes, 0.0)
        weights = train[s : s + 1, :].astype(f32)
        node_loss = jnp.sum(target * logp, 0, keepdims=True)
        loss = -jnp.sum(weights * node_loss, axis=1, keepdims=True)
        delta = (weights / count) * (jnp.exp(logp) - target)
        delta_low = lowered(delta)
        value_t = dot(delta_low, value)
        ght[...] = value_t if s == 0 else ght[...] + value_t
        column = dot(jnp.ones((8, rows), bf16), delta_low, NT)
        tall = jnp.concatenate([delta_low.astype(f32), jnp.zeros((64, rows), f32)], 0).T
        dh[s] = lowered(dot(lowered(tall), wt_head[...])).astype(f32)
        return loss, column

    def backward_sums(s, l, k, extra=None):
        def body(span, carry):
            grad = dh[s, span, :]
            return carry[0] + fold(grad), carry[1] + fold(grad * act[l, s, span, :])

        zero = jnp.zeros((8, hidden), f32)
        one, two = over_rows(body, (zero, zero))
        st[k, me] = jnp.zeros((8, hidden), f32)
        st[k, me, 0:1, :] = jnp.sum(one, 0, keepdims=True)
        st[k, me, 1:2, :] = jnp.sum(two, 0, keepdims=True)
        if extra is not None:
            st[k, me, 2:3, 0:64] = extra[1][0:1]
            st[k, me, 3:4, :] = jnp.broadcast_to(extra[0], (1, hidden))
        plane_send(k)

    def backward_pre(s, l, k):
        sums_all = plane_sum(k)
        sums[1 - l] = sums_all if s == 0 else sums[1 - l] + sums_all
        gain = w_norm[l, 0:1, :]
        inv = ms[l, s, 0:1, :]
        first = gain * sums_all[0:1] / total
        second = gain * sums_all[1:2] / total

        def body(span, carry):
            grad = dh[s, span, :] * gain - first - act[l, s, span, :] * second
            dp[l, s, span, :] = lowered(grad * inv * slope[l, s, span, :])
            return carry

        over_rows(body, 0)

    def conv_grads(s, l, left, right):
        turned = dp[l, s].T
        one, two = dot(turned, left), dot(turned, right)
        if s == 0:
            gt[l, :, :hidden] = one
            gt[l, :, hidden:] = two
        else:
            gt[l, :, :hidden] += one
            gt[l, :, hidden:] += two
        return turned

    rs_copies = {}

    def pieces_send(k, src, dst, where):
        rs_copies[k] = []
        for i, node in enumerate(peers):
            rs_copies[k].append(
                send(where(src, node), dst.at[me], rs_s.at[k, i], rs_r.at[k, i], g, node)
            )

    def pieces_sum(k, src, dst, own):
        dst[me] = own
        for copy in rs_copies[k]:
            copy.wait_recv()
        value = dst[0].astype(f32)
        for i in range(1, 8):
            value = value + dst[i].astype(f32)
        return value

    def conv_piece(ref, node):
        n_core, n_chip = lax.rem(node, 2), lax.div(node, 2)
        return ref.at[:, n_chip, :, pl.ds(pl.multiple_of(n_core * hidden, hidden), hidden)]

    def in_piece(ref, node):
        return ref.at[node]

    def head_piece(ref, node):
        n_core, n_chip = lax.rem(node, 2), lax.div(node, 2)
        return ref.at[n_chip, :, pl.ds(pl.multiple_of(n_core * (hidden // 2), hidden // 2), hidden // 2)]

    def over_z(k, buf):
        z_wait(k)
        value = buf[0].astype(f32)
        for i in range(1, groups):
            value = value + buf[i].astype(f32)
        return value

    ag_copies = {}

    def spread(k, view_of):
        view = view_of(me)
        ag_copies[k] = [
            send(view, view, ag_s.at[k, i], ag_r.at[k, i], g, node)
            for i, node in enumerate((n_d, n_x, n_y, n_sib))
        ]

    def spread_forward(k, view_of):
        for i, node in ((1, n_x), (2, n_y), (0, n_d)):
            ag_copies[k][i].wait_recv()
            view = view_of(node)
            ag_copies[k].append(
                send(view, view, ag_s.at[k, 4 + i], ag_r.at[k, 4 + i], g, n_sib)
            )

    def spread_wait(k):
        for copy in ag_copies[k][3:]:
            copy.wait_recv()

    head_lanes = lanes_of_core(hidden // 2)

    x_g[0][4]()
    product_x(0, 0, 3)
    x_g[1][1]()
    x_g[0][3]()
    z_forward(0, wa)
    x_g[0][5]()
    product_x(0, 3, 4)
    z_forwarded(0)
    wn[0] = wa[:, :wide].T
    layer_zero(0)
    x_g[1][2]()
    x_g[1][4]()
    product_x(1, 0, 3)
    x_g[1][3]()
    x_g[1][5]()
    product_x(1, 3, 4)
    count_plane = normalise(0, 0, 0, hg.at[0, me])
    h_g[0][6]()
    layer_zero(1)
    h_g[0][7]()
    zs[0, g] = count_plane
    z_send(3, zs.at[0, g])
    z_forward(1, wb)
    normalise(1, 0, 1, hg.at[1, me])
    h_g[0][1]()
    h_g[1][0]()
    z_send(6, mpc.at[0, g])
    z_send(7, mpc.at[1, g])
    z_send(8, mit.at[own_rows])
    z_forwarded(1)
    wn[1] = wb[...].T
    h_g[0][2]()
    h_g[0][4]()
    product(0, hg.at[0], acc, 0, 3)
    h_g[0][3]()
    h_g[0][5]()
    product(0, hg.at[0], acc, 3, 4)
    layer_one(0)
    h_g[1][1]()
    z_wait(3)
    count = zs[0, 0]
    for i in range(1, groups):
        count = count + zs[0, i]
    count = count[2:3, 0:1]
    h_g[1][2]()
    normalise(0, 1, 2, h2.at[0])
    loss_row = head(0, count)
    backward_sums(0, 1, 4, loss_row)
    h_g[1][3]()
    h_g[1][4]()
    product(1, hg.at[1], acc, 0, 3)
    h_g[1][5]()
    product(1, hg.at[1], acc, 3, 4)
    layer_one(1)
    backward_pre(0, 1, 4)
    dg[0, me] = lowered(dot(dp[1, 0], wb[:, hidden:]))
    d_g[0][0]()
    dh[0] = dot(dp[1, 0], wb[:, :hidden])
    normalise(1, 1, 3, h2.at[1])
    loss_row = head(1, count)
    backward_sums(1, 1, 5, loss_row)
    d_g[0][1]()
    conv_grads(0, 1, hg[0, me], agg[1, 0])
    backward_pre(1, 1, 5)
    dg[1, me] = lowered(dot(dp[1, 1], wb[:, hidden:]))
    d_g[1][0]()
    d_g[0][2]()
    dh[1] = dot(dp[1, 1], wb[:, :hidden])
    zs[1, g] = sums[0]
    z_send(4, zs.at[1, g])
    d_g[0][4]()
    product(0, dg.at[0], acc, 0, 3)
    d_g[0][3]()
    d_g[0][5]()
    product(0, dg.at[0], acc, 3, 4)
    dh[0] = lowered(dh[0] + acc[...]).astype(f32)
    backward_sums(0, 0, 6)
    d_g[1][1]()
    conv_grads(1, 1, hg[1, me], agg[1, 1])
    gbc[1] = lowered(gt[1]).reshape(groups, 4, part, wide)
    gbh[...] = lowered(ght[...]).reshape(4, 16, hidden)
    pieces_send(0, gbc.at[1], rsc.at[1], conv_piece)
    pieces_send(1, gbh, rsh, head_piece)
    d_g[1][2]()
    backward_pre(0, 0, 6)
    turned = conv_grads(0, 0, h0[0], agg[0, 0])
    q1[...] = dot(turned, xg[0, me], NT)
    q2[...] = dot(turned, axh[0])
    d_g[1][4]()
    product(1, dg.at[1], acc, 0, 3)
    d_g[1][3]()
    d_g[1][5]()
    product(1, dg.at[1], acc, 3, 4)
    dh[1] = lowered(dh[1] + acc[...]).astype(f32)
    backward_sums(1, 0, 7)
    zc[1, g] = lowered(pieces_sum(0, None, rsc.at[1], conv_piece(gbc.at[1], me)[...]))
    z_send(9, zc.at[1, g])
    zh[g] = lowered(pieces_sum(1, None, rsh, head_piece(gbh, me)[...]))
    z_send(10, zh.at[g])
    z_wait(6)
    z_wait(7)
    z_wait(8)
    tall_in[...] = mit[...]
    mi[...] = tall_in[...].T.reshape(8, 16, hidden)
    tall_in[...] = jnp.zeros_like(tall_in)
    backward_pre(1, 0, 7)
    turned = conv_grads(1, 0, h0[1], agg[0, 1])
    gbc[0] = lowered(gt[0]).reshape(groups, 4, part, wide)
    pieces_send(2, gbc.at[0], rsc.at[0], conv_piece)
    q1[...] += dot(turned, xg[1, me], NT)
    q2[...] += dot(turned, axh[1])
    one, two = split(q1[...]), split(q2[...])
    w_self, w_near = wn[0, :hidden, :], wn[0, hidden:, :]
    g_in = dot(w_self, one[0]) + dot(w_self, one[1]) + dot(w_near, two[0]) + dot(w_near, two[1])
    tall_in[:, pl.ds(0, span_in)] = g_in
    gbi[...] = lowered(tall_in[...].T).reshape(8, 16, hidden)
    pieces_send(3, gbi, rsi, in_piece)
    zs[2, g] = sums[1]
    z_send(5, zs.at[2, g])

    def conv_view(l):
        return lambda node: conv_piece(mf.at[l], node)

    def head_view(node):
        return head_piece(hf, node)

    def in_view(node):
        return mfi.at[node]

    def scaled(value):
        norm = jnp.sqrt(jnp.sum(jnp.sum(value * value, 0, keepdims=True), 1, keepdims=True))
        return value / (norm + 1e-07)

    def iterate(refs, first, last):
        for i in range(first, last):
            for ref in refs:
                value = ref[...]
                pair = split(value)
                gram = dot_three(pair, pair, NT)
                gram_high, gram_rest = split(gram)
                cross = dot(gram_high, gram_rest)
                square = dot(gram_high, gram_high) + cross + cross.T
                poly = split(poly_second * gram + poly_third * square)
                ref[...] = poly_first * value + dot_three(poly, pair)

    factor_conv = 0.2 * float(wide) ** 0.5
    factor_in = 0.2 * float(max(width, hidden)) ** 0.5

    def conv_out(l):
        o_conv_m[l] = mf[l, g].reshape(shard, wide)
        ortho = y_conv[l, own_rows, :]
        weight = w_conv[l]
        o_conv[l] = weight - muon_rate * (factor_conv * ortho + decay_rate * weight)

    mf[1, :, chip, :, core_lanes] = muon_beta * mpc[1] + over_z(9, zc.at[1])
    spread(0, conv_view(1))
    hf[chip, :, head_lanes] = over_z(10, zh)
    spread(1, head_view)
    zc[0, g] = lowered(pieces_sum(2, None, rsc.at[0], conv_piece(gbc.at[0], me)[...]))
    z_send(11, zc.at[0, g])
    zi[g] = lowered(pieces_sum(3, None, rsi, gbi[me]))
    z_send(12, zi.at[g])
    spread_forward(0, conv_view(1))
    spread_forward(1, head_view)
    spread_wait(0)
    y_conv[1] = scaled(mf[1].reshape(hidden, wide))
    iterate([y_conv.at[1]], 0, EARLY_STEPS)
    mf[0, :, chip, :, core_lanes] = muon_beta * mpc[0] + over_z(11, zc.at[0])
    spread(2, conv_view(0))
    mfi[me] = muon_beta * mi[me] + over_z(12, zi)
    spread(3, in_view)
    iterate([y_conv.at[1]], EARLY_STEPS, NS_STEPS)
    spread_forward(2, conv_view(0))
    spread_forward(3, in_view)
    conv_out(1)

    spread_wait(1)
    grad = hf[...].reshape(64, hidden)[:classes]
    o_head[...], o_head_f[...], o_head_s[...] = adamw(w_head[...], grad, f_head[...], s_head[...])
    z_wait(4)
    z_wait(5)
    late = zs[1, 0]
    early = zs[2, 0]
    for i in range(1, groups):
        late = late + zs[1, i]
        early = early + zs[2, i]
    for l, rows_l in ((0, early), (1, late)):
        grad = jnp.concatenate([rows_l[1:2], rows_l[0:1]], 0)
        o_norm[l], o_norm_f[l], o_norm_s[l] = adamw(w_norm[l], grad, f_norm[l], s_norm[l])
    o_bias[...], o_bias_f[...], o_bias_s[...] = adamw(
        w_bias[...], late[2:3, :classes], f_bias[...], s_bias[...]
    )
    o_loss[...] = jnp.concatenate([late[3:4, 0:1], count], 1)

    spread_wait(2)
    spread_wait(3)
    y_conv[0] = scaled(mf[0].reshape(hidden, wide))
    y_in[...] = scaled(mfi[...].reshape(128, hidden))
    iterate([y_conv.at[0], y_in], 0, NS_STEPS)
    conv_out(0)
    tall_in[...] = mfi[...].reshape(128, hidden).T
    o_in_m[...] = tall_in[own_rows, :][:, :width]
    tall_in[...] = y_in[...].T
    ortho = tall_in[own_rows, :][:, :width]
    weight = w_in[...]
    o_in[...] = weight - muon_rate * (factor_in * ortho + decay_rate * weight)
    for copy in started:
        copy.wait_send()


def planned(mesh):
    groups = mesh.shape["grp"]

    def call(
        features,
        adjacency,
        labels,
        train_mask,
        input_weight,
        input_moment,
        conv_weight,
        conv_moment,
        head_weight,
        head_first,
        head_second,
        head_bias,
        bias_first,
        bias_second,
        norm_params,
        norm_first,
        norm_second,
    ):
        f32, bf16 = jnp.float32, jnp.bfloat16
        graphs, rows, width = features.shape
        total = adjacency.shape[2]
        hidden, classes = head_weight.shape
        wide = 2 * hidden
        shard = hidden // groups
        part = shard // 4
        span_in = 16 * ((width + 15) // 16)
        vm = pltpu.VMEM
        sem = pltpu.SemaphoreType.DMA
        shape = jax.ShapeDtypeStruct
        near = pl.BlockSpec(memory_space=pltpu.VMEM)
        anywhere = pl.BlockSpec(memory_space=pl.ANY)
        results = [
            shape((1, 2), f32),
            shape((shard, width), f32),
            shape((shard, width), f32),
            shape((2, shard, wide), f32),
            shape((2, shard, wide), f32),
            shape((classes, hidden), f32),
            shape((classes, hidden), f32),
            shape((classes, hidden), f32),
            shape((1, classes), f32),
            shape((1, classes), f32),
            shape((1, classes), f32),
            shape(norm_params.shape, f32),
            shape(norm_params.shape, f32),
            shape(norm_params.shape, f32),
        ]
        outs = pl.pallas_call(
            functools.partial(step_kernel, groups, classes),
            out_shape=results,
            in_specs=[near, anywhere, near, near, near, near, near, anywhere] + [near] * 9,
            out_specs=[near] * 14,
            scratch_shapes=[
                vm((graphs, rows, total), bf16),
                vm((graphs, 8, span_in, rows), bf16),
                vm((graphs, 8, rows, hidden), bf16),
                vm((graphs, 8, rows, hidden), bf16),
                vm((128, 128), f32),
                vm((128, rows), f32),
                vm((hidden, wide + 128), bf16),
                vm((hidden, wide), bf16),
                vm((2, wide, hidden), bf16),
                vm((128, hidden), bf16),
                vm((graphs, rows, hidden), bf16),
                vm((2, graphs, rows, hidden), bf16),
                vm((2, graphs, rows, hidden), f32),
                vm((2, graphs, rows, hidden), f32),
                vm((2, graphs, 8, hidden), f32),
                vm((graphs, rows, span_in), bf16),
                vm((rows, span_in), f32),
                vm((rows, hidden), f32),
                vm((graphs, rows, hidden), bf16),
                vm((graphs, rows, hidden), f32),
                vm((2, graphs, rows, hidden), bf16),
                vm((2, hidden, wide), f32),
                vm((hidden, span_in), f32),
                vm((hidden, span_in), f32),
                vm((hidden, 128), f32),
                vm((64, hidden), f32),
                vm((ROUNDS, 8, 8, hidden), f32),
                vm((3, groups, 8, hidden), f32),
                vm((2, 8, hidden), f32),
                vm((2, groups, part, hidden), f32),
                vm((hidden, 128), f32),
                vm((8, 16, hidden), f32),
                vm((2, groups, 4, part, wide), bf16),
                vm((8, 16, hidden), bf16),
                vm((4, 16, hidden), bf16),
                vm((2, 8, groups, part, hidden), bf16),
                vm((8, 16, hidden), bf16),
                vm((8, 16, hidden // 2), bf16),
                vm((2, groups, groups, part, hidden), bf16),
                vm((groups, 16, hidden), bf16),
                vm((groups, 16, hidden // 2), bf16),
                vm((2, groups, 4, part, wide), f32),
                vm((8, 16, hidden), f32),
                vm((4, 16, hidden), f32),
                vm((2, hidden, wide), f32),
                vm((128, hidden), f32),
                sem((graphs + 2,)),
                sem((6, 10)),
                sem((6, 10)),
                sem((ROUNDS, 7)),
                sem((ROUNDS, 7)),
                sem((13, groups - 1)),
                sem((13, groups - 1)),
                sem((2, groups - 1)),
                sem((2, groups - 1)),
                sem((4, 7)),
                sem((4, 7)),
                sem((4, 7)),
                sem((4, 7)),
            ],
            compiler_params=pltpu.CompilerParams(
                collective_id=0, has_side_effects=True, vmem_limit_bytes=VMEM_BYTES
            ),
            name="train_step",
        )(
            jnp.transpose(features, (2, 0, 1)),
            adjacency,
            labels,
            train_mask,
            input_weight.T,
            input_moment.T,
            jnp.swapaxes(conv_weight, 1, 2),
            jnp.swapaxes(conv_moment, 1, 2),
            head_weight.T,
            head_first.T,
            head_second.T,
            head_bias[None, :],
            bias_first[None, :],
            bias_second[None, :],
            norm_params,
            norm_first,
            norm_second,
        )
        outs = pl.pallas_call(
            hand_over,
            out_shape=results,
            in_specs=[near] * 14,
            out_specs=[near] * 14,
            name="hand_over",
        )(*outs)
        loss, in_new, in_m, conv_new, conv_m, h_new, h_f, h_s, b_new, b_f, b_s, *norms = outs
        return (
            loss[0],
            in_new.T,
            in_m.T,
            jnp.swapaxes(conv_new, 1, 2),
            jnp.swapaxes(conv_m, 1, 2),
            h_new.T,
            h_f.T,
            h_s.T,
            b_new[0],
            b_f[0],
            b_s[0],
            *norms,
        )

    return call


def hand_over(*refs):
    for source, target in zip(refs[:14], refs[14:]):
        target[...] = source[...]


def solution(mesh):
    placed = (
        P("grp", "node", None),
        P("grp", "node", None),
        P("grp", "node"),
        P("grp", "node"),
        P(None, "grp"),
        P(None, "grp"),
        P(None, None, "grp"),
        P(None, None, "grp"),
        P(),
        P(),
        P(),
        P(),
        P(),
        P(),
        P(),
        P(),
        P(),
    )
    small = mesh.shape["node"] == 8 and mesh.shape["grp"] == 4
    return jax.shard_map(
        planned(mesh) if small else per_device,
        mesh=mesh,
        in_specs=placed,
        out_specs=(
            P(),
            P(None, "grp"),
            P(None, "grp"),
            P(None, None, "grp"),
            P(None, None, "grp"),
            P(),
            P(),
            P(),
            P(),
            P(),
            P(),
            P(),
            P(),
            P(),
        ),
        check_vma=False,
    )
```

```python
import functools

import jax
import jax.numpy as jnp
from jax import lax
from jax.experimental import pallas as pl
from jax.experimental.pallas import tpu as pltpu
from jax.sharding import PartitionSpec as P

NS_STEPS = 5
STEP = 10


norm_eps = 1e-05
smoothing = 0.1
poly_first = 3.4445
poly_second = -4.775
poly_third = 2.0315
muon_beta = 0.95
muon_rate = 0.2
decay_rate = 0.01
adam_rate = 0.05
beta_first = 0.9
beta_second = 0.95
adam_eps = 1e-08


def lowered(value):
    return value.astype(jnp.bfloat16)


def matmul_hi(left, right):
    return jnp.dot(left, right, precision=lax.Precision.HIGHEST)


def column_dot(left, right):
    return lax.dot_general(
        left, right, (((0,), (0,)), ((), ())), preferred_element_type=jnp.float32
    )


def row_dot(left, right):
    return lax.dot_general(
        left, right, (((1,), (1,)), ((), ())), preferred_element_type=jnp.float32
    )


def neighbour_sum(adj, values):
    return jnp.dot(
        adj, lax.all_gather(values, "node", axis=0, tiled=True), preferred_element_type=jnp.float32
    )


def neighbour_back(adj, grads):
    return lax.psum_scatter(column_dot(adj, grads), "node", scatter_dimension=0, tiled=True)


def layer_forward(adj, inputs_low, weight_low, gain, shift, total_rows):
    hidden = weight_low.shape[1]
    agg_low = lowered(neighbour_sum(adj, inputs_low))
    pre = jnp.dot(inputs_low, weight_low[:hidden], preferred_element_type=jnp.float32)
    pre = pre + jnp.dot(agg_low, weight_low[hidden:], preferred_element_type=jnp.float32)
    act = jax.nn.gelu(pre)
    sums, squares = lax.psum((jnp.sum(act, 0), jnp.sum(act * act, 0)), "node")
    mean = sums / total_rows
    var = squares / total_rows - mean * mean
    inv_std = lax.rsqrt(var + norm_eps)
    normed = (act - mean) * inv_std
    return (normed * gain + shift, (inputs_low, agg_low, pre, normed, inv_std))


def layer_backward(adj, weight_low, gain, kept, grad_out, total_rows):
    inputs_low, agg_low, pre, normed, inv_std = kept
    hidden = weight_low.shape[1]
    grad_gain = jnp.sum(grad_out * normed, 0)
    grad_shift = jnp.sum(grad_out, 0)
    grad_normed = grad_out * gain
    first, second = lax.psum((jnp.sum(grad_normed, 0), jnp.sum(grad_normed * normed, 0)), "node")
    grad_act = (grad_normed - first / total_rows - normed * (second / total_rows)) * inv_std
    grad_pre = jax.vjp(jax.nn.gelu, pre)[1](grad_act)[0]
    pre_low = lowered(grad_pre)
    grad_weight = jnp.concatenate(
        [column_dot(inputs_low, pre_low), column_dot(agg_low, pre_low)], 0
    )
    grad_agg = lowered(row_dot(pre_low, weight_low[hidden:]))
    grad_inputs = row_dot(pre_low, weight_low[:hidden]) + neighbour_back(adj, grad_agg)
    return (grad_inputs, grad_weight, jnp.stack([grad_gain, grad_shift]))


def gram_of(block):
    return matmul_hi(block, block.T)


def orthogonal_blocks(first_block, second_block, third_block):
    blocks = [first_block, second_block, third_block]
    for step in range(NS_STEPS):
        grams = lax.psum((gram_of(blocks[0]), gram_of(blocks[1]), gram_of(blocks[2])), "grp")
        grams = list(grams)
        if step == 0:
            scales = [jnp.sqrt(jnp.trace(gram)) + 1e-07 for gram in grams]
            blocks = [block / scale for block, scale in zip(blocks, scales)]
            grams = [gram / (scale * scale) for gram, scale in zip(grams, scales)]
        polys = [poly_second * gram + poly_third * matmul_hi(gram, gram) for gram in grams]
        blocks = [poly_first * block + matmul_hi(poly, block) for block, poly in zip(blocks, polys)]
    return blocks


def adamw(weight, grad, first, second):
    first_new = beta_first * first + (1.0 - beta_first) * grad
    second_new = beta_second * second + (1.0 - beta_second) * grad * grad
    fixed_first = first_new / (1.0 - beta_first**STEP)
    fixed_second = second_new / (1.0 - beta_second**STEP)
    update = fixed_first / (jnp.sqrt(fixed_second) + adam_eps) + decay_rate * weight
    return (weight - adam_rate * update, first_new, second_new)


def per_device(
    features,
    adjacency,
    labels,
    train_mask,
    input_weight,
    input_moment,
    conv_weight,
    conv_moment,
    head_weight,
    head_first,
    head_second,
    head_bias,
    bias_first,
    bias_second,
    norm_params,
    norm_first,
    norm_second,
):
    layers = conv_weight.shape[0]
    hidden = head_weight.shape[0]
    classes = head_weight.shape[1]
    f_width = input_weight.shape[0]
    total_rows = features.shape[1] * lax.axis_size("node")
    input_full, conv_full = (
        lax.all_gather(lowered(input_weight), "grp", axis=1, tiled=True),
        lax.all_gather(lowered(conv_weight), "grp", axis=2, tiled=True),
    )
    head_low = lowered(head_weight)
    count = lax.psum(jnp.sum(train_mask).astype(jnp.float32), ("grp", "node"))
    grad_input = jnp.zeros((f_width, hidden), jnp.float32)
    grad_conv = [jnp.zeros((2 * hidden, hidden), jnp.float32) for layer in range(layers)]
    grad_norm = [jnp.zeros((2, hidden), jnp.float32) for layer in range(layers)]
    grad_head = jnp.zeros((hidden, classes), jnp.float32)
    grad_bias = jnp.zeros((classes,), jnp.float32)
    loss_sum = jnp.float32(0.0)
    for graph in range(features.shape[0]):
        inputs = features[graph]
        adj = adjacency[graph]
        current_low = lowered(jnp.dot(inputs, input_full, preferred_element_type=jnp.float32))
        kept_list = []
        for layer in range(layers):
            output, kept = layer_forward(
                adj,
                current_low,
                conv_full[layer],
                norm_params[layer, 0],
                norm_params[layer, 1],
                total_rows,
            )
            kept_list.append(kept)
            current_low = lowered(output)
        logits = jnp.dot(current_low, head_low, preferred_element_type=jnp.float32) + head_bias
        logp = jax.nn.log_softmax(logits, -1)
        onehot = (labels[graph][:, None] == jnp.arange(classes, dtype=jnp.int32)[None, :]).astype(
            jnp.float32
        )
        target = (1.0 - smoothing) * onehot + smoothing / classes
        weights = train_mask[graph].astype(jnp.float32)
        loss_sum = loss_sum - jnp.sum(weights * jnp.sum(target * logp, -1))
        logits_low = lowered((weights / count)[:, None] * (jnp.exp(logp) - target))
        grad_head = grad_head + column_dot(current_low, logits_low)
        grad_bias = grad_bias + jnp.sum(logits_low.astype(jnp.float32), 0)
        grad_low = lowered(row_dot(logits_low, head_low))
        for layer in reversed(range(layers)):
            grad_inputs, grad_weight, grad_pair = layer_backward(
                adj,
                conv_full[layer],
                norm_params[layer, 0],
                kept_list[layer],
                grad_low.astype(jnp.float32),
                total_rows,
            )
            grad_conv[layer] = grad_conv[layer] + grad_weight
            grad_norm[layer] = grad_norm[layer] + grad_pair
            grad_low = lowered(grad_inputs)
        grad_input = grad_input + column_dot(inputs, grad_low)
    grad_conv_all = jnp.stack(grad_conv)
    grad_norm_all = jnp.stack(grad_norm)
    grad_input, grad_conv_all, grad_head, grad_bias, grad_norm_all, loss_sum = lax.psum(
        (grad_input, grad_conv_all, grad_head, grad_bias, grad_norm_all, loss_sum), "node"
    )
    grad_input, grad_conv_all = (
        lax.psum_scatter(grad_input, "grp", scatter_dimension=1, tiled=True),
        lax.psum_scatter(grad_conv_all, "grp", scatter_dimension=2, tiled=True),
    )
    grad_head, grad_bias, grad_norm_all, loss_sum = lax.psum(
        (grad_head, grad_bias, grad_norm_all, loss_sum), "grp"
    )
    moment_in = muon_beta * input_moment + grad_input
    moment_conv = muon_beta * conv_moment + grad_conv_all
    ortho_in, ortho_first, ortho_second = orthogonal_blocks(
        moment_in, moment_conv[0], moment_conv[1]
    )
    factor_in = 0.2 * float(max(f_width, hidden)) ** 0.5
    factor_conv = 0.2 * float(2 * hidden) ** 0.5
    input_new = input_weight - muon_rate * (factor_in * ortho_in + decay_rate * input_weight)
    ortho_conv = jnp.stack([ortho_first, ortho_second])
    conv_new = conv_weight - muon_rate * (factor_conv * ortho_conv + decay_rate * conv_weight)
    head_new, head_first_new, head_second_new = adamw(
        head_weight, grad_head, head_first, head_second
    )
    bias_new, bias_first_new, bias_second_new = adamw(head_bias, grad_bias, bias_first, bias_second)
    norm_new, norm_first_new, norm_second_new = adamw(
        norm_params, grad_norm_all, norm_first, norm_second
    )
    loss_parts = jnp.stack([loss_sum, count])
    return (
        loss_parts,
        input_new,
        moment_in,
        conv_new,
        moment_conv,
        head_new,
        head_first_new,
        head_second_new,
        bias_new,
        bias_first_new,
        bias_second_new,
        norm_new,
        norm_first_new,
        norm_second_new,
    )

MESH = pl.DeviceIdType.MESH
NT = (((1,), (1,)), ((), ()))
NN = (((1,), (0,)), ((), ()))
VMEM_BYTES = 56 * 1024 * 1024
ROUNDS = 8
EARLY_STEPS = 0


def flip(index, bit):
    return index + bit - 2 * bit * lax.rem(lax.div(index, bit), 2)


def dot(left, right, dims=NN):
    return lax.dot_general(left, right, dims, preferred_element_type=jnp.float32)


def split(value):
    high = lowered(value)
    return high, lowered(value - high.astype(jnp.float32))


def dot_three(left, right, dims=NN):
    left_high, left_rest = left
    right_high, right_rest = right
    axis = dims[0][1][0]
    return dot(
        jnp.concatenate([left_high, left_high, left_rest], 1),
        jnp.concatenate([right_high, right_rest, right_high], axis),
        dims,
    )


def step_kernel(
    groups,
    classes,
    feat,
    adj,
    labels,
    train,
    w_in,
    m_in,
    w_conv,
    m_conv,
    w_head,
    f_head,
    s_head,
    w_bias,
    f_bias,
    s_bias,
    w_norm,
    f_norm,
    s_norm,
    o_loss,
    o_in,
    o_in_m,
    o_conv,
    o_conv_m,
    o_head,
    o_head_f,
    o_head_s,
    o_bias,
    o_bias_f,
    o_bias_s,
    o_norm,
    o_norm_f,
    o_norm_s,
    av,
    xg,
    hg,
    dg,
    pad,
    padh,
    wa,
    wb,
    wn,
    wt_head,
    h0,
    agg,
    act,
    slope,
    ms,
    axh,
    accx,
    acc,
    h2,
    dh,
    dp,
    gt,
    q1,
    q2,
    tall_in,
    ght,
    st,
    zs,
    sums,
    mpc,
    mit,
    mi,
    gbc,
    gbi,
    gbh,
    rsc,
    rsi,
    rsh,
    zc,
    zi,
    zh,
    mf,
    mfi,
    hf,
    y_conv,
    y_in,
    loc,
    ga_s,
    ga_r,
    st_s,
    st_r,
    z_s,
    z_r,
    zf_s,
    zf_r,
    rs_s,
    rs_r,
    ag_s,
    ag_r,
):
    f32 = jnp.float32
    bf16 = jnp.bfloat16
    width, graphs, rows = feat.shape
    total = adj.shape[2]
    hidden = w_head.shape[1]
    wide = 2 * hidden
    shard = hidden // groups
    part = shard // 4
    half = rows // 2
    span_in = 16 * ((width + 15) // 16)
    chunk = min(rows, 128)
    chunks = rows // chunk
    g = lax.axis_index("grp")
    me = lax.axis_index("node")
    core = lax.rem(me, 2)
    chip = lax.div(me, 2)
    n_sib, n_x, n_y, n_d = flip(me, 1), flip(me, 2), flip(me, 4), flip(flip(me, 2), 4)
    peers = [n_d, flip(n_d, 1), n_x, n_y, flip(n_x, 1), flip(n_y, 1), n_sib]
    z_peers = [lax.rem(g + d, groups) for d in range(1, groups)]
    z_from = [lax.rem(g + groups - d, groups) for d in range(1, groups)]
    sent = []

    def send(src, dst, s_sem, r_sem, group, node):
        pltpu.make_async_remote_copy(
            src_ref=src,
            dst_ref=dst,
            send_sem=s_sem,
            recv_sem=r_sem,
            device_id=(group, node),
            device_id_type=MESH,
        ).start()

    def drain(sem, view):
        pltpu.make_async_copy(view, view, sem).wait()

    def lanes_of_core(span):
        return pl.ds(pl.multiple_of(core * span, span), span)

    barrier = pltpu.get_barrier_semaphore()
    for node in peers:
        pl.semaphore_signal(barrier, inc=1, device_id=(g, node), device_id_type=MESH)
    for group in z_peers:
        pl.semaphore_signal(barrier, inc=1, device_id=(group, me), device_id_type=MESH)

    own_a = [pltpu.make_async_copy(adj.at[s], av.at[s], loc.at[s]) for s in range(graphs)]
    part_rows = pl.ds(pl.multiple_of(chip * part, part), part)
    core_lanes = lanes_of_core(hidden)
    own_m = [
        pltpu.make_async_copy(m_conv.at[l, part_rows, core_lanes], mpc.at[l, g], loc.at[graphs + l])
        for l in range(2)
    ]
    for copy in own_a + own_m:
        copy.start()

    high_rows = pl.ds(pl.multiple_of(g * shard, shard), shard)
    padh[...] = jnp.zeros_like(padh)
    for s in range(graphs):
        padh[pl.ds(0, width), :] = feat[:, s, :].astype(f32)
        xg[s, me] = lowered(padh[pl.ds(0, span_in), :])
    mit[...] = jnp.zeros_like(mit)
    mit[high_rows, pl.ds(0, width)] = w_in[...]
    wa[high_rows, pl.ds(0, wide)] = lowered(w_conv[0])
    wa[high_rows, pl.ds(wide, 128)] = lowered(mit[high_rows, :])
    wb[high_rows, :] = lowered(w_conv[1])
    pl.semaphore_wait(barrier, 7 + groups - 1)

    def gather_of(index, ref, by_lane=False):
        low, high = pl.ds(0, half), pl.ds(half, half)

        def go(r, node, block, span=None):
            view = ref.at[block]
            if span is not None:
                view = ref.at[block, :, span] if by_lane else ref.at[block, span]
            send(view, view, ga_s.at[index], ga_r.at[5 * index + r], g, node)

        def arrived(r, blocks):
            drain(ga_r.at[5 * index + r], ref.at[pl.ds(0, blocks)])

        sent.append((ga_s.at[index], ref.at[pl.ds(0, 7)]))

        def own_first():
            go(0, n_x, me, low)
            go(0, n_y, me, high)
            go(3, n_sib, me)

        def own_second():
            go(1, n_x, me, high)
            go(1, n_y, me, low)

        def own():
            own_first()
            own_second()

        def relay():
            arrived(0, 1)
            go(2, n_y, n_x, low)
            go(2, n_x, n_y, high)

        def near():
            arrived(1, 1)
            go(3, n_sib, n_x)
            go(3, n_sib, n_y)

        def far():
            arrived(2, 1)
            go(4, n_sib, n_d)

        def near_ready():
            arrived(3, 3)

        def far_ready():
            arrived(4, 1)

        return own, relay, near, far, near_ready, far_ready, own_first, own_second

    def chip_at(i):
        cx = lax.rem(lax.rem(chip, 2) + lax.rem(i, 2), 2)
        cy = lax.rem(lax.div(chip, 2) + lax.div(i, 2), 2)
        return cx + 2 * cy

    def product(s, ref, out, first, last):
        if first == 0:
            out[...] = jnp.zeros_like(out)

        def body(i, carry):
            c = chip_at(i)
            block = ref[pl.ds(2 * c, 2)].reshape(2 * rows, ref.shape[2])
            left = av[s, :, pl.ds(pl.multiple_of(c * 2 * rows, 2 * rows), 2 * rows)]
            out[...] += dot(left, block)
            return carry

        lax.fori_loop(first, last, body, 0)

    def product_x(s, first, last):
        if first == 0:
            accx[...] = jnp.zeros_like(accx)

        def body(i, carry):
            block = 2 * chip_at(lax.div(i, 2)) + lax.rem(i, 2)
            left = av[s, :, pl.ds(pl.multiple_of(block * rows, rows), rows)]
            accx[...] += dot(left, xg[s, block], NT)
            return carry

        lax.fori_loop(2 * first, 2 * last, body, 0)

    def over_rows(body, carry):
        def one(i, value):
            return body(pl.ds(pl.multiple_of(i * chunk, chunk), chunk), value)

        return lax.fori_loop(0, chunks, one, carry)

    def fold(value):
        return jnp.sum(value.reshape(chunk // 8, 8, hidden), 0)

    def plane_send(k):
        view = st.at[k, me]
        for node in peers:
            send(view, view, st_s.at[k], st_r.at[k], g, node)
        sent.append((st_s.at[k], st.at[k, pl.ds(0, 7)]))

    def plane_sum(k):
        drain(st_r.at[k], st.at[k, pl.ds(0, 7)])
        value = st[k, 0]
        for i in range(1, 8):
            value = value + st[k, i]
        return value

    z_all = {}

    def z_send(k, view, all_views):
        for group in z_peers:
            send(view, view, z_s.at[k], z_r.at[k], group, me)
        z_all[k] = all_views
        sent.append((z_s.at[k], all_views))

    def z_wait(k):
        drain(z_r.at[k], z_all[k])

    others = pl.ds(0, groups - 1)

    x_g = [gather_of(s, xg.at[s], True) for s in range(2)]
    h_g = [gather_of(2 + s, hg.at[s]) for s in range(2)]
    d_g = [gather_of(4 + s, dg.at[s]) for s in range(2)]

    own_rows = pl.ds(pl.multiple_of(g * shard, shard), shard)
    strip = shard // 2

    def strip_of(group):
        return pl.ds(pl.multiple_of(group * shard + core * strip, strip), strip)

    strips = pl.ds(0, strip * (groups - 1))

    def z_forward(k, ref):
        z_wait(k)
        for group in z_from:
            view = ref.at[strip_of(group)]
            send(view, view, zf_s.at[k], zf_r.at[k], g, n_sib)
        sent.append((zf_s.at[k], ref.at[strips]))

    def z_forwarded(k):
        drain(zf_r.at[k], z_all[k])

    x_g[0][0]()
    z_send(0, wa.at[strip_of(g)], wa.at[strips])
    mit[high_rows, pl.ds(0, width)] = m_in[...]
    x_g[0][1]()
    x_g[1][0]()
    z_send(1, wb.at[strip_of(g)], wb.at[strips])
    padh[...] = jnp.zeros_like(padh)
    padh[pl.ds(0, classes), pl.ds(0, hidden)] = w_head[...]
    wt_head[...] = lowered(padh[:, :hidden])
    pad[...] = jnp.zeros_like(pad)
    pad[pl.ds(0, 8), pl.ds(0, classes)] = jnp.broadcast_to(w_bias[...], (8, classes))
    bias_col = pad[...].T[:64, :1]
    count_own = jnp.sum(train[...].astype(f32), axis=1, keepdims=True)
    count_own = count_own[0:1] + count_own[1:2]
    x_g[0][2]()
    for copy in own_m:
        copy.wait()
    for copy in own_a:
        copy.wait()

    def forward_act(s, l, k, first, second, w_first, w_second):
        acc[...] = dot(first, w_first) + dot(second, w_second)

        def body(span, carry):
            pre = acc[span, :]
            square = pre * pre
            inner = 0.7978845608028654 * pre * (1.0 + 0.044715 * square)
            t = jnp.tanh(inner)
            value = 0.5 * pre * (1.0 + t)
            act[l, s, span, :] = value
            slope[l, s, span, :] = 0.5 * (1.0 + t) + 0.5 * pre * (1.0 - t * t) * (
                0.7978845608028654 * (1.0 + 3.0 * 0.044715 * square)
            )
            return carry[0] + fold(value), carry[1] + fold(value * value)

        zero = jnp.zeros((8, hidden), f32)
        one, two = over_rows(body, (zero, zero))
        st[k, me] = jnp.zeros((8, hidden), f32)
        st[k, me, 0:1, :] = jnp.sum(one, 0, keepdims=True)
        st[k, me, 1:2, :] = jnp.sum(two, 0, keepdims=True)
        if k == 0:
            st[k, me, 2:3, :] = jnp.broadcast_to(count_own, (1, hidden))
        plane_send(k)

    def normalise(s, l, k, out):
        sums_all = plane_sum(k)
        mean = sums_all[0:1] / total
        var = sums_all[1:2] / total - mean * mean
        inv = lax.rsqrt(var + norm_eps)
        ms[l, s, 0:1, :] = inv
        gain, shift = w_norm[l, 0:1, :], w_norm[l, 1:2, :]

        def body(span, carry):
            normed = (act[l, s, span, :] - mean) * inv
            act[l, s, span, :] = normed
            out[span, :] = lowered(normed * gain + shift)
            return carry

        over_rows(body, 0)
        return sums_all

    def layer_zero(s):
        high, rest = split(accx[...])
        axh[s] = high
        w = wa[:, wide : wide + span_in]
        agg[0, s] = lowered(dot(high, w, NT) + dot(rest, w, NT))
        h0[s] = lowered(dot(xg[s, me].T, w, NT))
        forward_act(s, 0, s, h0[s], agg[0, s], wn[0, :hidden, :], wn[0, hidden:, :])

    def layer_one(s):
        agg[1, s] = lowered(acc[...])
        forward_act(s, 1, 2 + s, hg[s, me], agg[1, s], wn[1, :hidden, :], wn[1, hidden:, :])

    def head(s, count):
        value = h2[s]
        logits = dot(wt_head[pl.ds(0, 64), :], value, NT) + bias_col
        at = lax.broadcasted_iota(jnp.int32, (64, rows), 0)
        valid = at < classes
        logits = jnp.where(valid, logits, -1e30)
        shifted = logits - jnp.max(logits, 0, keepdims=True)
        logp = shifted - jnp.log(jnp.sum(jnp.exp(shifted), 0, keepdims=True))
        onehot = jnp.where(at == labels[s : s + 1, :], 1.0, 0.0)
        target = jnp.where(valid, (1.0 - smoothing) * onehot + smoothing / classes, 0.0)
        weights = train[s : s + 1, :].astype(f32)
        node_loss = jnp.sum(target * logp, 0, keepdims=True)
        loss = -jnp.sum(weights * node_loss, axis=1, keepdims=True)
        delta = (weights / count) * (jnp.exp(logp) - target)
        delta_low = lowered(delta)
        value_t = dot(delta_low, value)
        ght[...] = value_t if s == 0 else ght[...] + value_t
        column = dot(jnp.ones((8, rows), bf16), delta_low, NT)
        tall = jnp.concatenate([delta_low.astype(f32), jnp.zeros((64, rows), f32)], 0).T
        dh[s] = lowered(dot(lowered(tall), wt_head[...])).astype(f32)
        return loss, column

    def backward_sums(s, l, k, extra=None):
        def body(span, carry):
            grad = dh[s, span, :]
            return carry[0] + fold(grad), carry[1] + fold(grad * act[l, s, span, :])

        zero = jnp.zeros((8, hidden), f32)
        one, two = over_rows(body, (zero, zero))
        st[k, me] = jnp.zeros((8, hidden), f32)
        st[k, me, 0:1, :] = jnp.sum(one, 0, keepdims=True)
        st[k, me, 1:2, :] = jnp.sum(two, 0, keepdims=True)
        if extra is not None:
            st[k, me, 2:3, 0:64] = extra[1][0:1]
            st[k, me, 3:4, :] = jnp.broadcast_to(extra[0], (1, hidden))
        plane_send(k)

    def backward_pre(s, l, k):
        sums_all = plane_sum(k)
        sums[1 - l] = sums_all if s == 0 else sums[1 - l] + sums_all
        gain = w_norm[l, 0:1, :]
        inv = ms[l, s, 0:1, :]
        first = gain * sums_all[0:1] / total
        second = gain * sums_all[1:2] / total

        def body(span, carry):
            grad = dh[s, span, :] * gain - first - act[l, s, span, :] * second
            dp[l, s, span, :] = lowered(grad * inv * slope[l, s, span, :])
            return carry

        over_rows(body, 0)

    def conv_grads(s, l, left, right):
        turned = dp[l, s].T
        one, two = dot(turned, left), dot(turned, right)
        if s == 0:
            gt[l, :, :hidden] = one
            gt[l, :, hidden:] = two
        else:
            gt[l, :, :hidden] += one
            gt[l, :, hidden:] += two
        return turned

    def pieces_send(k, src, dst, where):
        for node in peers:
            send(where(src, node), dst.at[me], rs_s.at[k], rs_r.at[k], g, node)
        sent.append((rs_s.at[k], dst.at[pl.ds(0, 7)]))

    def pieces_sum(k, src, dst, own):
        dst[me] = own
        drain(rs_r.at[k], dst.at[pl.ds(0, 7)])
        value = dst[0].astype(f32)
        for i in range(1, 8):
            value = value + dst[i].astype(f32)
        return value

    def conv_piece(ref, node):
        n_core, n_chip = lax.rem(node, 2), lax.div(node, 2)
        return ref.at[:, n_chip, :, pl.ds(pl.multiple_of(n_core * hidden, hidden), hidden)]

    def in_piece(ref, node):
        return ref.at[node]

    def head_piece(ref, node):
        n_core, n_chip = lax.rem(node, 2), lax.div(node, 2)
        return ref.at[n_chip, :, pl.ds(pl.multiple_of(n_core * (hidden // 2), hidden // 2), hidden // 2)]

    def over_z(k, buf):
        z_wait(k)
        value = buf[0].astype(f32)
        for i in range(1, groups):
            value = value + buf[i].astype(f32)
        return value

    def spread(k, view_of, some):
        view = view_of(me)
        for node in (n_d, n_x, n_y):
            send(view, view, ag_s.at[k], ag_r.at[2 * k], g, node)
        send(view, view, ag_s.at[k], ag_r.at[2 * k + 1], g, n_sib)
        sent.append((ag_s.at[k], some(4)))

    def spread_forward(k, view_of, some):
        drain(ag_r.at[2 * k], some(3))
        for node in (n_x, n_y, n_d):
            view = view_of(node)
            send(view, view, ag_s.at[4 + k], ag_r.at[2 * k + 1], g, n_sib)
        sent.append((ag_s.at[4 + k], some(3)))

    def spread_wait(k, some):
        drain(ag_r.at[2 * k + 1], some(4))

    head_lanes = lanes_of_core(hidden // 2)

    x_g[0][4]()
    product_x(0, 0, 3)
    x_g[0][3]()
    z_forward(0, wa)
    x_g[0][5]()
    product_x(0, 3, 4)
    x_g[1][1]()
    z_forwarded(0)
    wn[0] = wa[:, :wide].T
    layer_zero(0)
    x_g[1][2]()
    x_g[1][4]()
    product_x(1, 0, 3)
    x_g[1][3]()
    x_g[1][5]()
    product_x(1, 3, 4)
    count_plane = normalise(0, 0, 0, hg.at[0, me])
    h_g[0][6]()
    layer_zero(1)
    h_g[0][7]()
    zs[0, g] = count_plane
    z_send(3, zs.at[0, g], zs.at[0, others])
    z_forward(1, wb)
    normalise(1, 0, 1, hg.at[1, me])
    h_g[0][1]()
    h_g[1][0]()
    z_send(6, mpc.at[0, g], mpc.at[0, others])
    z_send(7, mpc.at[1, g], mpc.at[1, others])
    z_send(8, mit.at[own_rows], mit.at[pl.ds(0, shard * (groups - 1))])
    z_forwarded(1)
    wn[1] = wb[...].T
    h_g[0][2]()
    h_g[0][4]()
    product(0, hg.at[0], acc, 0, 3)
    h_g[0][3]()
    h_g[0][5]()
    product(0, hg.at[0], acc, 3, 4)
    layer_one(0)
    h_g[1][1]()
    z_wait(3)
    count = zs[0, 0]
    for i in range(1, groups):
        count = count + zs[0, i]
    count = count[2:3, 0:1]
    h_g[1][2]()
    normalise(0, 1, 2, h2.at[0])
    loss_row = head(0, count)
    backward_sums(0, 1, 4, loss_row)
    h_g[1][3]()
    h_g[1][4]()
    product(1, hg.at[1], acc, 0, 3)
    h_g[1][5]()
    product(1, hg.at[1], acc, 3, 4)
    layer_one(1)
    backward_pre(0, 1, 4)
    dg[0, me] = lowered(dot(dp[1, 0], wb[:, hidden:]))
    d_g[0][0]()
    dh[0] = dot(dp[1, 0], wb[:, :hidden])
    normalise(1, 1, 3, h2.at[1])
    loss_row = head(1, count)
    backward_sums(1, 1, 5, loss_row)
    d_g[0][1]()
    conv_grads(0, 1, hg[0, me], agg[1, 0])
    backward_pre(1, 1, 5)
    dg[1, me] = lowered(dot(dp[1, 1], wb[:, hidden:]))
    d_g[1][0]()
    d_g[0][2]()
    dh[1] = dot(dp[1, 1], wb[:, :hidden])
    zs[1, g] = sums[0]
    z_send(4, zs.at[1, g], zs.at[1, others])
    d_g[0][4]()
    product(0, dg.at[0], acc, 0, 3)
    d_g[0][3]()
    d_g[0][5]()
    product(0, dg.at[0], acc, 3, 4)
    dh[0] = lowered(dh[0] + acc[...]).astype(f32)
    backward_sums(0, 0, 6)
    d_g[1][1]()
    conv_grads(1, 1, hg[1, me], agg[1, 1])
    gbc[1] = lowered(gt[1]).reshape(groups, 4, part, wide)
    gbh[...] = lowered(ght[...]).reshape(4, 16, hidden)
    pieces_send(0, gbc.at[1], rsc.at[1], conv_piece)
    pieces_send(1, gbh, rsh, head_piece)
    d_g[1][2]()
    backward_pre(0, 0, 6)
    turned = conv_grads(0, 0, h0[0], agg[0, 0])
    q1[...] = dot(turned, xg[0, me], NT)
    q2[...] = dot(turned, axh[0])
    d_g[1][4]()
    product(1, dg.at[1], acc, 0, 3)
    d_g[1][3]()
    d_g[1][5]()
    product(1, dg.at[1], acc, 3, 4)
    dh[1] = lowered(dh[1] + acc[...]).astype(f32)
    backward_sums(1, 0, 7)
    zc[1, g] = lowered(pieces_sum(0, None, rsc.at[1], conv_piece(gbc.at[1], me)[...]))
    z_send(9, zc.at[1, g], zc.at[1, others])
    zh[g] = lowered(pieces_sum(1, None, rsh, head_piece(gbh, me)[...]))
    z_send(10, zh.at[g], zh.at[others])
    z_wait(6)
    z_wait(7)
    z_wait(8)
    tall_in[...] = mit[...]
    mi[...] = tall_in[...].T.reshape(8, 16, hidden)
    tall_in[...] = jnp.zeros_like(tall_in)
    backward_pre(1, 0, 7)
    turned = conv_grads(1, 0, h0[1], agg[0, 1])
    gbc[0] = lowered(gt[0]).reshape(groups, 4, part, wide)
    pieces_send(2, gbc.at[0], rsc.at[0], conv_piece)
    q1[...] += dot(turned, xg[1, me], NT)
    q2[...] += dot(turned, axh[1])
    one, two = split(q1[...]), split(q2[...])
    w_self, w_near = wn[0, :hidden, :], wn[0, hidden:, :]
    g_in = dot(w_self, one[0]) + dot(w_self, one[1]) + dot(w_near, two[0]) + dot(w_near, two[1])
    tall_in[:, pl.ds(0, span_in)] = g_in
    gbi[...] = lowered(tall_in[...].T).reshape(8, 16, hidden)
    pieces_send(3, gbi, rsi, in_piece)
    zs[2, g] = sums[1]
    z_send(5, zs.at[2, g], zs.at[2, others])

    def conv_view(l):
        return lambda node: conv_piece(mf.at[l], node)

    def conv_some(l):
        return lambda n: mf.at[l, :, pl.ds(0, n), :, pl.ds(0, hidden)]

    def head_some(n):
        return hf.at[pl.ds(0, n), :, pl.ds(0, hidden // 2)]

    def in_some(n):
        return mfi.at[pl.ds(0, n)]

    def head_view(node):
        return head_piece(hf, node)

    def in_view(node):
        return mfi.at[node]

    def scaled(value):
        norm = jnp.sqrt(jnp.sum(jnp.sum(value * value, 0, keepdims=True), 1, keepdims=True))
        return value / (norm + 1e-07)

    def iterate(refs, first, last):
        for i in range(first, last):
            for ref in refs:
                value = ref[...]
                pair = split(value)
                gram = dot_three(pair, pair, NT)
                gram_high, gram_rest = split(gram)
                cross = dot(gram_high, gram_rest)
                square = dot(gram_high, gram_high) + cross + cross.T
                poly = split(poly_second * gram + poly_third * square)
                ref[...] = poly_first * value + dot_three(poly, pair)

    factor_conv = 0.2 * float(wide) ** 0.5
    factor_in = 0.2 * float(max(width, hidden)) ** 0.5

    def conv_out(l):
        o_conv_m[l] = mf[l, g].reshape(shard, wide)
        ortho = y_conv[l, own_rows, :]
        weight = w_conv[l]
        o_conv[l] = weight - muon_rate * (factor_conv * ortho + decay_rate * weight)

    mf[1, :, chip, :, core_lanes] = muon_beta * mpc[1] + over_z(9, zc.at[1])
    spread(0, conv_view(1), conv_some(1))
    hf[chip, :, head_lanes] = over_z(10, zh)
    spread(1, head_view, head_some)
    zc[0, g] = lowered(pieces_sum(2, None, rsc.at[0], conv_piece(gbc.at[0], me)[...]))
    z_send(11, zc.at[0, g], zc.at[0, others])
    zi[g] = lowered(pieces_sum(3, None, rsi, gbi[me]))
    z_send(12, zi.at[g], zi.at[others])
    spread_forward(0, conv_view(1), conv_some(1))
    spread_forward(1, head_view, head_some)
    spread_wait(0, conv_some(1))
    y_conv[1] = scaled(mf[1].reshape(hidden, wide))
    iterate([y_conv.at[1]], 0, EARLY_STEPS)
    mf[0, :, chip, :, core_lanes] = muon_beta * mpc[0] + over_z(11, zc.at[0])
    spread(2, conv_view(0), conv_some(0))
    mfi[me] = muon_beta * mi[me] + over_z(12, zi)
    spread(3, in_view, in_some)
    iterate([y_conv.at[1]], EARLY_STEPS, NS_STEPS)
    spread_forward(2, conv_view(0), conv_some(0))
    spread_forward(3, in_view, in_some)
    conv_out(1)

    spread_wait(1, head_some)
    grad = hf[...].reshape(64, hidden)[:classes]
    o_head[...], o_head_f[...], o_head_s[...] = adamw(w_head[...], grad, f_head[...], s_head[...])
    z_wait(4)
    z_wait(5)
    late = zs[1, 0]
    early = zs[2, 0]
    for i in range(1, groups):
        late = late + zs[1, i]
        early = early + zs[2, i]
    for l, rows_l in ((0, early), (1, late)):
        grad = jnp.concatenate([rows_l[1:2], rows_l[0:1]], 0)
        o_norm[l], o_norm_f[l], o_norm_s[l] = adamw(w_norm[l], grad, f_norm[l], s_norm[l])
    o_bias[...], o_bias_f[...], o_bias_s[...] = adamw(
        w_bias[...], late[2:3, :classes], f_bias[...], s_bias[...]
    )
    o_loss[...] = jnp.concatenate([late[3:4, 0:1], count], 1)

    spread_wait(2, conv_some(0))
    spread_wait(3, in_some)
    y_conv[0] = scaled(mf[0].reshape(hidden, wide))
    y_in[...] = scaled(mfi[...].reshape(128, hidden))
    iterate([y_conv.at[0], y_in], 0, NS_STEPS)
    conv_out(0)
    tall_in[...] = mfi[...].reshape(128, hidden).T
    o_in_m[...] = tall_in[own_rows, :][:, :width]
    tall_in[...] = y_in[...].T
    ortho = tall_in[own_rows, :][:, :width]
    weight = w_in[...]
    o_in[...] = weight - muon_rate * (factor_in * ortho + decay_rate * weight)
    for sem, view in sent:
        drain(sem, view)


def planned(mesh):
    groups = mesh.shape["grp"]

    def call(
        features,
        adjacency,
        labels,
        train_mask,
        input_weight,
        input_moment,
        conv_weight,
        conv_moment,
        head_weight,
        head_first,
        head_second,
        head_bias,
        bias_first,
        bias_second,
        norm_params,
        norm_first,
        norm_second,
    ):
        f32, bf16 = jnp.float32, jnp.bfloat16
        graphs, rows, width = features.shape
        total = adjacency.shape[2]
        hidden, classes = head_weight.shape
        wide = 2 * hidden
        shard = hidden // groups
        part = shard // 4
        span_in = 16 * ((width + 15) // 16)
        vm = pltpu.VMEM
        sem = pltpu.SemaphoreType.DMA
        shape = jax.ShapeDtypeStruct
        near = pl.BlockSpec(memory_space=pltpu.VMEM)
        anywhere = pl.BlockSpec(memory_space=pl.ANY)
        results = [
            shape((1, 2), f32),
            shape((shard, width), f32),
            shape((shard, width), f32),
            shape((2, shard, wide), f32),
            shape((2, shard, wide), f32),
            shape((classes, hidden), f32),
            shape((classes, hidden), f32),
            shape((classes, hidden), f32),
            shape((1, classes), f32),
            shape((1, classes), f32),
            shape((1, classes), f32),
            shape(norm_params.shape, f32),
            shape(norm_params.shape, f32),
            shape(norm_params.shape, f32),
        ]
        outs = pl.pallas_call(
            functools.partial(step_kernel, groups, classes),
            out_shape=results,
            in_specs=[near, anywhere, near, near, near, near, near, anywhere] + [near] * 9,
            out_specs=[near] * 14,
            scratch_shapes=[
                vm((graphs, rows, total), bf16),
                vm((graphs, 8, span_in, rows), bf16),
                vm((graphs, 8, rows, hidden), bf16),
                vm((graphs, 8, rows, hidden), bf16),
                vm((128, 128), f32),
                vm((128, rows), f32),
                vm((hidden, wide + 128), bf16),
                vm((hidden, wide), bf16),
                vm((2, wide, hidden), bf16),
                vm((128, hidden), bf16),
                vm((graphs, rows, hidden), bf16),
                vm((2, graphs, rows, hidden), bf16),
                vm((2, graphs, rows, hidden), f32),
                vm((2, graphs, rows, hidden), f32),
                vm((2, graphs, 8, hidden), f32),
                vm((graphs, rows, span_in), bf16),
                vm((rows, span_in), f32),
                vm((rows, hidden), f32),
                vm((graphs, rows, hidden), bf16),
                vm((graphs, rows, hidden), f32),
                vm((2, graphs, rows, hidden), bf16),
                vm((2, hidden, wide), f32),
                vm((hidden, span_in), f32),
                vm((hidden, span_in), f32),
                vm((hidden, 128), f32),
                vm((64, hidden), f32),
                vm((ROUNDS, 8, 8, hidden), f32),
                vm((3, groups, 8, hidden), f32),
                vm((2, 8, hidden), f32),
                vm((2, groups, part, hidden), f32),
                vm((hidden, 128), f32),
                vm((8, 16, hidden), f32),
                vm((2, groups, 4, part, wide), bf16),
                vm((8, 16, hidden), bf16),
                vm((4, 16, hidden), bf16),
                vm((2, 8, groups, part, hidden), bf16),
                vm((8, 16, hidden), bf16),
                vm((8, 16, hidden // 2), bf16),
                vm((2, groups, groups, part, hidden), bf16),
                vm((groups, 16, hidden), bf16),
                vm((groups, 16, hidden // 2), bf16),
                vm((2, groups, 4, part, wide), f32),
                vm((8, 16, hidden), f32),
                vm((4, 16, hidden), f32),
                vm((2, hidden, wide), f32),
                vm((128, hidden), f32),
                sem((graphs + 2,)),
                sem((6,)),
                sem((30,)),
                sem((ROUNDS,)),
                sem((ROUNDS,)),
                sem((13,)),
                sem((13,)),
                sem((2,)),
                sem((2,)),
                sem((4,)),
                sem((4,)),
                sem((8,)),
                sem((8,)),
            ],
            compiler_params=pltpu.CompilerParams(
                collective_id=0, has_side_effects=True, vmem_limit_bytes=VMEM_BYTES
            ),
            name="train_step",
        )(
            jnp.transpose(features, (2, 0, 1)),
            adjacency,
            labels,
            train_mask,
            input_weight.T,
            input_moment.T,
            jnp.swapaxes(conv_weight, 1, 2),
            jnp.swapaxes(conv_moment, 1, 2),
            head_weight.T,
            head_first.T,
            head_second.T,
            head_bias[None, :],
            bias_first[None, :],
            bias_second[None, :],
            norm_params,
            norm_first,
            norm_second,
        )
        outs = pl.pallas_call(
            hand_over,
            out_shape=results,
            in_specs=[near] * 14,
            out_specs=[near] * 14,
            name="hand_over",
        )(*outs)
        loss, in_new, in_m, conv_new, conv_m, h_new, h_f, h_s, b_new, b_f, b_s, *norms = outs
        return (
            loss[0],
            in_new.T,
            in_m.T,
            jnp.swapaxes(conv_new, 1, 2),
            jnp.swapaxes(conv_m, 1, 2),
            h_new.T,
            h_f.T,
            h_s.T,
            b_new[0],
            b_f[0],
            b_s[0],
            *norms,
        )

    return call


def hand_over(*refs):
    for source, target in zip(refs[:14], refs[14:]):
        target[...] = source[...]


def solution(mesh):
    placed = (
        P("grp", "node", None),
        P("grp", "node", None),
        P("grp", "node"),
        P("grp", "node"),
        P(None, "grp"),
        P(None, "grp"),
        P(None, None, "grp"),
        P(None, None, "grp"),
        P(),
        P(),
        P(),
        P(),
        P(),
        P(),
        P(),
        P(),
        P(),
    )
    small = mesh.shape["node"] == 8 and mesh.shape["grp"] == 4
    return jax.shard_map(
        planned(mesh) if small else per_device,
        mesh=mesh,
        in_specs=placed,
        out_specs=(
            P(),
            P(None, "grp"),
            P(None, "grp"),
            P(None, None, "grp"),
            P(None, None, "grp"),
            P(),
            P(),
            P(),
            P(),
            P(),
            P(),
            P(),
            P(),
            P(),
        ),
        check_vma=False,
    )
```

```python
import functools

import jax
import jax.numpy as jnp
from jax import lax
from jax.experimental import pallas as pl
from jax.experimental.pallas import tpu as pltpu
from jax.sharding import PartitionSpec as P

NS_STEPS = 5
STEP = 10


norm_eps = 1e-05
smoothing = 0.1
poly_first = 3.4445
poly_second = -4.775
poly_third = 2.0315
muon_beta = 0.95
muon_rate = 0.2
decay_rate = 0.01
adam_rate = 0.05
beta_first = 0.9
beta_second = 0.95
adam_eps = 1e-08


def lowered(value):
    return value.astype(jnp.bfloat16)


def matmul_hi(left, right):
    return jnp.dot(left, right, precision=lax.Precision.HIGHEST)


def column_dot(left, right):
    return lax.dot_general(
        left, right, (((0,), (0,)), ((), ())), preferred_element_type=jnp.float32
    )


def row_dot(left, right):
    return lax.dot_general(
        left, right, (((1,), (1,)), ((), ())), preferred_element_type=jnp.float32
    )


def neighbour_sum(adj, values):
    return jnp.dot(
        adj, lax.all_gather(values, "node", axis=0, tiled=True), preferred_element_type=jnp.float32
    )


def neighbour_back(adj, grads):
    return lax.psum_scatter(column_dot(adj, grads), "node", scatter_dimension=0, tiled=True)


def layer_forward(adj, inputs_low, weight_low, gain, shift, total_rows):
    hidden = weight_low.shape[1]
    agg_low = lowered(neighbour_sum(adj, inputs_low))
    pre = jnp.dot(inputs_low, weight_low[:hidden], preferred_element_type=jnp.float32)
    pre = pre + jnp.dot(agg_low, weight_low[hidden:], preferred_element_type=jnp.float32)
    act = jax.nn.gelu(pre)
    sums, squares = lax.psum((jnp.sum(act, 0), jnp.sum(act * act, 0)), "node")
    mean = sums / total_rows
    var = squares / total_rows - mean * mean
    inv_std = lax.rsqrt(var + norm_eps)
    normed = (act - mean) * inv_std
    return (normed * gain + shift, (inputs_low, agg_low, pre, normed, inv_std))


def layer_backward(adj, weight_low, gain, kept, grad_out, total_rows):
    inputs_low, agg_low, pre, normed, inv_std = kept
    hidden = weight_low.shape[1]
    grad_gain = jnp.sum(grad_out * normed, 0)
    grad_shift = jnp.sum(grad_out, 0)
    grad_normed = grad_out * gain
    first, second = lax.psum((jnp.sum(grad_normed, 0), jnp.sum(grad_normed * normed, 0)), "node")
    grad_act = (grad_normed - first / total_rows - normed * (second / total_rows)) * inv_std
    grad_pre = jax.vjp(jax.nn.gelu, pre)[1](grad_act)[0]
    pre_low = lowered(grad_pre)
    grad_weight = jnp.concatenate(
        [column_dot(inputs_low, pre_low), column_dot(agg_low, pre_low)], 0
    )
    grad_agg = lowered(row_dot(pre_low, weight_low[hidden:]))
    grad_inputs = row_dot(pre_low, weight_low[:hidden]) + neighbour_back(adj, grad_agg)
    return (grad_inputs, grad_weight, jnp.stack([grad_gain, grad_shift]))


def gram_of(block):
    return matmul_hi(block, block.T)


def orthogonal_blocks(first_block, second_block, third_block):
    blocks = [first_block, second_block, third_block]
    for step in range(NS_STEPS):
        grams = lax.psum((gram_of(blocks[0]), gram_of(blocks[1]), gram_of(blocks[2])), "grp")
        grams = list(grams)
        if step == 0:
            scales = [jnp.sqrt(jnp.trace(gram)) + 1e-07 for gram in grams]
            blocks = [block / scale for block, scale in zip(blocks, scales)]
            grams = [gram / (scale * scale) for gram, scale in zip(grams, scales)]
        polys = [poly_second * gram + poly_third * matmul_hi(gram, gram) for gram in grams]
        blocks = [poly_first * block + matmul_hi(poly, block) for block, poly in zip(blocks, polys)]
    return blocks


def adamw(weight, grad, first, second):
    first_new = beta_first * first + (1.0 - beta_first) * grad
    second_new = beta_second * second + (1.0 - beta_second) * grad * grad
    fixed_first = first_new / (1.0 - beta_first**STEP)
    fixed_second = second_new / (1.0 - beta_second**STEP)
    update = fixed_first / (jnp.sqrt(fixed_second) + adam_eps) + decay_rate * weight
    return (weight - adam_rate * update, first_new, second_new)


def per_device(
    features,
    adjacency,
    labels,
    train_mask,
    input_weight,
    input_moment,
    conv_weight,
    conv_moment,
    head_weight,
    head_first,
    head_second,
    head_bias,
    bias_first,
    bias_second,
    norm_params,
    norm_first,
    norm_second,
):
    layers = conv_weight.shape[0]
    hidden = head_weight.shape[0]
    classes = head_weight.shape[1]
    f_width = input_weight.shape[0]
    total_rows = features.shape[1] * lax.axis_size("node")
    input_full, conv_full = (
        lax.all_gather(lowered(input_weight), "grp", axis=1, tiled=True),
        lax.all_gather(lowered(conv_weight), "grp", axis=2, tiled=True),
    )
    head_low = lowered(head_weight)
    count = lax.psum(jnp.sum(train_mask).astype(jnp.float32), ("grp", "node"))
    grad_input = jnp.zeros((f_width, hidden), jnp.float32)
    grad_conv = [jnp.zeros((2 * hidden, hidden), jnp.float32) for layer in range(layers)]
    grad_norm = [jnp.zeros((2, hidden), jnp.float32) for layer in range(layers)]
    grad_head = jnp.zeros((hidden, classes), jnp.float32)
    grad_bias = jnp.zeros((classes,), jnp.float32)
    loss_sum = jnp.float32(0.0)
    for graph in range(features.shape[0]):
        inputs = features[graph]
        adj = adjacency[graph]
        current_low = lowered(jnp.dot(inputs, input_full, preferred_element_type=jnp.float32))
        kept_list = []
        for layer in range(layers):
            output, kept = layer_forward(
                adj,
                current_low,
                conv_full[layer],
                norm_params[layer, 0],
                norm_params[layer, 1],
                total_rows,
            )
            kept_list.append(kept)
            current_low = lowered(output)
        logits = jnp.dot(current_low, head_low, preferred_element_type=jnp.float32) + head_bias
        logp = jax.nn.log_softmax(logits, -1)
        onehot = (labels[graph][:, None] == jnp.arange(classes, dtype=jnp.int32)[None, :]).astype(
            jnp.float32
        )
        target = (1.0 - smoothing) * onehot + smoothing / classes
        weights = train_mask[graph].astype(jnp.float32)
        loss_sum = loss_sum - jnp.sum(weights * jnp.sum(target * logp, -1))
        logits_low = lowered((weights / count)[:, None] * (jnp.exp(logp) - target))
        grad_head = grad_head + column_dot(current_low, logits_low)
        grad_bias = grad_bias + jnp.sum(logits_low.astype(jnp.float32), 0)
        grad_low = lowered(row_dot(logits_low, head_low))
        for layer in reversed(range(layers)):
            grad_inputs, grad_weight, grad_pair = layer_backward(
                adj,
                conv_full[layer],
                norm_params[layer, 0],
                kept_list[layer],
                grad_low.astype(jnp.float32),
                total_rows,
            )
            grad_conv[layer] = grad_conv[layer] + grad_weight
            grad_norm[layer] = grad_norm[layer] + grad_pair
            grad_low = lowered(grad_inputs)
        grad_input = grad_input + column_dot(inputs, grad_low)
    grad_conv_all = jnp.stack(grad_conv)
    grad_norm_all = jnp.stack(grad_norm)
    grad_input, grad_conv_all, grad_head, grad_bias, grad_norm_all, loss_sum = lax.psum(
        (grad_input, grad_conv_all, grad_head, grad_bias, grad_norm_all, loss_sum), "node"
    )
    grad_input, grad_conv_all = (
        lax.psum_scatter(grad_input, "grp", scatter_dimension=1, tiled=True),
        lax.psum_scatter(grad_conv_all, "grp", scatter_dimension=2, tiled=True),
    )
    grad_head, grad_bias, grad_norm_all, loss_sum = lax.psum(
        (grad_head, grad_bias, grad_norm_all, loss_sum), "grp"
    )
    moment_in = muon_beta * input_moment + grad_input
    moment_conv = muon_beta * conv_moment + grad_conv_all
    ortho_in, ortho_first, ortho_second = orthogonal_blocks(
        moment_in, moment_conv[0], moment_conv[1]
    )
    factor_in = 0.2 * float(max(f_width, hidden)) ** 0.5
    factor_conv = 0.2 * float(2 * hidden) ** 0.5
    input_new = input_weight - muon_rate * (factor_in * ortho_in + decay_rate * input_weight)
    ortho_conv = jnp.stack([ortho_first, ortho_second])
    conv_new = conv_weight - muon_rate * (factor_conv * ortho_conv + decay_rate * conv_weight)
    head_new, head_first_new, head_second_new = adamw(
        head_weight, grad_head, head_first, head_second
    )
    bias_new, bias_first_new, bias_second_new = adamw(head_bias, grad_bias, bias_first, bias_second)
    norm_new, norm_first_new, norm_second_new = adamw(
        norm_params, grad_norm_all, norm_first, norm_second
    )
    loss_parts = jnp.stack([loss_sum, count])
    return (
        loss_parts,
        input_new,
        moment_in,
        conv_new,
        moment_conv,
        head_new,
        head_first_new,
        head_second_new,
        bias_new,
        bias_first_new,
        bias_second_new,
        norm_new,
        norm_first_new,
        norm_second_new,
    )

MESH = pl.DeviceIdType.MESH
NT = (((1,), (1,)), ((), ()))
NN = (((1,), (0,)), ((), ()))
VMEM_BYTES = 56 * 1024 * 1024
ROUNDS = 8
EARLY_STEPS = 0


def flip(index, bit):
    return index + bit - 2 * bit * lax.rem(lax.div(index, bit), 2)


def dot(left, right, dims=NN):
    return lax.dot_general(left, right, dims, preferred_element_type=jnp.float32)


def split(value):
    high = lowered(value)
    return high, lowered(value - high.astype(jnp.float32))


def dot_three(left, right, dims=NN):
    left_high, left_rest = left
    right_high, right_rest = right
    axis = dims[0][1][0]
    return dot(
        jnp.concatenate([left_high, left_high, left_rest], 1),
        jnp.concatenate([right_high, right_rest, right_high], axis),
        dims,
    )


def step_kernel(
    groups,
    classes,
    feat,
    adj,
    labels,
    train,
    w_in,
    m_in,
    w_conv,
    m_conv,
    w_head,
    f_head,
    s_head,
    w_bias,
    f_bias,
    s_bias,
    w_norm,
    f_norm,
    s_norm,
    o_loss,
    o_in,
    o_in_m,
    o_conv,
    o_conv_m,
    o_head,
    o_head_f,
    o_head_s,
    o_bias,
    o_bias_f,
    o_bias_s,
    o_norm,
    o_norm_f,
    o_norm_s,
    av,
    xg,
    hg,
    dg,
    pad,
    padh,
    wa,
    wb,
    wn,
    wt_head,
    h0,
    agg,
    act,
    slope,
    ms,
    axh,
    accx,
    acc,
    h2,
    dh,
    dp,
    gt,
    q1,
    q2,
    tall_in,
    ght,
    st,
    zs,
    sums,
    mpc,
    mit,
    mi,
    gbc,
    gbi,
    gbh,
    rsc,
    rsi,
    rsh,
    zc,
    zi,
    zh,
    mf,
    mfi,
    hf,
    y_conv,
    y_in,
    loc,
    ga_s,
    ga_r,
    st_s,
    st_r,
    z_s,
    z_r,
    zf_s,
    zf_r,
    rs_s,
    rs_r,
    ag_s,
    ag_r,
):
    f32 = jnp.float32
    bf16 = jnp.bfloat16
    width, graphs, rows = feat.shape
    total = adj.shape[2]
    hidden = w_head.shape[1]
    wide = 2 * hidden
    shard = hidden // groups
    part = shard // 4
    half = rows // 2
    span_in = 16 * ((width + 15) // 16)
    chunk = min(rows, 128)
    chunks = rows // chunk
    g = lax.axis_index("grp")
    me = lax.axis_index("node")
    core = lax.rem(me, 2)
    chip = lax.div(me, 2)
    n_sib, n_x, n_y, n_d = flip(me, 1), flip(me, 2), flip(me, 4), flip(flip(me, 2), 4)
    peers = [n_d, flip(n_d, 1), n_x, n_y, flip(n_x, 1), flip(n_y, 1), n_sib]
    z_peers = [lax.rem(g + d, groups) for d in range(1, groups)]
    z_from = [lax.rem(g + groups - d, groups) for d in range(1, groups)]
    sent = []

    def send(src, dst, s_sem, r_sem, group, node):
        pltpu.make_async_remote_copy(
            src_ref=src,
            dst_ref=dst,
            send_sem=s_sem,
            recv_sem=r_sem,
            device_id=(group, node),
            device_id_type=MESH,
        ).start()

    def drain(sem, view):
        pltpu.make_async_copy(view, view, sem).wait()

    def lanes_of_core(span):
        return pl.ds(pl.multiple_of(core * span, span), span)

    barrier = pltpu.get_barrier_semaphore()
    for node in peers:
        pl.semaphore_signal(barrier, inc=1, device_id=(g, node), device_id_type=MESH)
    for group in z_peers:
        pl.semaphore_signal(barrier, inc=1, device_id=(group, me), device_id_type=MESH)

    own_a = [pltpu.make_async_copy(adj.at[s], av.at[s], loc.at[s]) for s in range(graphs)]
    part_rows = pl.ds(pl.multiple_of(chip * part, part), part)
    core_lanes = lanes_of_core(hidden)
    own_m = [
        pltpu.make_async_copy(m_conv.at[l, part_rows, core_lanes], mpc.at[l, g], loc.at[graphs + l])
        for l in range(2)
    ]
    for copy in own_a + own_m:
        copy.start()

    high_rows = pl.ds(pl.multiple_of(g * shard, shard), shard)
    padh[...] = jnp.zeros_like(padh)
    for s in range(graphs):
        padh[pl.ds(0, width), :] = feat[:, s, :].astype(f32)
        xg[s, me] = lowered(padh[pl.ds(0, span_in), :])
    mit[...] = jnp.zeros_like(mit)
    mit[high_rows, pl.ds(0, width)] = w_in[...]
    wa[high_rows, pl.ds(0, wide)] = lowered(w_conv[0])
    wa[high_rows, pl.ds(wide, 128)] = lowered(mit[high_rows, :])
    wb[high_rows, :] = lowered(w_conv[1])
    pl.semaphore_wait(barrier, 7 + groups - 1)

    def gather_of(index, ref, by_lane=False):
        low, high = pl.ds(0, half), pl.ds(half, half)

        def go(r, node, block, span=None):
            view = ref.at[block]
            if span is not None:
                view = ref.at[block, :, span] if by_lane else ref.at[block, span]
            send(view, view, ga_s.at[index], ga_r.at[5 * index + r], g, node)

        def arrived(r, blocks):
            drain(ga_r.at[5 * index + r], ref.at[pl.ds(0, blocks)])

        sent.append((ga_s.at[index], ref.at[pl.ds(0, 7)]))

        def own_first():
            go(0, n_x, me, low)
            go(0, n_y, me, high)
            go(3, n_sib, me)

        def own_second():
            go(1, n_x, me, high)
            go(1, n_y, me, low)

        def own():
            own_first()
            own_second()

        def relay():
            arrived(0, 1)
            go(2, n_y, n_x, low)
            go(2, n_x, n_y, high)

        def near():
            arrived(1, 1)
            go(3, n_sib, n_x)
            go(3, n_sib, n_y)

        def far():
            arrived(2, 1)
            go(4, n_sib, n_d)

        def near_ready():
            arrived(3, 3)

        def far_ready():
            arrived(4, 1)

        return own, relay, near, far, near_ready, far_ready, own_first, own_second

    def chip_at(i):
        cx = lax.rem(lax.rem(chip, 2) + lax.rem(i, 2), 2)
        cy = lax.rem(lax.div(chip, 2) + lax.div(i, 2), 2)
        return cx + 2 * cy

    def product(s, ref, out, first, last):
        if first == 0:
            out[...] = jnp.zeros_like(out)

        def body(i, carry):
            c = chip_at(i)
            block = ref[pl.ds(2 * c, 2)].reshape(2 * rows, ref.shape[2])
            left = av[s, :, pl.ds(pl.multiple_of(c * 2 * rows, 2 * rows), 2 * rows)]
            out[...] += dot(left, block)
            return carry

        lax.fori_loop(first, last, body, 0)

    def product_x(s, first, last):
        if first == 0:
            accx[...] = jnp.zeros_like(accx)

        def body(i, carry):
            c = chip_at(i)
            left = av[s, :, pl.ds(pl.multiple_of(c * 2 * rows, 2 * rows), 2 * rows)]
            right = jnp.concatenate([xg[s, 2 * c], xg[s, 2 * c + 1]], 1)
            accx[...] += dot(left, right, NT)
            return carry

        lax.fori_loop(first, last, body, 0)

    def over_rows(body, carry):
        def one(i, value):
            return body(pl.ds(pl.multiple_of(i * chunk, chunk), chunk), value)

        return lax.fori_loop(0, chunks, one, carry)

    def fold(value):
        return jnp.sum(value.reshape(chunk // 8, 8, hidden), 0)

    def plane_send(k, lines):
        side = hidden // 2
        for i, line in enumerate(lines):
            st[k, me, 2 * i : 2 * i + 1, :] = line[:, :side]
            st[k, me, 2 * i + 1 : 2 * i + 2, :] = line[:, side:]
        view = st.at[k, me]
        for node in peers:
            send(view, view, st_s.at[k], st_r.at[k], g, node)
        sent.append((st_s.at[k], st.at[k, pl.ds(0, 7)]))

    def plane_sum(k):
        drain(st_r.at[k], st.at[k, pl.ds(0, 7)])
        value = st[k, 0]
        for i in range(1, 8):
            value = value + st[k, i]
        lines = [jnp.concatenate([value[i : i + 1], value[i + 1 : i + 2]], 1) for i in (0, 2, 4, 6)]
        return jnp.concatenate([*lines, jnp.zeros((4, hidden), f32)], 0)

    z_all = {}

    def z_send(k, view, all_views):
        for group in z_peers:
            send(view, view, z_s.at[k], z_r.at[k], group, me)
        z_all[k] = all_views
        sent.append((z_s.at[k], all_views))

    def z_wait(k):
        drain(z_r.at[k], z_all[k])

    others = pl.ds(0, groups - 1)

    x_g = [gather_of(s, xg.at[s], True) for s in range(2)]
    h_g = [gather_of(2 + s, hg.at[s]) for s in range(2)]
    d_g = [gather_of(4 + s, dg.at[s]) for s in range(2)]

    own_rows = pl.ds(pl.multiple_of(g * shard, shard), shard)
    strip = shard // 2

    def strip_of(group):
        return pl.ds(pl.multiple_of(group * shard + core * strip, strip), strip)

    strips = pl.ds(0, strip * (groups - 1))

    def z_forward(k, ref):
        z_wait(k)
        for group in z_from:
            view = ref.at[strip_of(group)]
            send(view, view, zf_s.at[k], zf_r.at[k], g, n_sib)
        sent.append((zf_s.at[k], ref.at[strips]))

    def z_forwarded(k):
        drain(zf_r.at[k], z_all[k])

    x_g[0][0]()
    z_send(0, wa.at[strip_of(g)], wa.at[strips])
    mit[high_rows, pl.ds(0, width)] = m_in[...]
    x_g[0][1]()
    x_g[1][0]()
    z_send(1, wb.at[strip_of(g)], wb.at[strips])
    padh[...] = jnp.zeros_like(padh)
    padh[pl.ds(0, classes), pl.ds(0, hidden)] = w_head[...]
    wt_head[...] = lowered(padh[:, :hidden])
    pad[...] = jnp.zeros_like(pad)
    pad[pl.ds(0, 8), pl.ds(0, classes)] = jnp.broadcast_to(w_bias[...], (8, classes))
    bias_col = pad[...].T[:64, :1]
    count_own = jnp.sum(train[...].astype(f32), axis=1, keepdims=True)
    count_own = count_own[0:1] + count_own[1:2]
    x_g[0][2]()
    for copy in own_m:
        copy.wait()
    for copy in own_a:
        copy.wait()

    def forward_act(s, l, k, first, second, w_first, w_second):
        acc[...] = dot(first, w_first, NT) + dot(second, w_second, NT)

        def body(span, carry):
            pre = acc[span, :]
            square = pre * pre
            inner = 0.7978845608028654 * pre * (1.0 + 0.044715 * square)
            t = jnp.tanh(inner)
            value = 0.5 * pre * (1.0 + t)
            act[l, s, span, :] = value
            slope[l, s, span, :] = 0.5 * (1.0 + t) + 0.5 * pre * (1.0 - t * t) * (
                0.7978845608028654 * (1.0 + 3.0 * 0.044715 * square)
            )
            return carry[0] + fold(value), carry[1] + fold(value * value)

        zero = jnp.zeros((8, hidden), f32)
        one, two = over_rows(body, (zero, zero))
        lines = [jnp.sum(one, 0, keepdims=True), jnp.sum(two, 0, keepdims=True)]
        none = jnp.zeros((1, hidden), f32)
        lines.append(jnp.broadcast_to(count_own, (1, hidden)) if k == 0 else none)
        plane_send(k, lines + [none])

    def normalise(s, l, k, out):
        sums_all = plane_sum(k)
        mean = sums_all[0:1] / total
        var = sums_all[1:2] / total - mean * mean
        inv = lax.rsqrt(var + norm_eps)
        ms[l, s, 0:1, :] = inv
        gain, shift = w_norm[l, 0:1, :], w_norm[l, 1:2, :]

        def body(span, carry):
            normed = (act[l, s, span, :] - mean) * inv
            act[l, s, span, :] = normed
            out[span, :] = lowered(normed * gain + shift)
            return carry

        over_rows(body, 0)
        return sums_all

    def layer_zero(s):
        high, rest = split(accx[...])
        axh[s] = high
        w = wa[:, wide : wide + span_in]
        agg[0, s] = lowered(dot(high, w, NT) + dot(rest, w, NT))
        h0[s] = lowered(dot(xg[s, me].T, w, NT))
        forward_act(s, 0, s, h0[s], agg[0, s], wa[:, :hidden], wa[:, hidden:wide])

    def layer_one(s):
        agg[1, s] = lowered(acc[...])
        forward_act(s, 1, 2 + s, hg[s, me], agg[1, s], wb[:, :hidden], wb[:, hidden:])

    def head(s, count):
        value = h2[s]
        logits = dot(wt_head[pl.ds(0, 64), :], value, NT) + bias_col
        at = lax.broadcasted_iota(jnp.int32, (64, rows), 0)
        valid = at < classes
        logits = jnp.where(valid, logits, -1e30)
        shifted = logits - jnp.max(logits, 0, keepdims=True)
        logp = shifted - jnp.log(jnp.sum(jnp.exp(shifted), 0, keepdims=True))
        onehot = jnp.where(at == labels[s : s + 1, :], 1.0, 0.0)
        target = jnp.where(valid, (1.0 - smoothing) * onehot + smoothing / classes, 0.0)
        weights = train[s : s + 1, :].astype(f32)
        node_loss = jnp.sum(target * logp, 0, keepdims=True)
        loss = -jnp.sum(weights * node_loss, axis=1, keepdims=True)
        delta = (weights / count) * (jnp.exp(logp) - target)
        delta_low = lowered(delta)
        value_t = dot(delta_low, value)
        ght[...] = value_t if s == 0 else ght[...] + value_t
        column = dot(jnp.ones((8, rows), bf16), delta_low, NT)
        tall = jnp.concatenate([delta_low.astype(f32), jnp.zeros((64, rows), f32)], 0).T
        dh[s] = lowered(dot(lowered(tall), wt_head[...])).astype(f32)
        return loss, column

    def backward_sums(s, l, k, extra=None):
        def body(span, carry):
            grad = dh[s, span, :]
            return carry[0] + fold(grad), carry[1] + fold(grad * act[l, s, span, :])

        zero = jnp.zeros((8, hidden), f32)
        one, two = over_rows(body, (zero, zero))
        lines = [jnp.sum(one, 0, keepdims=True), jnp.sum(two, 0, keepdims=True)]
        if extra is None:
            lines += [jnp.zeros((1, hidden), f32)] * 2
        else:
            rest = jnp.zeros((1, hidden - 64), f32)
            lines.append(jnp.concatenate([extra[1][0:1], rest], 1))
            lines.append(jnp.broadcast_to(extra[0], (1, hidden)))
        plane_send(k, lines)

    def backward_pre(s, l, k):
        sums_all = plane_sum(k)
        sums[1 - l] = sums_all if s == 0 else sums[1 - l] + sums_all
        gain = w_norm[l, 0:1, :]
        inv = ms[l, s, 0:1, :]
        first = gain * sums_all[0:1] / total
        second = gain * sums_all[1:2] / total

        def body(span, carry):
            grad = dh[s, span, :] * gain - first - act[l, s, span, :] * second
            dp[l, s, span, :] = lowered(grad * inv * slope[l, s, span, :])
            return carry

        over_rows(body, 0)

    def conv_grads(s, l, left, right):
        turned = dp[l, s].T
        one, two = dot(turned, left), dot(turned, right)
        if s == 0:
            gt[l, :, :hidden] = one
            gt[l, :, hidden:] = two
        else:
            gt[l, :, :hidden] += one
            gt[l, :, hidden:] += two
        return turned

    def pieces_send(k, src, dst, where):
        for node in peers:
            send(where(src, node), dst.at[me], rs_s.at[k], rs_r.at[k], g, node)
        sent.append((rs_s.at[k], dst.at[pl.ds(0, 7)]))

    def pieces_sum(k, src, dst, own):
        dst[me] = own
        drain(rs_r.at[k], dst.at[pl.ds(0, 7)])
        value = dst[0].astype(f32)
        for i in range(1, 8):
            value = value + dst[i].astype(f32)
        return value

    def conv_piece(ref, node):
        n_core, n_chip = lax.rem(node, 2), lax.div(node, 2)
        return ref.at[:, n_chip, :, pl.ds(pl.multiple_of(n_core * hidden, hidden), hidden)]

    def in_piece(ref, node):
        return ref.at[node]

    def head_piece(ref, node):
        n_core, n_chip = lax.rem(node, 2), lax.div(node, 2)
        return ref.at[n_chip, :, pl.ds(pl.multiple_of(n_core * (hidden // 2), hidden // 2), hidden // 2)]

    def over_z(k, buf):
        z_wait(k)
        value = buf[0].astype(f32)
        for i in range(1, groups):
            value = value + buf[i].astype(f32)
        return value

    def spread(k, view_of, some):
        view = view_of(me)
        for node in (n_d, n_x, n_y):
            send(view, view, ag_s.at[k], ag_r.at[2 * k], g, node)
        send(view, view, ag_s.at[k], ag_r.at[2 * k + 1], g, n_sib)
        sent.append((ag_s.at[k], some(4)))

    def spread_forward(k, view_of, some):
        drain(ag_r.at[2 * k], some(3))
        for node in (n_x, n_y, n_d):
            view = view_of(node)
            send(view, view, ag_s.at[4 + k], ag_r.at[2 * k + 1], g, n_sib)
        sent.append((ag_s.at[4 + k], some(3)))

    def spread_wait(k, some):
        drain(ag_r.at[2 * k + 1], some(4))

    head_lanes = lanes_of_core(hidden // 2)

    x_g[0][4]()
    product_x(0, 0, 3)
    x_g[0][3]()
    z_forward(0, wa)
    x_g[0][5]()
    product_x(0, 3, 4)
    x_g[1][1]()
    z_forwarded(0)
    layer_zero(0)
    x_g[1][2]()
    x_g[1][4]()
    product_x(1, 0, 3)
    x_g[1][3]()
    x_g[1][5]()
    product_x(1, 3, 4)
    count_plane = normalise(0, 0, 0, hg.at[0, me])
    h_g[0][6]()
    layer_zero(1)
    h_g[0][7]()
    zs[0, g] = count_plane
    z_send(3, zs.at[0, g], zs.at[0, others])
    z_forward(1, wb)
    normalise(1, 0, 1, hg.at[1, me])
    h_g[0][1]()
    h_g[1][0]()
    z_send(6, mpc.at[0, g], mpc.at[0, others])
    z_send(7, mpc.at[1, g], mpc.at[1, others])
    z_send(8, mit.at[own_rows], mit.at[pl.ds(0, shard * (groups - 1))])
    z_forwarded(1)
    wn[...] = wa[:, :wide].T
    h_g[0][2]()
    h_g[0][4]()
    product(0, hg.at[0], acc, 0, 3)
    h_g[0][3]()
    h_g[0][5]()
    product(0, hg.at[0], acc, 3, 4)
    layer_one(0)
    h_g[1][1]()
    z_wait(3)
    count = zs[0, 0]
    for i in range(1, groups):
        count = count + zs[0, i]
    count = count[2:3, 0:1]
    h_g[1][2]()
    normalise(0, 1, 2, h2.at[0])
    loss_row = head(0, count)
    backward_sums(0, 1, 4, loss_row)
    h_g[1][3]()
    h_g[1][4]()
    product(1, hg.at[1], acc, 0, 3)
    h_g[1][5]()
    product(1, hg.at[1], acc, 3, 4)
    layer_one(1)
    backward_pre(0, 1, 4)
    dg[0, me] = lowered(dot(dp[1, 0], wb[:, hidden:]))
    d_g[0][0]()
    dh[0] = dot(dp[1, 0], wb[:, :hidden])
    normalise(1, 1, 3, h2.at[1])
    loss_row = head(1, count)
    backward_sums(1, 1, 5, loss_row)
    d_g[0][1]()
    conv_grads(0, 1, hg[0, me], agg[1, 0])
    backward_pre(1, 1, 5)
    dg[1, me] = lowered(dot(dp[1, 1], wb[:, hidden:]))
    d_g[1][0]()
    d_g[0][2]()
    dh[1] = dot(dp[1, 1], wb[:, :hidden])
    zs[1, g] = sums[0]
    z_send(4, zs.at[1, g], zs.at[1, others])
    d_g[0][4]()
    product(0, dg.at[0], acc, 0, 3)
    d_g[0][3]()
    d_g[0][5]()
    product(0, dg.at[0], acc, 3, 4)
    dh[0] = lowered(dh[0] + acc[...]).astype(f32)
    backward_sums(0, 0, 6)
    d_g[1][1]()
    conv_grads(1, 1, hg[1, me], agg[1, 1])
    gbc[1] = lowered(gt[1]).reshape(groups, 4, part, wide)
    gbh[...] = lowered(ght[...]).reshape(4, 16, hidden)
    pieces_send(0, gbc.at[1], rsc.at[1], conv_piece)
    pieces_send(1, gbh, rsh, head_piece)
    d_g[1][2]()
    backward_pre(0, 0, 6)
    turned = conv_grads(0, 0, h0[0], agg[0, 0])
    q1[...] = dot(turned, xg[0, me], NT)
    q2[...] = dot(turned, axh[0])
    d_g[1][4]()
    product(1, dg.at[1], acc, 0, 3)
    d_g[1][3]()
    d_g[1][5]()
    product(1, dg.at[1], acc, 3, 4)
    dh[1] = lowered(dh[1] + acc[...]).astype(f32)
    backward_sums(1, 0, 7)
    zc[1, g] = lowered(pieces_sum(0, None, rsc.at[1], conv_piece(gbc.at[1], me)[...]))
    z_send(9, zc.at[1, g], zc.at[1, others])
    zh[g] = lowered(pieces_sum(1, None, rsh, head_piece(gbh, me)[...]))
    z_send(10, zh.at[g], zh.at[others])
    z_wait(6)
    z_wait(7)
    z_wait(8)
    tall_in[...] = mit[...]
    mi[...] = tall_in[...].T.reshape(8, 16, hidden)
    tall_in[...] = jnp.zeros_like(tall_in)
    backward_pre(1, 0, 7)
    turned = conv_grads(1, 0, h0[1], agg[0, 1])
    gbc[0] = lowered(gt[0]).reshape(groups, 4, part, wide)
    pieces_send(2, gbc.at[0], rsc.at[0], conv_piece)
    q1[...] += dot(turned, xg[1, me], NT)
    q2[...] += dot(turned, axh[1])
    one, two = split(q1[...]), split(q2[...])
    w_self, w_near = wn[:hidden, :], wn[hidden:, :]
    g_in = dot(w_self, one[0]) + dot(w_self, one[1]) + dot(w_near, two[0]) + dot(w_near, two[1])
    tall_in[:, pl.ds(0, span_in)] = g_in
    gbi[...] = lowered(tall_in[...].T).reshape(8, 16, hidden)
    pieces_send(3, gbi, rsi, in_piece)
    zs[2, g] = sums[1]
    z_send(5, zs.at[2, g], zs.at[2, others])

    def conv_view(l):
        return lambda node: conv_piece(mf.at[l], node)

    def conv_some(l):
        return lambda n: mf.at[l, :, pl.ds(0, n), :, pl.ds(0, hidden)]

    def head_some(n):
        return hf.at[pl.ds(0, n), :, pl.ds(0, hidden // 2)]

    def in_some(n):
        return mfi.at[pl.ds(0, n)]

    def head_view(node):
        return head_piece(hf, node)

    def in_view(node):
        return mfi.at[node]

    def scaled(value):
        norm = jnp.sqrt(jnp.sum(jnp.sum(value * value, 0, keepdims=True), 1, keepdims=True))
        return value / (norm + 1e-07)

    def iterate(refs, first, last):
        for i in range(first, last):
            for ref in refs:
                value = ref[...]
                pair = split(value)
                gram = dot_three(pair, pair, NT)
                gram_high, gram_rest = split(gram)
                cross = dot(gram_high, gram_rest)
                square = dot(gram_high, gram_high) + cross + cross.T
                poly = split(poly_second * gram + poly_third * square)
                ref[...] = poly_first * value + dot_three(poly, pair)

    factor_conv = 0.2 * float(wide) ** 0.5
    factor_in = 0.2 * float(max(width, hidden)) ** 0.5

    def conv_out(l):
        o_conv_m[l] = mf[l, g].reshape(shard, wide)
        ortho = y_conv[l, own_rows, :]
        weight = w_conv[l]
        o_conv[l] = weight - muon_rate * (factor_conv * ortho + decay_rate * weight)

    mf[1, :, chip, :, core_lanes] = muon_beta * mpc[1] + over_z(9, zc.at[1])
    spread(0, conv_view(1), conv_some(1))
    hf[chip, :, head_lanes] = over_z(10, zh)
    spread(1, head_view, head_some)
    zc[0, g] = lowered(pieces_sum(2, None, rsc.at[0], conv_piece(gbc.at[0], me)[...]))
    z_send(11, zc.at[0, g], zc.at[0, others])
    zi[g] = lowered(pieces_sum(3, None, rsi, gbi[me]))
    z_send(12, zi.at[g], zi.at[others])
    spread_forward(0, conv_view(1), conv_some(1))
    spread_forward(1, head_view, head_some)
    spread_wait(0, conv_some(1))
    y_conv[1] = scaled(mf[1].reshape(hidden, wide))
    iterate([y_conv.at[1]], 0, EARLY_STEPS)
    mf[0, :, chip, :, core_lanes] = muon_beta * mpc[0] + over_z(11, zc.at[0])
    spread(2, conv_view(0), conv_some(0))
    mfi[me] = muon_beta * mi[me] + over_z(12, zi)
    spread(3, in_view, in_some)
    iterate([y_conv.at[1]], EARLY_STEPS, NS_STEPS)
    spread_forward(2, conv_view(0), conv_some(0))
    spread_forward(3, in_view, in_some)
    conv_out(1)

    spread_wait(1, head_some)
    grad = hf[...].reshape(64, hidden)[:classes]
    o_head[...], o_head_f[...], o_head_s[...] = adamw(w_head[...], grad, f_head[...], s_head[...])
    z_wait(4)
    z_wait(5)
    late = zs[1, 0]
    early = zs[2, 0]
    for i in range(1, groups):
        late = late + zs[1, i]
        early = early + zs[2, i]
    for l, rows_l in ((0, early), (1, late)):
        grad = jnp.concatenate([rows_l[1:2], rows_l[0:1]], 0)
        o_norm[l], o_norm_f[l], o_norm_s[l] = adamw(w_norm[l], grad, f_norm[l], s_norm[l])
    o_bias[...], o_bias_f[...], o_bias_s[...] = adamw(
        w_bias[...], late[2:3, :classes], f_bias[...], s_bias[...]
    )
    o_loss[...] = jnp.concatenate([late[3:4, 0:1], count], 1)

    spread_wait(2, conv_some(0))
    spread_wait(3, in_some)
    y_conv[0] = scaled(mf[0].reshape(hidden, wide))
    y_in[...] = scaled(mfi[...].reshape(128, hidden))
    iterate([y_conv.at[0], y_in], 0, NS_STEPS)
    conv_out(0)
    tall_in[...] = mfi[...].reshape(128, hidden).T
    o_in_m[...] = tall_in[own_rows, :][:, :width]
    tall_in[...] = y_in[...].T
    ortho = tall_in[own_rows, :][:, :width]
    weight = w_in[...]
    o_in[...] = weight - muon_rate * (factor_in * ortho + decay_rate * weight)
    for sem, view in sent:
        drain(sem, view)


def planned(mesh):
    groups = mesh.shape["grp"]

    def call(
        features,
        adjacency,
        labels,
        train_mask,
        input_weight,
        input_moment,
        conv_weight,
        conv_moment,
        head_weight,
        head_first,
        head_second,
        head_bias,
        bias_first,
        bias_second,
        norm_params,
        norm_first,
        norm_second,
    ):
        f32, bf16 = jnp.float32, jnp.bfloat16
        graphs, rows, width = features.shape
        total = adjacency.shape[2]
        hidden, classes = head_weight.shape
        wide = 2 * hidden
        shard = hidden // groups
        part = shard // 4
        span_in = 16 * ((width + 15) // 16)
        vm = pltpu.VMEM
        sem = pltpu.SemaphoreType.DMA
        shape = jax.ShapeDtypeStruct
        near = pl.BlockSpec(memory_space=pltpu.VMEM)
        anywhere = pl.BlockSpec(memory_space=pl.ANY)
        results = [
            shape((1, 2), f32),
            shape((shard, width), f32),
            shape((shard, width), f32),
            shape((2, shard, wide), f32),
            shape((2, shard, wide), f32),
            shape((classes, hidden), f32),
            shape((classes, hidden), f32),
            shape((classes, hidden), f32),
            shape((1, classes), f32),
            shape((1, classes), f32),
            shape((1, classes), f32),
            shape(norm_params.shape, f32),
            shape(norm_params.shape, f32),
            shape(norm_params.shape, f32),
        ]
        outs = pl.pallas_call(
            functools.partial(step_kernel, groups, classes),
            out_shape=results,
            in_specs=[near, anywhere, near, near, near, near, near, anywhere] + [near] * 9,
            out_specs=[near] * 14,
            scratch_shapes=[
                vm((graphs, rows, total), bf16),
                vm((graphs, 8, span_in, rows), bf16),
                vm((graphs, 8, rows, hidden), bf16),
                vm((graphs, 8, rows, hidden), bf16),
                vm((128, 128), f32),
                vm((128, rows), f32),
                vm((hidden, wide + 128), bf16),
                vm((hidden, wide), bf16),
                vm((wide, hidden), bf16),
                vm((128, hidden), bf16),
                vm((graphs, rows, hidden), bf16),
                vm((2, graphs, rows, hidden), bf16),
                vm((2, graphs, rows, hidden), f32),
                vm((2, graphs, rows, hidden), f32),
                vm((2, graphs, 8, hidden), f32),
                vm((graphs, rows, span_in), bf16),
                vm((rows, span_in), f32),
                vm((rows, hidden), f32),
                vm((graphs, rows, hidden), bf16),
                vm((graphs, rows, hidden), f32),
                vm((2, graphs, rows, hidden), bf16),
                vm((2, hidden, wide), f32),
                vm((hidden, span_in), f32),
                vm((hidden, span_in), f32),
                vm((hidden, 128), f32),
                vm((64, hidden), f32),
                vm((ROUNDS, 8, 8, hidden // 2), f32),
                vm((3, groups, 8, hidden), f32),
                vm((2, 8, hidden), f32),
                vm((2, groups, part, hidden), f32),
                vm((hidden, 128), f32),
                vm((8, 16, hidden), f32),
                vm((2, groups, 4, part, wide), bf16),
                vm((8, 16, hidden), bf16),
                vm((4, 16, hidden), bf16),
                vm((2, 8, groups, part, hidden), bf16),
                vm((8, 16, hidden), bf16),
                vm((8, 16, hidden // 2), bf16),
                vm((2, groups, groups, part, hidden), bf16),
                vm((groups, 16, hidden), bf16),
                vm((groups, 16, hidden // 2), bf16),
                vm((2, groups, 4, part, wide), f32),
                vm((8, 16, hidden), f32),
                vm((4, 16, hidden), f32),
                vm((2, hidden, wide), f32),
                vm((128, hidden), f32),
                sem((graphs + 2,)),
                sem((6,)),
                sem((30,)),
                sem((ROUNDS,)),
                sem((ROUNDS,)),
                sem((13,)),
                sem((13,)),
                sem((2,)),
                sem((2,)),
                sem((4,)),
                sem((4,)),
                sem((8,)),
                sem((8,)),
            ],
            compiler_params=pltpu.CompilerParams(
                collective_id=0, has_side_effects=True, vmem_limit_bytes=VMEM_BYTES
            ),
            name="train_step",
        )(
            jnp.transpose(features, (2, 0, 1)),
            adjacency,
            labels,
            train_mask,
            input_weight.T,
            input_moment.T,
            jnp.swapaxes(conv_weight, 1, 2),
            jnp.swapaxes(conv_moment, 1, 2),
            head_weight.T,
            head_first.T,
            head_second.T,
            head_bias[None, :],
            bias_first[None, :],
            bias_second[None, :],
            norm_params,
            norm_first,
            norm_second,
        )
        outs = pl.pallas_call(
            hand_over,
            out_shape=results,
            in_specs=[near] * 14,
            out_specs=[near] * 14,
            name="hand_over",
        )(*outs)
        loss, in_new, in_m, conv_new, conv_m, h_new, h_f, h_s, b_new, b_f, b_s, *norms = outs
        return (
            loss[0],
            in_new.T,
            in_m.T,
            jnp.swapaxes(conv_new, 1, 2),
            jnp.swapaxes(conv_m, 1, 2),
            h_new.T,
            h_f.T,
            h_s.T,
            b_new[0],
            b_f[0],
            b_s[0],
            *norms,
        )

    return call


def hand_over(*refs):
    for source, target in zip(refs[:14], refs[14:]):
        target[...] = source[...]


def solution(mesh):
    placed = (
        P("grp", "node", None),
        P("grp", "node", None),
        P("grp", "node"),
        P("grp", "node"),
        P(None, "grp"),
        P(None, "grp"),
        P(None, None, "grp"),
        P(None, None, "grp"),
        P(),
        P(),
        P(),
        P(),
        P(),
        P(),
        P(),
        P(),
        P(),
    )
    small = mesh.shape["node"] == 8 and mesh.shape["grp"] == 4
    return jax.shard_map(
        planned(mesh) if small else per_device,
        mesh=mesh,
        in_specs=placed,
        out_specs=(
            P(),
            P(None, "grp"),
            P(None, "grp"),
            P(None, None, "grp"),
            P(None, None, "grp"),
            P(),
            P(),
            P(),
            P(),
            P(),
            P(),
            P(),
            P(),
            P(),
        ),
        check_vma=False,
    )
```

```python
import functools

import jax
import jax.numpy as jnp
from jax import lax
from jax.experimental import pallas as pl
from jax.experimental.pallas import tpu as pltpu
from jax.sharding import PartitionSpec as P

NS_STEPS = 5
STEP = 10


norm_eps = 1e-05
smoothing = 0.1
poly_first = 3.4445
poly_second = -4.775
poly_third = 2.0315
muon_beta = 0.95
muon_rate = 0.2
decay_rate = 0.01
adam_rate = 0.05
beta_first = 0.9
beta_second = 0.95
adam_eps = 1e-08


def lowered(value):
    return value.astype(jnp.bfloat16)


def matmul_hi(left, right):
    return jnp.dot(left, right, precision=lax.Precision.HIGHEST)


def column_dot(left, right):
    return lax.dot_general(
        left, right, (((0,), (0,)), ((), ())), preferred_element_type=jnp.float32
    )


def row_dot(left, right):
    return lax.dot_general(
        left, right, (((1,), (1,)), ((), ())), preferred_element_type=jnp.float32
    )


def neighbour_sum(adj, values):
    return jnp.dot(
        adj, lax.all_gather(values, "node", axis=0, tiled=True), preferred_element_type=jnp.float32
    )


def neighbour_back(adj, grads):
    return lax.psum_scatter(column_dot(adj, grads), "node", scatter_dimension=0, tiled=True)


def layer_forward(adj, inputs_low, weight_low, gain, shift, total_rows):
    hidden = weight_low.shape[1]
    agg_low = lowered(neighbour_sum(adj, inputs_low))
    pre = jnp.dot(inputs_low, weight_low[:hidden], preferred_element_type=jnp.float32)
    pre = pre + jnp.dot(agg_low, weight_low[hidden:], preferred_element_type=jnp.float32)
    act = jax.nn.gelu(pre)
    sums, squares = lax.psum((jnp.sum(act, 0), jnp.sum(act * act, 0)), "node")
    mean = sums / total_rows
    var = squares / total_rows - mean * mean
    inv_std = lax.rsqrt(var + norm_eps)
    normed = (act - mean) * inv_std
    return (normed * gain + shift, (inputs_low, agg_low, pre, normed, inv_std))


def layer_backward(adj, weight_low, gain, kept, grad_out, total_rows):
    inputs_low, agg_low, pre, normed, inv_std = kept
    hidden = weight_low.shape[1]
    grad_gain = jnp.sum(grad_out * normed, 0)
    grad_shift = jnp.sum(grad_out, 0)
    grad_normed = grad_out * gain
    first, second = lax.psum((jnp.sum(grad_normed, 0), jnp.sum(grad_normed * normed, 0)), "node")
    grad_act = (grad_normed - first / total_rows - normed * (second / total_rows)) * inv_std
    grad_pre = jax.vjp(jax.nn.gelu, pre)[1](grad_act)[0]
    pre_low = lowered(grad_pre)
    grad_weight = jnp.concatenate(
        [column_dot(inputs_low, pre_low), column_dot(agg_low, pre_low)], 0
    )
    grad_agg = lowered(row_dot(pre_low, weight_low[hidden:]))
    grad_inputs = row_dot(pre_low, weight_low[:hidden]) + neighbour_back(adj, grad_agg)
    return (grad_inputs, grad_weight, jnp.stack([grad_gain, grad_shift]))


def gram_of(block):
    return matmul_hi(block, block.T)


def orthogonal_blocks(first_block, second_block, third_block):
    blocks = [first_block, second_block, third_block]
    for step in range(NS_STEPS):
        grams = lax.psum((gram_of(blocks[0]), gram_of(blocks[1]), gram_of(blocks[2])), "grp")
        grams = list(grams)
        if step == 0:
            scales = [jnp.sqrt(jnp.trace(gram)) + 1e-07 for gram in grams]
            blocks = [block / scale for block, scale in zip(blocks, scales)]
            grams = [gram / (scale * scale) for gram, scale in zip(grams, scales)]
        polys = [poly_second * gram + poly_third * matmul_hi(gram, gram) for gram in grams]
        blocks = [poly_first * block + matmul_hi(poly, block) for block, poly in zip(blocks, polys)]
    return blocks


def adamw(weight, grad, first, second):
    first_new = beta_first * first + (1.0 - beta_first) * grad
    second_new = beta_second * second + (1.0 - beta_second) * grad * grad
    fixed_first = first_new / (1.0 - beta_first**STEP)
    fixed_second = second_new / (1.0 - beta_second**STEP)
    update = fixed_first / (jnp.sqrt(fixed_second) + adam_eps) + decay_rate * weight
    return (weight - adam_rate * update, first_new, second_new)


def per_device(
    features,
    adjacency,
    labels,
    train_mask,
    input_weight,
    input_moment,
    conv_weight,
    conv_moment,
    head_weight,
    head_first,
    head_second,
    head_bias,
    bias_first,
    bias_second,
    norm_params,
    norm_first,
    norm_second,
):
    layers = conv_weight.shape[0]
    hidden = head_weight.shape[0]
    classes = head_weight.shape[1]
    f_width = input_weight.shape[0]
    total_rows = features.shape[1] * lax.axis_size("node")
    input_full, conv_full = (
        lax.all_gather(lowered(input_weight), "grp", axis=1, tiled=True),
        lax.all_gather(lowered(conv_weight), "grp", axis=2, tiled=True),
    )
    head_low = lowered(head_weight)
    count = lax.psum(jnp.sum(train_mask).astype(jnp.float32), ("grp", "node"))
    grad_input = jnp.zeros((f_width, hidden), jnp.float32)
    grad_conv = [jnp.zeros((2 * hidden, hidden), jnp.float32) for layer in range(layers)]
    grad_norm = [jnp.zeros((2, hidden), jnp.float32) for layer in range(layers)]
    grad_head = jnp.zeros((hidden, classes), jnp.float32)
    grad_bias = jnp.zeros((classes,), jnp.float32)
    loss_sum = jnp.float32(0.0)
    for graph in range(features.shape[0]):
        inputs = features[graph]
        adj = adjacency[graph]
        current_low = lowered(jnp.dot(inputs, input_full, preferred_element_type=jnp.float32))
        kept_list = []
        for layer in range(layers):
            output, kept = layer_forward(
                adj,
                current_low,
                conv_full[layer],
                norm_params[layer, 0],
                norm_params[layer, 1],
                total_rows,
            )
            kept_list.append(kept)
            current_low = lowered(output)
        logits = jnp.dot(current_low, head_low, preferred_element_type=jnp.float32) + head_bias
        logp = jax.nn.log_softmax(logits, -1)
        onehot = (labels[graph][:, None] == jnp.arange(classes, dtype=jnp.int32)[None, :]).astype(
            jnp.float32
        )
        target = (1.0 - smoothing) * onehot + smoothing / classes
        weights = train_mask[graph].astype(jnp.float32)
        loss_sum = loss_sum - jnp.sum(weights * jnp.sum(target * logp, -1))
        logits_low = lowered((weights / count)[:, None] * (jnp.exp(logp) - target))
        grad_head = grad_head + column_dot(current_low, logits_low)
        grad_bias = grad_bias + jnp.sum(logits_low.astype(jnp.float32), 0)
        grad_low = lowered(row_dot(logits_low, head_low))
        for layer in reversed(range(layers)):
            grad_inputs, grad_weight, grad_pair = layer_backward(
                adj,
                conv_full[layer],
                norm_params[layer, 0],
                kept_list[layer],
                grad_low.astype(jnp.float32),
                total_rows,
            )
            grad_conv[layer] = grad_conv[layer] + grad_weight
            grad_norm[layer] = grad_norm[layer] + grad_pair
            grad_low = lowered(grad_inputs)
        grad_input = grad_input + column_dot(inputs, grad_low)
    grad_conv_all = jnp.stack(grad_conv)
    grad_norm_all = jnp.stack(grad_norm)
    grad_input, grad_conv_all, grad_head, grad_bias, grad_norm_all, loss_sum = lax.psum(
        (grad_input, grad_conv_all, grad_head, grad_bias, grad_norm_all, loss_sum), "node"
    )
    grad_input, grad_conv_all = (
        lax.psum_scatter(grad_input, "grp", scatter_dimension=1, tiled=True),
        lax.psum_scatter(grad_conv_all, "grp", scatter_dimension=2, tiled=True),
    )
    grad_head, grad_bias, grad_norm_all, loss_sum = lax.psum(
        (grad_head, grad_bias, grad_norm_all, loss_sum), "grp"
    )
    moment_in = muon_beta * input_moment + grad_input
    moment_conv = muon_beta * conv_moment + grad_conv_all
    ortho_in, ortho_first, ortho_second = orthogonal_blocks(
        moment_in, moment_conv[0], moment_conv[1]
    )
    factor_in = 0.2 * float(max(f_width, hidden)) ** 0.5
    factor_conv = 0.2 * float(2 * hidden) ** 0.5
    input_new = input_weight - muon_rate * (factor_in * ortho_in + decay_rate * input_weight)
    ortho_conv = jnp.stack([ortho_first, ortho_second])
    conv_new = conv_weight - muon_rate * (factor_conv * ortho_conv + decay_rate * conv_weight)
    head_new, head_first_new, head_second_new = adamw(
        head_weight, grad_head, head_first, head_second
    )
    bias_new, bias_first_new, bias_second_new = adamw(head_bias, grad_bias, bias_first, bias_second)
    norm_new, norm_first_new, norm_second_new = adamw(
        norm_params, grad_norm_all, norm_first, norm_second
    )
    loss_parts = jnp.stack([loss_sum, count])
    return (
        loss_parts,
        input_new,
        moment_in,
        conv_new,
        moment_conv,
        head_new,
        head_first_new,
        head_second_new,
        bias_new,
        bias_first_new,
        bias_second_new,
        norm_new,
        norm_first_new,
        norm_second_new,
    )

MESH = pl.DeviceIdType.MESH
NT = (((1,), (1,)), ((), ()))
NN = (((1,), (0,)), ((), ()))
VMEM_BYTES = 56 * 1024 * 1024
ROUNDS = 8
EARLY_STEPS = 0


def flip(index, bit):
    return index + bit - 2 * bit * lax.rem(lax.div(index, bit), 2)


def dot(left, right, dims=NN):
    return lax.dot_general(left, right, dims, preferred_element_type=jnp.float32)


def split(value):
    high = lowered(value)
    return high, lowered(value - high.astype(jnp.float32))


def dot_three(left, right, dims=NN):
    left_high, left_rest = left
    right_high, right_rest = right
    axis = dims[0][1][0]
    return dot(
        jnp.concatenate([left_high, left_high, left_rest], 1),
        jnp.concatenate([right_high, right_rest, right_high], axis),
        dims,
    )


def step_kernel(
    groups,
    classes,
    feat_far,
    adj,
    labels_far,
    train_far,
    w_in_far,
    m_in_far,
    w_conv_far,
    m_conv,
    w_head_far,
    f_head_far,
    s_head_far,
    w_bias_far,
    f_bias_far,
    s_bias_far,
    w_norm_far,
    f_norm_far,
    s_norm_far,
    o_loss,
    o_in,
    o_in_m,
    o_conv,
    o_conv_m,
    o_head,
    o_head_f,
    o_head_s,
    o_bias,
    o_bias_f,
    o_bias_s,
    o_norm,
    o_norm_f,
    o_norm_s,
    av,
    xg,
    hg,
    dg,
    pad,
    padh,
    wa,
    wb,
    wn,
    wt_head,
    h0,
    agg,
    act,
    slope,
    ms,
    axh,
    accx,
    acc,
    h2,
    dh,
    dp,
    gt,
    q1,
    q2,
    tall_in,
    ght,
    st,
    zs,
    sums,
    mpc,
    mit,
    mi,
    gbc,
    gbi,
    gbh,
    rsc,
    rsi,
    rsh,
    zc,
    zi,
    zh,
    mf,
    mfi,
    hf,
    y_conv,
    y_in,
    feat,
    w_in,
    w_conv,
    labels,
    train,
    m_in,
    w_head,
    f_head,
    s_head,
    w_bias,
    f_bias,
    s_bias,
    w_norm,
    f_norm,
    s_norm,
    loc,
    ga_s,
    ga_r,
    st_s,
    st_r,
    z_s,
    z_r,
    zf_s,
    zf_r,
    rs_s,
    rs_r,
    ag_s,
    ag_r,
):
    f32 = jnp.float32
    bf16 = jnp.bfloat16
    width, graphs, rows = feat.shape
    total = adj.shape[2]
    hidden = w_head.shape[1]
    wide = 2 * hidden
    shard = hidden // groups
    part = shard // 4
    half = rows // 2
    span_in = 16 * ((width + 15) // 16)
    chunk = min(rows, 128)
    chunks = rows // chunk
    g = lax.axis_index("grp")
    me = lax.axis_index("node")
    core = lax.rem(me, 2)
    chip = lax.div(me, 2)
    n_sib, n_x, n_y, n_d = flip(me, 1), flip(me, 2), flip(me, 4), flip(flip(me, 2), 4)
    peers = [n_d, flip(n_d, 1), n_x, n_y, flip(n_x, 1), flip(n_y, 1), n_sib]
    z_peers = [lax.rem(g + d, groups) for d in range(1, groups)]
    z_from = [lax.rem(g + groups - d, groups) for d in range(1, groups)]
    sent = []

    def send(src, dst, s_sem, r_sem, group, node):
        pltpu.make_async_remote_copy(
            src_ref=src,
            dst_ref=dst,
            send_sem=s_sem,
            recv_sem=r_sem,
            device_id=(group, node),
            device_id_type=MESH,
        ).start()

    def drain(sem, view):
        pltpu.make_async_copy(view, view, sem).wait()

    def lanes_of_core(span):
        return pl.ds(pl.multiple_of(core * span, span), span)

    barrier = pltpu.get_barrier_semaphore()
    for node in peers:
        pl.semaphore_signal(barrier, inc=1, device_id=(g, node), device_id_type=MESH)
    for group in z_peers:
        pl.semaphore_signal(barrier, inc=1, device_id=(group, me), device_id_type=MESH)

    far_refs = (
        (feat_far, feat),
        (w_in_far, w_in),
        (w_conv_far, w_conv),
        (labels_far, labels),
        (train_far, train),
        (m_in_far, m_in),
        (w_head_far, w_head),
        (f_head_far, f_head),
        (s_head_far, s_head),
        (w_bias_far, w_bias),
        (f_bias_far, f_bias),
        (s_bias_far, s_bias),
        (w_norm_far, w_norm),
        (f_norm_far, f_norm),
        (s_norm_far, s_norm),
    )
    own_in = [
        pltpu.make_async_copy(far, here, loc.at[graphs + 2 + i])
        for i, (far, here) in enumerate(far_refs)
    ]
    for copy in own_in:
        copy.start()
    own_a = [pltpu.make_async_copy(adj.at[s], av.at[s], loc.at[s]) for s in range(graphs)]
    part_rows = pl.ds(pl.multiple_of(chip * part, part), part)
    core_lanes = lanes_of_core(hidden)
    own_m = [
        pltpu.make_async_copy(m_conv.at[l, part_rows, core_lanes], mpc.at[l, g], loc.at[graphs + l])
        for l in range(2)
    ]
    for copy in own_a + own_m:
        copy.start()

    high_rows = pl.ds(pl.multiple_of(g * shard, shard), shard)
    padh[...] = jnp.zeros_like(padh)
    mit[...] = jnp.zeros_like(mit)
    for copy in own_in[:3]:
        copy.wait()
    for s in range(graphs):
        padh[pl.ds(0, width), :] = feat[:, s, :].astype(f32)
        xg[s, me] = lowered(padh[pl.ds(0, span_in), :])
    mit[high_rows, pl.ds(0, width)] = w_in[...]
    wa[high_rows, pl.ds(0, wide)] = lowered(w_conv[0])
    wa[high_rows, pl.ds(wide, 128)] = lowered(mit[high_rows, :])
    wb[high_rows, :] = lowered(w_conv[1])
    pl.semaphore_wait(barrier, 7 + groups - 1)

    def gather_of(index, ref, by_lane=False):
        low, high = pl.ds(0, half), pl.ds(half, half)

        def go(r, node, block, span=None):
            view = ref.at[block]
            if span is not None:
                view = ref.at[block, :, span] if by_lane else ref.at[block, span]
            send(view, view, ga_s.at[index], ga_r.at[5 * index + r], g, node)

        def arrived(r, blocks):
            drain(ga_r.at[5 * index + r], ref.at[pl.ds(0, blocks)])

        sent.append((ga_s.at[index], ref.at[pl.ds(0, 7)]))

        def own_first():
            go(0, n_x, me, low)
            go(0, n_y, me, high)
            go(3, n_sib, me)

        def own_second():
            go(1, n_x, me, high)
            go(1, n_y, me, low)

        def own():
            own_first()
            own_second()

        def relay():
            arrived(0, 1)
            go(2, n_y, n_x, low)
            go(2, n_x, n_y, high)

        def near():
            arrived(1, 1)
            go(3, n_sib, n_x)
            go(3, n_sib, n_y)

        def far():
            arrived(2, 1)
            go(4, n_sib, n_d)

        def near_ready():
            arrived(3, 3)

        def far_ready():
            arrived(4, 1)

        return own, relay, near, far, near_ready, far_ready, own_first, own_second

    def chip_at(i):
        cx = lax.rem(lax.rem(chip, 2) + lax.rem(i, 2), 2)
        cy = lax.rem(lax.div(chip, 2) + lax.div(i, 2), 2)
        return cx + 2 * cy

    def product(s, ref, out, first, last):
        if first == 0:
            out[...] = jnp.zeros_like(out)

        def body(i, carry):
            c = chip_at(i)
            block = ref[pl.ds(2 * c, 2)].reshape(2 * rows, ref.shape[2])
            left = av[s, :, pl.ds(pl.multiple_of(c * 2 * rows, 2 * rows), 2 * rows)]
            out[...] += dot(left, block)
            return carry

        lax.fori_loop(first, last, body, 0)

    def product_x(s, first, last):
        if first == 0:
            accx[...] = jnp.zeros_like(accx)

        def body(i, carry):
            c = chip_at(i)
            left = av[s, :, pl.ds(pl.multiple_of(c * 2 * rows, 2 * rows), 2 * rows)]
            right = jnp.concatenate([xg[s, 2 * c], xg[s, 2 * c + 1]], 1)
            accx[...] += dot(left, right, NT)
            return carry

        lax.fori_loop(first, last, body, 0)

    def over_rows(body, carry):
        def one(i, value):
            return body(pl.ds(pl.multiple_of(i * chunk, chunk), chunk), value)

        return lax.fori_loop(0, chunks, one, carry)

    def fold(value):
        return jnp.sum(value.reshape(chunk // 8, 8, hidden), 0)

    def plane_send(k, lines):
        side = hidden // 2
        for i, line in enumerate(lines):
            st[k, me, 2 * i : 2 * i + 1, :] = line[:, :side]
            st[k, me, 2 * i + 1 : 2 * i + 2, :] = line[:, side:]
        view = st.at[k, me]
        for node in peers:
            send(view, view, st_s.at[k], st_r.at[k], g, node)
        sent.append((st_s.at[k], st.at[k, pl.ds(0, 7)]))

    def plane_sum(k):
        drain(st_r.at[k], st.at[k, pl.ds(0, 7)])
        value = st[k, 0]
        for i in range(1, 8):
            value = value + st[k, i]
        lines = [jnp.concatenate([value[i : i + 1], value[i + 1 : i + 2]], 1) for i in (0, 2, 4, 6)]
        return jnp.concatenate([*lines, jnp.zeros((4, hidden), f32)], 0)

    z_all = {}

    def z_send(k, view, all_views):
        for group in z_peers:
            send(view, view, z_s.at[k], z_r.at[k], group, me)
        z_all[k] = all_views
        sent.append((z_s.at[k], all_views))

    def z_wait(k):
        drain(z_r.at[k], z_all[k])

    others = pl.ds(0, groups - 1)

    x_g = [gather_of(s, xg.at[s], True) for s in range(2)]
    h_g = [gather_of(2 + s, hg.at[s]) for s in range(2)]
    d_g = [gather_of(4 + s, dg.at[s]) for s in range(2)]

    own_rows = pl.ds(pl.multiple_of(g * shard, shard), shard)
    strip = shard // 2

    def strip_of(group):
        return pl.ds(pl.multiple_of(group * shard + core * strip, strip), strip)

    strips = pl.ds(0, strip * (groups - 1))

    def z_forward(k, ref):
        z_wait(k)
        for group in z_from:
            view = ref.at[strip_of(group)]
            send(view, view, zf_s.at[k], zf_r.at[k], g, n_sib)
        sent.append((zf_s.at[k], ref.at[strips]))

    def z_forwarded(k):
        drain(zf_r.at[k], z_all[k])

    x_g[0][0]()
    z_send(0, wa.at[strip_of(g)], wa.at[strips])
    for copy in own_in[3:]:
        copy.wait()
    mit[high_rows, pl.ds(0, width)] = m_in[...]
    x_g[0][1]()
    x_g[1][0]()
    z_send(1, wb.at[strip_of(g)], wb.at[strips])
    padh[...] = jnp.zeros_like(padh)
    padh[pl.ds(0, classes), pl.ds(0, hidden)] = w_head[...]
    wt_head[...] = lowered(padh[:, :hidden])
    pad[...] = jnp.zeros_like(pad)
    pad[pl.ds(0, 8), pl.ds(0, classes)] = jnp.broadcast_to(w_bias[...], (8, classes))
    bias_col = pad[...].T[:64, :1]
    count_own = jnp.sum(train[...].astype(f32), axis=1, keepdims=True)
    count_own = count_own[0:1] + count_own[1:2]
    x_g[0][2]()
    for copy in own_m:
        copy.wait()
    for copy in own_a:
        copy.wait()

    def forward_act(s, l, k, first, second, w_first, w_second):
        acc[...] = dot(first, w_first, NT) + dot(second, w_second, NT)

        def body(span, carry):
            pre = acc[span, :]
            square = pre * pre
            inner = 0.7978845608028654 * pre * (1.0 + 0.044715 * square)
            t = jnp.tanh(inner)
            value = 0.5 * pre * (1.0 + t)
            act[l, s, span, :] = value
            slope[l, s, span, :] = 0.5 * (1.0 + t) + 0.5 * pre * (1.0 - t * t) * (
                0.7978845608028654 * (1.0 + 3.0 * 0.044715 * square)
            )
            return carry[0] + fold(value), carry[1] + fold(value * value)

        zero = jnp.zeros((8, hidden), f32)
        one, two = over_rows(body, (zero, zero))
        lines = [jnp.sum(one, 0, keepdims=True), jnp.sum(two, 0, keepdims=True)]
        none = jnp.zeros((1, hidden), f32)
        lines.append(jnp.broadcast_to(count_own, (1, hidden)) if k == 0 else none)
        plane_send(k, lines + [none])

    def normalise(s, l, k, out):
        sums_all = plane_sum(k)
        mean = sums_all[0:1] / total
        var = sums_all[1:2] / total - mean * mean
        inv = lax.rsqrt(var + norm_eps)
        ms[l, s, 0:1, :] = inv
        gain, shift = w_norm[l, 0:1, :], w_norm[l, 1:2, :]

        def body(span, carry):
            normed = (act[l, s, span, :] - mean) * inv
            act[l, s, span, :] = normed
            out[span, :] = lowered(normed * gain + shift)
            return carry

        over_rows(body, 0)
        return sums_all

    def layer_zero(s):
        high, rest = split(accx[...])
        axh[s] = high
        w = wa[:, wide : wide + span_in]
        agg[0, s] = lowered(dot(high, w, NT) + dot(rest, w, NT))
        h0[s] = lowered(dot(xg[s, me].T, w, NT))
        forward_act(s, 0, s, h0[s], agg[0, s], wa[:, :hidden], wa[:, hidden:wide])

    def layer_one(s):
        agg[1, s] = lowered(acc[...])
        forward_act(s, 1, 2 + s, hg[s, me], agg[1, s], wb[:, :hidden], wb[:, hidden:])

    def head(s, count):
        value = h2[s]
        logits = dot(wt_head[pl.ds(0, 64), :], value, NT) + bias_col
        at = lax.broadcasted_iota(jnp.int32, (64, rows), 0)
        valid = at < classes
        logits = jnp.where(valid, logits, -1e30)
        shifted = logits - jnp.max(logits, 0, keepdims=True)
        logp = shifted - jnp.log(jnp.sum(jnp.exp(shifted), 0, keepdims=True))
        onehot = jnp.where(at == labels[s : s + 1, :], 1.0, 0.0)
        target = jnp.where(valid, (1.0 - smoothing) * onehot + smoothing / classes, 0.0)
        weights = train[s : s + 1, :].astype(f32)
        node_loss = jnp.sum(target * logp, 0, keepdims=True)
        loss = -jnp.sum(weights * node_loss, axis=1, keepdims=True)
        delta = (weights / count) * (jnp.exp(logp) - target)
        delta_low = lowered(delta)
        value_t = dot(delta_low, value)
        ght[...] = value_t if s == 0 else ght[...] + value_t
        column = dot(jnp.ones((8, rows), bf16), delta_low, NT)
        tall = jnp.concatenate([delta_low.astype(f32), jnp.zeros((64, rows), f32)], 0).T
        dh[s] = lowered(dot(lowered(tall), wt_head[...])).astype(f32)
        return loss, column

    def backward_sums(s, l, k, extra=None):
        def body(span, carry):
            grad = dh[s, span, :]
            return carry[0] + fold(grad), carry[1] + fold(grad * act[l, s, span, :])

        zero = jnp.zeros((8, hidden), f32)
        one, two = over_rows(body, (zero, zero))
        lines = [jnp.sum(one, 0, keepdims=True), jnp.sum(two, 0, keepdims=True)]
        if extra is None:
            lines += [jnp.zeros((1, hidden), f32)] * 2
        else:
            rest = jnp.zeros((1, hidden - 64), f32)
            lines.append(jnp.concatenate([extra[1][0:1], rest], 1))
            lines.append(jnp.broadcast_to(extra[0], (1, hidden)))
        plane_send(k, lines)

    def backward_pre(s, l, k):
        sums_all = plane_sum(k)
        sums[1 - l] = sums_all if s == 0 else sums[1 - l] + sums_all
        gain = w_norm[l, 0:1, :]
        inv = ms[l, s, 0:1, :]
        first = gain * sums_all[0:1] / total
        second = gain * sums_all[1:2] / total

        def body(span, carry):
            grad = dh[s, span, :] * gain - first - act[l, s, span, :] * second
            dp[l, s, span, :] = lowered(grad * inv * slope[l, s, span, :])
            return carry

        over_rows(body, 0)

    def conv_grads(s, l, left, right):
        turned = dp[l, s].T
        one, two = dot(turned, left), dot(turned, right)
        if s == 0:
            gt[l, :, :hidden] = one
            gt[l, :, hidden:] = two
        else:
            gt[l, :, :hidden] += one
            gt[l, :, hidden:] += two
        return turned

    def pieces_send(k, src, dst, where):
        for node in peers:
            send(where(src, node), dst.at[me], rs_s.at[k], rs_r.at[k], g, node)
        sent.append((rs_s.at[k], dst.at[pl.ds(0, 7)]))

    def pieces_sum(k, src, dst, own):
        dst[me] = own
        drain(rs_r.at[k], dst.at[pl.ds(0, 7)])
        value = dst[0].astype(f32)
        for i in range(1, 8):
            value = value + dst[i].astype(f32)
        return value

    def conv_piece(ref, node):
        n_core, n_chip = lax.rem(node, 2), lax.div(node, 2)
        return ref.at[:, n_chip, :, pl.ds(pl.multiple_of(n_core * hidden, hidden), hidden)]

    def in_piece(ref, node):
        return ref.at[node]

    def head_piece(ref, node):
        n_core, n_chip = lax.rem(node, 2), lax.div(node, 2)
        return ref.at[n_chip, :, pl.ds(pl.multiple_of(n_core * (hidden // 2), hidden // 2), hidden // 2)]

    def over_z(k, buf):
        z_wait(k)
        value = buf[0].astype(f32)
        for i in range(1, groups):
            value = value + buf[i].astype(f32)
        return value

    def spread(k, view_of, some):
        view = view_of(me)
        for node in (n_d, n_x, n_y):
            send(view, view, ag_s.at[k], ag_r.at[2 * k], g, node)
        send(view, view, ag_s.at[k], ag_r.at[2 * k + 1], g, n_sib)
        sent.append((ag_s.at[k], some(4)))

    def spread_forward(k, view_of, some):
        drain(ag_r.at[2 * k], some(3))
        for node in (n_x, n_y, n_d):
            view = view_of(node)
            send(view, view, ag_s.at[4 + k], ag_r.at[2 * k + 1], g, n_sib)
        sent.append((ag_s.at[4 + k], some(3)))

    def spread_wait(k, some):
        drain(ag_r.at[2 * k + 1], some(4))

    head_lanes = lanes_of_core(hidden // 2)

    x_g[0][4]()
    product_x(0, 0, 3)
    x_g[0][3]()
    z_forward(0, wa)
    x_g[0][5]()
    product_x(0, 3, 4)
    x_g[1][1]()
    z_forwarded(0)
    layer_zero(0)
    x_g[1][2]()
    x_g[1][4]()
    product_x(1, 0, 3)
    x_g[1][3]()
    x_g[1][5]()
    product_x(1, 3, 4)
    count_plane = normalise(0, 0, 0, hg.at[0, me])
    h_g[0][6]()
    layer_zero(1)
    h_g[0][7]()
    zs[0, g] = count_plane
    z_send(3, zs.at[0, g], zs.at[0, others])
    z_forward(1, wb)
    normalise(1, 0, 1, hg.at[1, me])
    h_g[0][1]()
    h_g[1][0]()
    z_send(6, mpc.at[0, g], mpc.at[0, others])
    z_send(7, mpc.at[1, g], mpc.at[1, others])
    z_send(8, mit.at[own_rows], mit.at[pl.ds(0, shard * (groups - 1))])
    z_forwarded(1)
    wn[...] = wa[:, :wide].T
    h_g[0][2]()
    h_g[0][4]()
    product(0, hg.at[0], acc, 0, 3)
    h_g[0][3]()
    h_g[0][5]()
    product(0, hg.at[0], acc, 3, 4)
    layer_one(0)
    h_g[1][1]()
    z_wait(3)
    count = zs[0, 0]
    for i in range(1, groups):
        count = count + zs[0, i]
    count = count[2:3, 0:1]
    h_g[1][2]()
    normalise(0, 1, 2, h2.at[0])
    loss_row = head(0, count)
    backward_sums(0, 1, 4, loss_row)
    h_g[1][3]()
    h_g[1][4]()
    product(1, hg.at[1], acc, 0, 3)
    h_g[1][5]()
    product(1, hg.at[1], acc, 3, 4)
    layer_one(1)
    backward_pre(0, 1, 4)
    dg[0, me] = lowered(dot(dp[1, 0], wb[:, hidden:]))
    d_g[0][0]()
    dh[0] = dot(dp[1, 0], wb[:, :hidden])
    normalise(1, 1, 3, h2.at[1])
    loss_row = head(1, count)
    backward_sums(1, 1, 5, loss_row)
    d_g[0][1]()
    conv_grads(0, 1, hg[0, me], agg[1, 0])
    backward_pre(1, 1, 5)
    dg[1, me] = lowered(dot(dp[1, 1], wb[:, hidden:]))
    d_g[1][0]()
    d_g[0][2]()
    dh[1] = dot(dp[1, 1], wb[:, :hidden])
    zs[1, g] = sums[0]
    z_send(4, zs.at[1, g], zs.at[1, others])
    d_g[0][4]()
    product(0, dg.at[0], acc, 0, 3)
    d_g[0][3]()
    d_g[0][5]()
    product(0, dg.at[0], acc, 3, 4)
    dh[0] = lowered(dh[0] + acc[...]).astype(f32)
    backward_sums(0, 0, 6)
    d_g[1][1]()
    conv_grads(1, 1, hg[1, me], agg[1, 1])
    gbc[1] = lowered(gt[1]).reshape(groups, 4, part, wide)
    gbh[...] = lowered(ght[...]).reshape(4, 16, hidden)
    pieces_send(0, gbc.at[1], rsc.at[1], conv_piece)
    pieces_send(1, gbh, rsh, head_piece)
    d_g[1][2]()
    backward_pre(0, 0, 6)
    turned = conv_grads(0, 0, h0[0], agg[0, 0])
    q1[...] = dot(turned, xg[0, me], NT)
    q2[...] = dot(turned, axh[0])
    d_g[1][4]()
    product(1, dg.at[1], acc, 0, 3)
    d_g[1][3]()
    d_g[1][5]()
    product(1, dg.at[1], acc, 3, 4)
    dh[1] = lowered(dh[1] + acc[...]).astype(f32)
    backward_sums(1, 0, 7)
    zc[1, g] = lowered(pieces_sum(0, None, rsc.at[1], conv_piece(gbc.at[1], me)[...]))
    z_send(9, zc.at[1, g], zc.at[1, others])
    zh[g] = lowered(pieces_sum(1, None, rsh, head_piece(gbh, me)[...]))
    z_send(10, zh.at[g], zh.at[others])
    z_wait(6)
    z_wait(7)
    z_wait(8)
    tall_in[...] = mit[...]
    mi[...] = tall_in[...].T.reshape(8, 16, hidden)
    tall_in[...] = jnp.zeros_like(tall_in)
    backward_pre(1, 0, 7)
    turned = conv_grads(1, 0, h0[1], agg[0, 1])
    gbc[0] = lowered(gt[0]).reshape(groups, 4, part, wide)
    pieces_send(2, gbc.at[0], rsc.at[0], conv_piece)
    q1[...] += dot(turned, xg[1, me], NT)
    q2[...] += dot(turned, axh[1])
    one, two = split(q1[...]), split(q2[...])
    w_self, w_near = wn[:hidden, :], wn[hidden:, :]
    g_in = dot(w_self, one[0]) + dot(w_self, one[1]) + dot(w_near, two[0]) + dot(w_near, two[1])
    tall_in[:, pl.ds(0, span_in)] = g_in
    gbi[...] = lowered(tall_in[...].T).reshape(8, 16, hidden)
    pieces_send(3, gbi, rsi, in_piece)
    zs[2, g] = sums[1]
    z_send(5, zs.at[2, g], zs.at[2, others])

    def conv_view(l):
        return lambda node: conv_piece(mf.at[l], node)

    def conv_some(l):
        return lambda n: mf.at[l, :, pl.ds(0, n), :, pl.ds(0, hidden)]

    def head_some(n):
        return hf.at[pl.ds(0, n), :, pl.ds(0, hidden // 2)]

    def in_some(n):
        return mfi.at[pl.ds(0, n)]

    def head_view(node):
        return head_piece(hf, node)

    def in_view(node):
        return mfi.at[node]

    def scaled(value):
        norm = jnp.sqrt(jnp.sum(jnp.sum(value * value, 0, keepdims=True), 1, keepdims=True))
        return value / (norm + 1e-07)

    def iterate(refs, first, last):
        for i in range(first, last):
            for ref in refs:
                value = ref[...]
                pair = split(value)
                gram = dot_three(pair, pair, NT)
                gram_high, gram_rest = split(gram)
                cross = dot(gram_high, gram_rest)
                square = dot(gram_high, gram_high) + cross + cross.T
                poly = split(poly_second * gram + poly_third * square)
                ref[...] = poly_first * value + dot_three(poly, pair)

    factor_conv = 0.2 * float(wide) ** 0.5
    factor_in = 0.2 * float(max(width, hidden)) ** 0.5

    def conv_out(l):
        o_conv_m[l] = mf[l, g].reshape(shard, wide)
        ortho = y_conv[l, own_rows, :]
        weight = w_conv[l]
        o_conv[l] = weight - muon_rate * (factor_conv * ortho + decay_rate * weight)

    mf[1, :, chip, :, core_lanes] = muon_beta * mpc[1] + over_z(9, zc.at[1])
    spread(0, conv_view(1), conv_some(1))
    hf[chip, :, head_lanes] = over_z(10, zh)
    spread(1, head_view, head_some)
    zc[0, g] = lowered(pieces_sum(2, None, rsc.at[0], conv_piece(gbc.at[0], me)[...]))
    z_send(11, zc.at[0, g], zc.at[0, others])
    zi[g] = lowered(pieces_sum(3, None, rsi, gbi[me]))
    z_send(12, zi.at[g], zi.at[others])
    spread_forward(0, conv_view(1), conv_some(1))
    spread_forward(1, head_view, head_some)
    spread_wait(0, conv_some(1))
    y_conv[1] = scaled(mf[1].reshape(hidden, wide))
    iterate([y_conv.at[1]], 0, EARLY_STEPS)
    mf[0, :, chip, :, core_lanes] = muon_beta * mpc[0] + over_z(11, zc.at[0])
    spread(2, conv_view(0), conv_some(0))
    mfi[me] = muon_beta * mi[me] + over_z(12, zi)
    spread(3, in_view, in_some)
    iterate([y_conv.at[1]], EARLY_STEPS, NS_STEPS)
    spread_forward(2, conv_view(0), conv_some(0))
    spread_forward(3, in_view, in_some)
    conv_out(1)

    spread_wait(1, head_some)
    grad = hf[...].reshape(64, hidden)[:classes]
    o_head[...], o_head_f[...], o_head_s[...] = adamw(w_head[...], grad, f_head[...], s_head[...])
    z_wait(4)
    z_wait(5)
    late = zs[1, 0]
    early = zs[2, 0]
    for i in range(1, groups):
        late = late + zs[1, i]
        early = early + zs[2, i]
    for l, rows_l in ((0, early), (1, late)):
        grad = jnp.concatenate([rows_l[1:2], rows_l[0:1]], 0)
        o_norm[l], o_norm_f[l], o_norm_s[l] = adamw(w_norm[l], grad, f_norm[l], s_norm[l])
    o_bias[...], o_bias_f[...], o_bias_s[...] = adamw(
        w_bias[...], late[2:3, :classes], f_bias[...], s_bias[...]
    )
    o_loss[...] = jnp.concatenate([late[3:4, 0:1], count], 1)

    spread_wait(2, conv_some(0))
    spread_wait(3, in_some)
    y_conv[0] = scaled(mf[0].reshape(hidden, wide))
    y_in[...] = scaled(mfi[...].reshape(128, hidden))
    iterate([y_conv.at[0], y_in], 0, NS_STEPS)
    conv_out(0)
    tall_in[...] = mfi[...].reshape(128, hidden).T
    o_in_m[...] = tall_in[own_rows, :][:, :width]
    tall_in[...] = y_in[...].T
    ortho = tall_in[own_rows, :][:, :width]
    weight = w_in[...]
    o_in[...] = weight - muon_rate * (factor_in * ortho + decay_rate * weight)
    for sem, view in sent:
        drain(sem, view)


def planned(mesh):
    groups = mesh.shape["grp"]

    def call(
        features,
        adjacency,
        labels,
        train_mask,
        input_weight,
        input_moment,
        conv_weight,
        conv_moment,
        head_weight,
        head_first,
        head_second,
        head_bias,
        bias_first,
        bias_second,
        norm_params,
        norm_first,
        norm_second,
    ):
        f32, bf16 = jnp.float32, jnp.bfloat16
        graphs, rows, width = features.shape
        total = adjacency.shape[2]
        hidden, classes = head_weight.shape
        wide = 2 * hidden
        shard = hidden // groups
        part = shard // 4
        span_in = 16 * ((width + 15) // 16)
        vm = pltpu.VMEM
        sem = pltpu.SemaphoreType.DMA
        shape = jax.ShapeDtypeStruct
        near = pl.BlockSpec(memory_space=pltpu.VMEM)
        anywhere = pl.BlockSpec(memory_space=pl.ANY)
        results = [
            shape((1, 2), f32),
            shape((shard, width), f32),
            shape((shard, width), f32),
            shape((2, shard, wide), f32),
            shape((2, shard, wide), f32),
            shape((classes, hidden), f32),
            shape((classes, hidden), f32),
            shape((classes, hidden), f32),
            shape((1, classes), f32),
            shape((1, classes), f32),
            shape((1, classes), f32),
            shape(norm_params.shape, f32),
            shape(norm_params.shape, f32),
            shape(norm_params.shape, f32),
        ]
        outs = pl.pallas_call(
            functools.partial(step_kernel, groups, classes),
            out_shape=results,
            in_specs=[anywhere] * 17,
            out_specs=[near] * 14,
            scratch_shapes=[
                vm((graphs, rows, total), bf16),
                vm((graphs, 8, span_in, rows), bf16),
                vm((graphs, 8, rows, hidden), bf16),
                vm((graphs, 8, rows, hidden), bf16),
                vm((128, 128), f32),
                vm((128, rows), f32),
                vm((hidden, wide + 128), bf16),
                vm((hidden, wide), bf16),
                vm((wide, hidden), bf16),
                vm((128, hidden), bf16),
                vm((graphs, rows, hidden), bf16),
                vm((2, graphs, rows, hidden), bf16),
                vm((2, graphs, rows, hidden), f32),
                vm((2, graphs, rows, hidden), f32),
                vm((2, graphs, 8, hidden), f32),
                vm((graphs, rows, span_in), bf16),
                vm((rows, span_in), f32),
                vm((rows, hidden), f32),
                vm((graphs, rows, hidden), bf16),
                vm((graphs, rows, hidden), f32),
                vm((2, graphs, rows, hidden), bf16),
                vm((2, hidden, wide), f32),
                vm((hidden, span_in), f32),
                vm((hidden, span_in), f32),
                vm((hidden, 128), f32),
                vm((64, hidden), f32),
                vm((ROUNDS, 8, 8, hidden // 2), f32),
                vm((3, groups, 8, hidden), f32),
                vm((2, 8, hidden), f32),
                vm((2, groups, part, hidden), f32),
                vm((hidden, 128), f32),
                vm((8, 16, hidden), f32),
                vm((2, groups, 4, part, wide), bf16),
                vm((8, 16, hidden), bf16),
                vm((4, 16, hidden), bf16),
                vm((2, 8, groups, part, hidden), bf16),
                vm((8, 16, hidden), bf16),
                vm((8, 16, hidden // 2), bf16),
                vm((2, groups, groups, part, hidden), bf16),
                vm((groups, 16, hidden), bf16),
                vm((groups, 16, hidden // 2), bf16),
                vm((2, groups, 4, part, wide), f32),
                vm((8, 16, hidden), f32),
                vm((4, 16, hidden), f32),
                vm((2, hidden, wide), f32),
                vm((128, hidden), f32),
                vm((width, graphs, rows), bf16),
                vm((shard, width), f32),
                vm((2, shard, wide), f32),
                vm((graphs, rows), jnp.int32),
                vm((graphs, rows), jnp.int32),
                vm((shard, width), f32),
                vm((classes, hidden), f32),
                vm((classes, hidden), f32),
                vm((classes, hidden), f32),
                vm((1, classes), f32),
                vm((1, classes), f32),
                vm((1, classes), f32),
                vm(norm_params.shape, f32),
                vm(norm_params.shape, f32),
                vm(norm_params.shape, f32),
                sem((graphs + 17,)),
                sem((6,)),
                sem((30,)),
                sem((ROUNDS,)),
                sem((ROUNDS,)),
                sem((13,)),
                sem((13,)),
                sem((2,)),
                sem((2,)),
                sem((4,)),
                sem((4,)),
                sem((8,)),
                sem((8,)),
            ],
            compiler_params=pltpu.CompilerParams(
                collective_id=0, has_side_effects=True, vmem_limit_bytes=VMEM_BYTES
            ),
            name="train_step",
        )(
            jnp.transpose(features, (2, 0, 1)),
            adjacency,
            labels,
            train_mask,
            input_weight.T,
            input_moment.T,
            jnp.swapaxes(conv_weight, 1, 2),
            jnp.swapaxes(conv_moment, 1, 2),
            head_weight.T,
            head_first.T,
            head_second.T,
            head_bias[None, :],
            bias_first[None, :],
            bias_second[None, :],
            norm_params,
            norm_first,
            norm_second,
        )
        outs = pl.pallas_call(
            hand_over,
            out_shape=results,
            in_specs=[near] * 14,
            out_specs=[near] * 14,
            name="hand_over",
        )(*outs)
        loss, in_new, in_m, conv_new, conv_m, h_new, h_f, h_s, b_new, b_f, b_s, *norms = outs
        return (
            loss[0],
            in_new.T,
            in_m.T,
            jnp.swapaxes(conv_new, 1, 2),
            jnp.swapaxes(conv_m, 1, 2),
            h_new.T,
            h_f.T,
            h_s.T,
            b_new[0],
            b_f[0],
            b_s[0],
            *norms,
        )

    return call


def hand_over(*refs):
    for source, target in zip(refs[:14], refs[14:]):
        target[...] = source[...]


def solution(mesh):
    placed = (
        P("grp", "node", None),
        P("grp", "node", None),
        P("grp", "node"),
        P("grp", "node"),
        P(None, "grp"),
        P(None, "grp"),
        P(None, None, "grp"),
        P(None, None, "grp"),
        P(),
        P(),
        P(),
        P(),
        P(),
        P(),
        P(),
        P(),
        P(),
    )
    small = mesh.shape["node"] == 8 and mesh.shape["grp"] == 4
    return jax.shard_map(
        planned(mesh) if small else per_device,
        mesh=mesh,
        in_specs=placed,
        out_specs=(
            P(),
            P(None, "grp"),
            P(None, "grp"),
            P(None, None, "grp"),
            P(None, None, "grp"),
            P(),
            P(),
            P(),
            P(),
            P(),
            P(),
            P(),
            P(),
            P(),
        ),
        check_vma=False,
    )
```

```python
import functools

import jax
import jax.numpy as jnp
from jax import lax
from jax.experimental import pallas as pl
from jax.experimental.pallas import tpu as pltpu
from jax.sharding import PartitionSpec as P

NS_STEPS = 5
STEP = 10


norm_eps = 1e-05
smoothing = 0.1
poly_first = 3.4445
poly_second = -4.775
poly_third = 2.0315
muon_beta = 0.95
muon_rate = 0.2
decay_rate = 0.01
adam_rate = 0.05
beta_first = 0.9
beta_second = 0.95
adam_eps = 1e-08


def lowered(value):
    return value.astype(jnp.bfloat16)


def matmul_hi(left, right):
    return jnp.dot(left, right, precision=lax.Precision.HIGHEST)


def column_dot(left, right):
    return lax.dot_general(
        left, right, (((0,), (0,)), ((), ())), preferred_element_type=jnp.float32
    )


def row_dot(left, right):
    return lax.dot_general(
        left, right, (((1,), (1,)), ((), ())), preferred_element_type=jnp.float32
    )


def neighbour_sum(adj, values):
    return jnp.dot(
        adj, lax.all_gather(values, "node", axis=0, tiled=True), preferred_element_type=jnp.float32
    )


def neighbour_back(adj, grads):
    return lax.psum_scatter(column_dot(adj, grads), "node", scatter_dimension=0, tiled=True)


def layer_forward(adj, inputs_low, weight_low, gain, shift, total_rows):
    hidden = weight_low.shape[1]
    agg_low = lowered(neighbour_sum(adj, inputs_low))
    pre = jnp.dot(inputs_low, weight_low[:hidden], preferred_element_type=jnp.float32)
    pre = pre + jnp.dot(agg_low, weight_low[hidden:], preferred_element_type=jnp.float32)
    act = jax.nn.gelu(pre)
    sums, squares = lax.psum((jnp.sum(act, 0), jnp.sum(act * act, 0)), "node")
    mean = sums / total_rows
    var = squares / total_rows - mean * mean
    inv_std = lax.rsqrt(var + norm_eps)
    normed = (act - mean) * inv_std
    return (normed * gain + shift, (inputs_low, agg_low, pre, normed, inv_std))


def layer_backward(adj, weight_low, gain, kept, grad_out, total_rows):
    inputs_low, agg_low, pre, normed, inv_std = kept
    hidden = weight_low.shape[1]
    grad_gain = jnp.sum(grad_out * normed, 0)
    grad_shift = jnp.sum(grad_out, 0)
    grad_normed = grad_out * gain
    first, second = lax.psum((jnp.sum(grad_normed, 0), jnp.sum(grad_normed * normed, 0)), "node")
    grad_act = (grad_normed - first / total_rows - normed * (second / total_rows)) * inv_std
    grad_pre = jax.vjp(jax.nn.gelu, pre)[1](grad_act)[0]
    pre_low = lowered(grad_pre)
    grad_weight = jnp.concatenate(
        [column_dot(inputs_low, pre_low), column_dot(agg_low, pre_low)], 0
    )
    grad_agg = lowered(row_dot(pre_low, weight_low[hidden:]))
    grad_inputs = row_dot(pre_low, weight_low[:hidden]) + neighbour_back(adj, grad_agg)
    return (grad_inputs, grad_weight, jnp.stack([grad_gain, grad_shift]))


def gram_of(block):
    return matmul_hi(block, block.T)


def orthogonal_blocks(first_block, second_block, third_block):
    blocks = [first_block, second_block, third_block]
    for step in range(NS_STEPS):
        grams = lax.psum((gram_of(blocks[0]), gram_of(blocks[1]), gram_of(blocks[2])), "grp")
        grams = list(grams)
        if step == 0:
            scales = [jnp.sqrt(jnp.trace(gram)) + 1e-07 for gram in grams]
            blocks = [block / scale for block, scale in zip(blocks, scales)]
            grams = [gram / (scale * scale) for gram, scale in zip(grams, scales)]
        polys = [poly_second * gram + poly_third * matmul_hi(gram, gram) for gram in grams]
        blocks = [poly_first * block + matmul_hi(poly, block) for block, poly in zip(blocks, polys)]
    return blocks


def adamw(weight, grad, first, second):
    first_new = beta_first * first + (1.0 - beta_first) * grad
    second_new = beta_second * second + (1.0 - beta_second) * grad * grad
    fixed_first = first_new / (1.0 - beta_first**STEP)
    fixed_second = second_new / (1.0 - beta_second**STEP)
    update = fixed_first / (jnp.sqrt(fixed_second) + adam_eps) + decay_rate * weight
    return (weight - adam_rate * update, first_new, second_new)


def per_device(
    features,
    adjacency,
    labels,
    train_mask,
    input_weight,
    input_moment,
    conv_weight,
    conv_moment,
    head_weight,
    head_first,
    head_second,
    head_bias,
    bias_first,
    bias_second,
    norm_params,
    norm_first,
    norm_second,
):
    layers = conv_weight.shape[0]
    hidden = head_weight.shape[0]
    classes = head_weight.shape[1]
    f_width = input_weight.shape[0]
    total_rows = features.shape[1] * lax.axis_size("node")
    input_full, conv_full = (
        lax.all_gather(lowered(input_weight), "grp", axis=1, tiled=True),
        lax.all_gather(lowered(conv_weight), "grp", axis=2, tiled=True),
    )
    head_low = lowered(head_weight)
    count = lax.psum(jnp.sum(train_mask).astype(jnp.float32), ("grp", "node"))
    grad_input = jnp.zeros((f_width, hidden), jnp.float32)
    grad_conv = [jnp.zeros((2 * hidden, hidden), jnp.float32) for layer in range(layers)]
    grad_norm = [jnp.zeros((2, hidden), jnp.float32) for layer in range(layers)]
    grad_head = jnp.zeros((hidden, classes), jnp.float32)
    grad_bias = jnp.zeros((classes,), jnp.float32)
    loss_sum = jnp.float32(0.0)
    for graph in range(features.shape[0]):
        inputs = features[graph]
        adj = adjacency[graph]
        current_low = lowered(jnp.dot(inputs, input_full, preferred_element_type=jnp.float32))
        kept_list = []
        for layer in range(layers):
            output, kept = layer_forward(
                adj,
                current_low,
                conv_full[layer],
                norm_params[layer, 0],
                norm_params[layer, 1],
                total_rows,
            )
            kept_list.append(kept)
            current_low = lowered(output)
        logits = jnp.dot(current_low, head_low, preferred_element_type=jnp.float32) + head_bias
        logp = jax.nn.log_softmax(logits, -1)
        onehot = (labels[graph][:, None] == jnp.arange(classes, dtype=jnp.int32)[None, :]).astype(
            jnp.float32
        )
        target = (1.0 - smoothing) * onehot + smoothing / classes
        weights = train_mask[graph].astype(jnp.float32)
        loss_sum = loss_sum - jnp.sum(weights * jnp.sum(target * logp, -1))
        logits_low = lowered((weights / count)[:, None] * (jnp.exp(logp) - target))
        grad_head = grad_head + column_dot(current_low, logits_low)
        grad_bias = grad_bias + jnp.sum(logits_low.astype(jnp.float32), 0)
        grad_low = lowered(row_dot(logits_low, head_low))
        for layer in reversed(range(layers)):
            grad_inputs, grad_weight, grad_pair = layer_backward(
                adj,
                conv_full[layer],
                norm_params[layer, 0],
                kept_list[layer],
                grad_low.astype(jnp.float32),
                total_rows,
            )
            grad_conv[layer] = grad_conv[layer] + grad_weight
            grad_norm[layer] = grad_norm[layer] + grad_pair
            grad_low = lowered(grad_inputs)
        grad_input = grad_input + column_dot(inputs, grad_low)
    grad_conv_all = jnp.stack(grad_conv)
    grad_norm_all = jnp.stack(grad_norm)
    grad_input, grad_conv_all, grad_head, grad_bias, grad_norm_all, loss_sum = lax.psum(
        (grad_input, grad_conv_all, grad_head, grad_bias, grad_norm_all, loss_sum), "node"
    )
    grad_input, grad_conv_all = (
        lax.psum_scatter(grad_input, "grp", scatter_dimension=1, tiled=True),
        lax.psum_scatter(grad_conv_all, "grp", scatter_dimension=2, tiled=True),
    )
    grad_head, grad_bias, grad_norm_all, loss_sum = lax.psum(
        (grad_head, grad_bias, grad_norm_all, loss_sum), "grp"
    )
    moment_in = muon_beta * input_moment + grad_input
    moment_conv = muon_beta * conv_moment + grad_conv_all
    ortho_in, ortho_first, ortho_second = orthogonal_blocks(
        moment_in, moment_conv[0], moment_conv[1]
    )
    factor_in = 0.2 * float(max(f_width, hidden)) ** 0.5
    factor_conv = 0.2 * float(2 * hidden) ** 0.5
    input_new = input_weight - muon_rate * (factor_in * ortho_in + decay_rate * input_weight)
    ortho_conv = jnp.stack([ortho_first, ortho_second])
    conv_new = conv_weight - muon_rate * (factor_conv * ortho_conv + decay_rate * conv_weight)
    head_new, head_first_new, head_second_new = adamw(
        head_weight, grad_head, head_first, head_second
    )
    bias_new, bias_first_new, bias_second_new = adamw(head_bias, grad_bias, bias_first, bias_second)
    norm_new, norm_first_new, norm_second_new = adamw(
        norm_params, grad_norm_all, norm_first, norm_second
    )
    loss_parts = jnp.stack([loss_sum, count])
    return (
        loss_parts,
        input_new,
        moment_in,
        conv_new,
        moment_conv,
        head_new,
        head_first_new,
        head_second_new,
        bias_new,
        bias_first_new,
        bias_second_new,
        norm_new,
        norm_first_new,
        norm_second_new,
    )

MESH = pl.DeviceIdType.MESH
NT = (((1,), (1,)), ((), ()))
NN = (((1,), (0,)), ((), ()))
VMEM_BYTES = 56 * 1024 * 1024
ROUNDS = 8
EARLY_STEPS = 0


def flip(index, bit):
    return index + bit - 2 * bit * lax.rem(lax.div(index, bit), 2)


def dot(left, right, dims=NN):
    return lax.dot_general(left, right, dims, preferred_element_type=jnp.float32)


def split(value):
    high = lowered(value)
    return high, lowered(value - high.astype(jnp.float32))


def dot_three(left, right, dims=NN):
    left_high, left_rest = left
    right_high, right_rest = right
    axis = dims[0][1][0]
    return dot(
        jnp.concatenate([left_high, left_high, left_rest], 1),
        jnp.concatenate([right_high, right_rest, right_high], axis),
        dims,
    )


def step_kernel(
    groups,
    classes,
    feat_far,
    adj,
    labels_far,
    train_far,
    w_in_far,
    m_in_far,
    w_conv_far,
    m_conv,
    w_head_far,
    f_head_far,
    s_head_far,
    w_bias_far,
    f_bias_far,
    s_bias_far,
    w_norm_far,
    f_norm_far,
    s_norm_far,
    o_loss,
    o_in,
    o_in_m,
    o_conv,
    o_conv_m,
    o_head,
    o_head_f,
    o_head_s,
    o_bias,
    o_bias_f,
    o_bias_s,
    o_norm,
    o_norm_f,
    o_norm_s,
    av,
    xg,
    hg,
    dg,
    pad,
    padh,
    wa,
    wb,
    wn,
    wt_head,
    h0,
    agg,
    act,
    slope,
    ms,
    axh,
    accx,
    acc,
    h2,
    dh,
    dp,
    gt,
    q1,
    q2,
    tall_in,
    ght,
    st,
    zs,
    sums,
    mpc,
    mit,
    mi,
    gbc,
    gbi,
    gbh,
    rsc,
    rsi,
    rsh,
    zc,
    zi,
    zh,
    mf,
    mfi,
    hf,
    y_conv,
    y_in,
    feat,
    w_in,
    w_conv,
    labels,
    train,
    m_in,
    w_head,
    f_head,
    s_head,
    w_bias,
    f_bias,
    s_bias,
    w_norm,
    f_norm,
    s_norm,
    loc,
    ga_s,
    ga_r,
    st_s,
    st_r,
    z_s,
    z_r,
    zf_s,
    zf_r,
    rs_s,
    rs_r,
    ag_s,
    ag_r,
):
    f32 = jnp.float32
    bf16 = jnp.bfloat16
    width, graphs, rows = feat.shape
    total = adj.shape[2]
    hidden = w_head.shape[1]
    wide = 2 * hidden
    shard = hidden // groups
    part = shard // 4
    half = rows // 2
    span_in = 16 * ((width + 15) // 16)
    chunk = min(rows, 512)
    chunks = rows // chunk
    g = lax.axis_index("grp")
    me = lax.axis_index("node")
    core = lax.rem(me, 2)
    chip = lax.div(me, 2)
    n_sib, n_x, n_y, n_d = flip(me, 1), flip(me, 2), flip(me, 4), flip(flip(me, 2), 4)
    peers = [n_d, flip(n_d, 1), n_x, n_y, flip(n_x, 1), flip(n_y, 1), n_sib]
    z_peers = [lax.rem(g + d, groups) for d in range(1, groups)]
    z_from = [lax.rem(g + groups - d, groups) for d in range(1, groups)]
    sent = []

    def send(src, dst, s_sem, r_sem, group, node):
        pltpu.make_async_remote_copy(
            src_ref=src,
            dst_ref=dst,
            send_sem=s_sem,
            recv_sem=r_sem,
            device_id=(group, node),
            device_id_type=MESH,
        ).start()

    def drain(sem, view):
        pltpu.make_async_copy(view, view, sem).wait()

    def lanes_of_core(span):
        return pl.ds(pl.multiple_of(core * span, span), span)

    barrier = pltpu.get_barrier_semaphore()
    for node in peers:
        pl.semaphore_signal(barrier, inc=1, device_id=(g, node), device_id_type=MESH)
    for group in z_peers:
        pl.semaphore_signal(barrier, inc=1, device_id=(group, me), device_id_type=MESH)

    far_refs = (
        (feat_far, feat),
        (w_in_far, w_in),
        (w_conv_far, w_conv),
        (labels_far, labels),
        (train_far, train),
        (m_in_far, m_in),
        (w_head_far, w_head),
        (f_head_far, f_head),
        (s_head_far, s_head),
        (w_bias_far, w_bias),
        (f_bias_far, f_bias),
        (s_bias_far, s_bias),
        (w_norm_far, w_norm),
        (f_norm_far, f_norm),
        (s_norm_far, s_norm),
    )
    own_in = [
        pltpu.make_async_copy(far, here, loc.at[graphs + 2 + i])
        for i, (far, here) in enumerate(far_refs)
    ]
    for copy in own_in:
        copy.start()
    own_a = [pltpu.make_async_copy(adj.at[s], av.at[s], loc.at[s]) for s in range(graphs)]
    part_rows = pl.ds(pl.multiple_of(chip * part, part), part)
    core_lanes = lanes_of_core(hidden)
    own_m = [
        pltpu.make_async_copy(m_conv.at[l, part_rows, core_lanes], mpc.at[l, g], loc.at[graphs + l])
        for l in range(2)
    ]
    for copy in own_a + own_m:
        copy.start()

    high_rows = pl.ds(pl.multiple_of(g * shard, shard), shard)
    padh[...] = jnp.zeros_like(padh)
    mit[...] = jnp.zeros_like(mit)
    for copy in own_in[:3]:
        copy.wait()
    for s in range(graphs):
        padh[pl.ds(0, width), :] = feat[:, s, :].astype(f32)
        xg[s, me] = lowered(padh[pl.ds(0, span_in), :])
    mit[high_rows, pl.ds(0, width)] = w_in[...]
    wa[high_rows, pl.ds(0, wide)] = lowered(w_conv[0])
    wa[high_rows, pl.ds(wide, 128)] = lowered(mit[high_rows, :])
    wb[high_rows, :] = lowered(w_conv[1])
    pl.semaphore_wait(barrier, 7 + groups - 1)

    def gather_of(index, ref, by_lane=False):
        low, high = pl.ds(0, half), pl.ds(half, half)

        def go(r, node, block, span=None):
            view = ref.at[block]
            if span is not None:
                view = ref.at[block, :, span] if by_lane else ref.at[block, span]
            send(view, view, ga_s.at[index], ga_r.at[5 * index + r], g, node)

        def arrived(r, blocks):
            drain(ga_r.at[5 * index + r], ref.at[pl.ds(0, blocks)])

        sent.append((ga_s.at[index], ref.at[pl.ds(0, 7)]))

        def own_first():
            go(0, n_x, me, low)
            go(0, n_y, me, high)
            go(3, n_sib, me)

        def own_second():
            go(1, n_x, me, high)
            go(1, n_y, me, low)

        def own():
            own_first()
            own_second()

        def relay():
            arrived(0, 1)
            go(2, n_y, n_x, low)
            go(2, n_x, n_y, high)

        def near():
            arrived(1, 1)
            go(3, n_sib, n_x)
            go(3, n_sib, n_y)

        def far():
            arrived(2, 1)
            go(4, n_sib, n_d)

        def near_ready():
            arrived(3, 3)

        def far_ready():
            arrived(4, 1)

        return own, relay, near, far, near_ready, far_ready, own_first, own_second

    def chip_at(i):
        cx = lax.rem(lax.rem(chip, 2) + lax.rem(i, 2), 2)
        cy = lax.rem(lax.div(chip, 2) + lax.div(i, 2), 2)
        return cx + 2 * cy

    def product(s, ref, out, first, last):
        if first == 0:
            out[...] = jnp.zeros_like(out)

        def body(i, carry):
            c = chip_at(i)
            block = ref[pl.ds(2 * c, 2)].reshape(2 * rows, ref.shape[2])
            left = av[s, :, pl.ds(pl.multiple_of(c * 2 * rows, 2 * rows), 2 * rows)]
            out[...] += dot(left, block)
            return carry

        lax.fori_loop(first, last, body, 0)

    def product_x(s, first, last):
        if first == 0:
            accx[...] = jnp.zeros_like(accx)

        def body(i, carry):
            c = chip_at(i)
            left = av[s, :, pl.ds(pl.multiple_of(c * 2 * rows, 2 * rows), 2 * rows)]
            right = jnp.concatenate([xg[s, 2 * c], xg[s, 2 * c + 1]], 1)
            accx[...] += dot(left, right, NT)
            return carry

        lax.fori_loop(first, last, body, 0)

    def over_rows(body, carry):
        def one(i, value):
            return body(pl.ds(pl.multiple_of(i * chunk, chunk), chunk), value)

        return lax.fori_loop(0, chunks, one, carry)

    def fold(value):
        return jnp.sum(value.reshape(chunk // 8, 8, hidden), 0)

    def plane_send(k, lines):
        side = hidden // 2
        for i, line in enumerate(lines):
            st[k, me, 2 * i : 2 * i + 1, :] = line[:, :side]
            st[k, me, 2 * i + 1 : 2 * i + 2, :] = line[:, side:]
        view = st.at[k, me]
        for node in peers:
            send(view, view, st_s.at[k], st_r.at[k], g, node)
        sent.append((st_s.at[k], st.at[k, pl.ds(0, 7)]))

    def plane_sum(k):
        drain(st_r.at[k], st.at[k, pl.ds(0, 7)])
        value = st[k, 0]
        for i in range(1, 8):
            value = value + st[k, i]
        lines = [jnp.concatenate([value[i : i + 1], value[i + 1 : i + 2]], 1) for i in (0, 2, 4, 6)]
        return jnp.concatenate([*lines, jnp.zeros((4, hidden), f32)], 0)

    z_all = {}

    def z_send(k, view, all_views):
        for group in z_peers:
            send(view, view, z_s.at[k], z_r.at[k], group, me)
        z_all[k] = all_views
        sent.append((z_s.at[k], all_views))

    def z_wait(k):
        drain(z_r.at[k], z_all[k])

    others = pl.ds(0, groups - 1)

    x_g = [gather_of(s, xg.at[s], True) for s in range(2)]
    h_g = [gather_of(2 + s, hg.at[s]) for s in range(2)]
    d_g = [gather_of(4 + s, dg.at[s]) for s in range(2)]

    own_rows = pl.ds(pl.multiple_of(g * shard, shard), shard)
    strip = shard // 2

    def strip_of(group):
        return pl.ds(pl.multiple_of(group * shard + core * strip, strip), strip)

    strips = pl.ds(0, strip * (groups - 1))

    def z_forward(k, ref):
        z_wait(k)
        for group in z_from:
            view = ref.at[strip_of(group)]
            send(view, view, zf_s.at[k], zf_r.at[k], g, n_sib)
        sent.append((zf_s.at[k], ref.at[strips]))

    def z_forwarded(k):
        drain(zf_r.at[k], z_all[k])

    x_g[0][0]()
    z_send(0, wa.at[strip_of(g)], wa.at[strips])
    for copy in own_in[3:]:
        copy.wait()
    mit[high_rows, pl.ds(0, width)] = m_in[...]
    x_g[0][1]()
    x_g[1][0]()
    z_send(1, wb.at[strip_of(g)], wb.at[strips])
    padh[...] = jnp.zeros_like(padh)
    padh[pl.ds(0, classes), pl.ds(0, hidden)] = w_head[...]
    wt_head[...] = lowered(padh[:, :hidden])
    pad[...] = jnp.zeros_like(pad)
    pad[pl.ds(0, 8), pl.ds(0, classes)] = jnp.broadcast_to(w_bias[...], (8, classes))
    bias_col = pad[...].T[:64, :1]
    count_own = jnp.sum(train[...].astype(f32), axis=1, keepdims=True)
    count_own = count_own[0:1] + count_own[1:2]
    x_g[0][2]()
    for copy in own_m:
        copy.wait()
    for copy in own_a:
        copy.wait()

    def forward_act(s, l, k, first, second, w_first, w_second):
        acc[...] = dot(first, w_first, NT) + dot(second, w_second, NT)

        def body(span, carry):
            pre = acc[span, :]
            square = pre * pre
            inner = 0.7978845608028654 * pre * (1.0 + 0.044715 * square)
            t = jnp.tanh(inner)
            value = 0.5 * pre * (1.0 + t)
            act[l, s, span, :] = value
            slope[l, s, span, :] = 0.5 * (1.0 + t) + 0.5 * pre * (1.0 - t * t) * (
                0.7978845608028654 * (1.0 + 3.0 * 0.044715 * square)
            )
            return carry[0] + fold(value), carry[1] + fold(value * value)

        zero = jnp.zeros((8, hidden), f32)
        one, two = over_rows(body, (zero, zero))
        lines = [jnp.sum(one, 0, keepdims=True), jnp.sum(two, 0, keepdims=True)]
        none = jnp.zeros((1, hidden), f32)
        lines.append(jnp.broadcast_to(count_own, (1, hidden)) if k == 0 else none)
        plane_send(k, lines + [none])

    def normalise(s, l, k, out):
        sums_all = plane_sum(k)
        mean = sums_all[0:1] / total
        var = sums_all[1:2] / total - mean * mean
        inv = lax.rsqrt(var + norm_eps)
        ms[l, s, 0:1, :] = inv
        gain, shift = w_norm[l, 0:1, :], w_norm[l, 1:2, :]

        def body(span, carry):
            normed = (act[l, s, span, :] - mean) * inv
            act[l, s, span, :] = normed
            out[span, :] = lowered(normed * gain + shift)
            return carry

        over_rows(body, 0)
        return sums_all

    def layer_zero(s):
        high, rest = split(accx[...])
        axh[s] = high
        w = wa[:, wide : wide + span_in]
        agg[0, s] = lowered(dot(high, w, NT) + dot(rest, w, NT))
        h0[s] = lowered(dot(xg[s, me].T, w, NT))
        forward_act(s, 0, s, h0[s], agg[0, s], wa[:, :hidden], wa[:, hidden:wide])

    def layer_one(s):
        agg[1, s] = lowered(acc[...])
        forward_act(s, 1, 2 + s, hg[s, me], agg[1, s], wb[:, :hidden], wb[:, hidden:])

    def head(s, count):
        value = h2[s]
        logits = dot(wt_head[pl.ds(0, 64), :], value, NT) + bias_col
        at = lax.broadcasted_iota(jnp.int32, (64, rows), 0)
        valid = at < classes
        logits = jnp.where(valid, logits, -1e30)
        shifted = logits - jnp.max(logits, 0, keepdims=True)
        logp = shifted - jnp.log(jnp.sum(jnp.exp(shifted), 0, keepdims=True))
        onehot = jnp.where(at == labels[s : s + 1, :], 1.0, 0.0)
        target = jnp.where(valid, (1.0 - smoothing) * onehot + smoothing / classes, 0.0)
        weights = train[s : s + 1, :].astype(f32)
        node_loss = jnp.sum(target * logp, 0, keepdims=True)
        loss = -jnp.sum(weights * node_loss, axis=1, keepdims=True)
        delta = (weights / count) * (jnp.exp(logp) - target)
        delta_low = lowered(delta)
        value_t = dot(delta_low, value)
        ght[...] = value_t if s == 0 else ght[...] + value_t
        column = dot(jnp.ones((8, rows), bf16), delta_low, NT)
        tall = jnp.concatenate([delta_low.astype(f32), jnp.zeros((64, rows), f32)], 0).T
        dh[s] = lowered(dot(lowered(tall), wt_head[...])).astype(f32)
        return loss, column

    def backward_sums(s, l, k, extra=None):
        def body(span, carry):
            grad = dh[s, span, :]
            return carry[0] + fold(grad), carry[1] + fold(grad * act[l, s, span, :])

        zero = jnp.zeros((8, hidden), f32)
        one, two = over_rows(body, (zero, zero))
        lines = [jnp.sum(one, 0, keepdims=True), jnp.sum(two, 0, keepdims=True)]
        if extra is None:
            lines += [jnp.zeros((1, hidden), f32)] * 2
        else:
            rest = jnp.zeros((1, hidden - 64), f32)
            lines.append(jnp.concatenate([extra[1][0:1], rest], 1))
            lines.append(jnp.broadcast_to(extra[0], (1, hidden)))
        plane_send(k, lines)

    def backward_pre(s, l, k):
        sums_all = plane_sum(k)
        sums[1 - l] = sums_all if s == 0 else sums[1 - l] + sums_all
        gain = w_norm[l, 0:1, :]
        inv = ms[l, s, 0:1, :]
        first = gain * sums_all[0:1] / total
        second = gain * sums_all[1:2] / total

        def body(span, carry):
            grad = dh[s, span, :] * gain - first - act[l, s, span, :] * second
            dp[l, s, span, :] = lowered(grad * inv * slope[l, s, span, :])
            return carry

        over_rows(body, 0)

    def conv_grads(s, l, left, right):
        turned = dp[l, s].T
        one, two = dot(turned, left), dot(turned, right)
        if s == 0:
            gt[l, :, :hidden] = one
            gt[l, :, hidden:] = two
        else:
            gt[l, :, :hidden] += one
            gt[l, :, hidden:] += two
        return turned

    def pieces_send(k, src, dst, where):
        for node in peers:
            send(where(src, node), dst.at[me], rs_s.at[k], rs_r.at[k], g, node)
        sent.append((rs_s.at[k], dst.at[pl.ds(0, 7)]))

    def pieces_sum(k, src, dst, own):
        dst[me] = own
        drain(rs_r.at[k], dst.at[pl.ds(0, 7)])
        value = dst[0].astype(f32)
        for i in range(1, 8):
            value = value + dst[i].astype(f32)
        return value

    def conv_piece(ref, node):
        n_core, n_chip = lax.rem(node, 2), lax.div(node, 2)
        return ref.at[:, n_chip, :, pl.ds(pl.multiple_of(n_core * hidden, hidden), hidden)]

    def in_piece(ref, node):
        return ref.at[node]

    def head_piece(ref, node):
        n_core, n_chip = lax.rem(node, 2), lax.div(node, 2)
        return ref.at[n_chip, :, pl.ds(pl.multiple_of(n_core * (hidden // 2), hidden // 2), hidden // 2)]

    def over_z(k, buf):
        z_wait(k)
        value = buf[0].astype(f32)
        for i in range(1, groups):
            value = value + buf[i].astype(f32)
        return value

    def spread(k, view_of, some):
        view = view_of(me)
        for node in (n_d, n_x, n_y):
            send(view, view, ag_s.at[k], ag_r.at[2 * k], g, node)
        send(view, view, ag_s.at[k], ag_r.at[2 * k + 1], g, n_sib)
        sent.append((ag_s.at[k], some(4)))

    def spread_forward(k, view_of, some):
        drain(ag_r.at[2 * k], some(3))
        for node in (n_x, n_y, n_d):
            view = view_of(node)
            send(view, view, ag_s.at[4 + k], ag_r.at[2 * k + 1], g, n_sib)
        sent.append((ag_s.at[4 + k], some(3)))

    def spread_wait(k, some):
        drain(ag_r.at[2 * k + 1], some(4))

    head_lanes = lanes_of_core(hidden // 2)

    x_g[0][4]()
    product_x(0, 0, 3)
    x_g[0][3]()
    z_forward(0, wa)
    x_g[0][5]()
    product_x(0, 3, 4)
    x_g[1][1]()
    z_forwarded(0)
    layer_zero(0)
    x_g[1][2]()
    x_g[1][4]()
    product_x(1, 0, 3)
    x_g[1][3]()
    x_g[1][5]()
    product_x(1, 3, 4)
    count_plane = normalise(0, 0, 0, hg.at[0, me])
    h_g[0][6]()
    layer_zero(1)
    h_g[0][7]()
    zs[0, g] = count_plane
    z_send(3, zs.at[0, g], zs.at[0, others])
    z_forward(1, wb)
    normalise(1, 0, 1, hg.at[1, me])
    h_g[0][1]()
    h_g[1][0]()
    z_send(6, mpc.at[0, g], mpc.at[0, others])
    z_send(7, mpc.at[1, g], mpc.at[1, others])
    z_send(8, mit.at[own_rows], mit.at[pl.ds(0, shard * (groups - 1))])
    z_forwarded(1)
    wn[...] = wa[:, :wide].T
    h_g[0][2]()
    h_g[0][4]()
    product(0, hg.at[0], acc, 0, 3)
    h_g[0][3]()
    h_g[0][5]()
    product(0, hg.at[0], acc, 3, 4)
    layer_one(0)
    h_g[1][1]()
    z_wait(3)
    count = zs[0, 0]
    for i in range(1, groups):
        count = count + zs[0, i]
    count = count[2:3, 0:1]
    h_g[1][2]()
    normalise(0, 1, 2, h2.at[0])
    loss_row = head(0, count)
    backward_sums(0, 1, 4, loss_row)
    h_g[1][3]()
    h_g[1][4]()
    product(1, hg.at[1], acc, 0, 3)
    h_g[1][5]()
    product(1, hg.at[1], acc, 3, 4)
    layer_one(1)
    backward_pre(0, 1, 4)
    dg[0, me] = lowered(dot(dp[1, 0], wb[:, hidden:]))
    d_g[0][0]()
    dh[0] = dot(dp[1, 0], wb[:, :hidden])
    normalise(1, 1, 3, h2.at[1])
    loss_row = head(1, count)
    backward_sums(1, 1, 5, loss_row)
    d_g[0][1]()
    conv_grads(0, 1, hg[0, me], agg[1, 0])
    backward_pre(1, 1, 5)
    dg[1, me] = lowered(dot(dp[1, 1], wb[:, hidden:]))
    d_g[1][0]()
    d_g[0][2]()
    dh[1] = dot(dp[1, 1], wb[:, :hidden])
    zs[1, g] = sums[0]
    z_send(4, zs.at[1, g], zs.at[1, others])
    d_g[0][4]()
    product(0, dg.at[0], acc, 0, 3)
    d_g[0][3]()
    d_g[0][5]()
    product(0, dg.at[0], acc, 3, 4)
    dh[0] = lowered(dh[0] + acc[...]).astype(f32)
    backward_sums(0, 0, 6)
    d_g[1][1]()
    conv_grads(1, 1, hg[1, me], agg[1, 1])
    gbc[1] = lowered(gt[1]).reshape(groups, 4, part, wide)
    gbh[...] = lowered(ght[...]).reshape(4, 16, hidden)
    pieces_send(0, gbc.at[1], rsc.at[1], conv_piece)
    pieces_send(1, gbh, rsh, head_piece)
    d_g[1][2]()
    backward_pre(0, 0, 6)
    turned = conv_grads(0, 0, h0[0], agg[0, 0])
    q1[...] = dot(turned, xg[0, me], NT)
    q2[...] = dot(turned, axh[0])
    d_g[1][4]()
    product(1, dg.at[1], acc, 0, 3)
    d_g[1][3]()
    d_g[1][5]()
    product(1, dg.at[1], acc, 3, 4)
    dh[1] = lowered(dh[1] + acc[...]).astype(f32)
    backward_sums(1, 0, 7)
    zc[1, g] = lowered(pieces_sum(0, None, rsc.at[1], conv_piece(gbc.at[1], me)[...]))
    z_send(9, zc.at[1, g], zc.at[1, others])
    zh[g] = lowered(pieces_sum(1, None, rsh, head_piece(gbh, me)[...]))
    z_send(10, zh.at[g], zh.at[others])
    z_wait(6)
    z_wait(7)
    z_wait(8)
    tall_in[...] = mit[...]
    mi[...] = tall_in[...].T.reshape(8, 16, hidden)
    tall_in[...] = jnp.zeros_like(tall_in)
    backward_pre(1, 0, 7)
    turned = conv_grads(1, 0, h0[1], agg[0, 1])
    gbc[0] = lowered(gt[0]).reshape(groups, 4, part, wide)
    pieces_send(2, gbc.at[0], rsc.at[0], conv_piece)
    q1[...] += dot(turned, xg[1, me], NT)
    q2[...] += dot(turned, axh[1])
    one, two = split(q1[...]), split(q2[...])
    w_self, w_near = wn[:hidden, :], wn[hidden:, :]
    g_in = dot(w_self, one[0]) + dot(w_self, one[1]) + dot(w_near, two[0]) + dot(w_near, two[1])
    tall_in[:, pl.ds(0, span_in)] = g_in
    gbi[...] = lowered(tall_in[...].T).reshape(8, 16, hidden)
    pieces_send(3, gbi, rsi, in_piece)
    zs[2, g] = sums[1]
    z_send(5, zs.at[2, g], zs.at[2, others])

    def conv_view(l):
        return lambda node: conv_piece(mf.at[l], node)

    def conv_some(l):
        return lambda n: mf.at[l, :, pl.ds(0, n), :, pl.ds(0, hidden)]

    def head_some(n):
        return hf.at[pl.ds(0, n), :, pl.ds(0, hidden // 2)]

    def in_some(n):
        return mfi.at[pl.ds(0, n)]

    def head_view(node):
        return head_piece(hf, node)

    def in_view(node):
        return mfi.at[node]

    def scaled(value):
        norm = jnp.sqrt(jnp.sum(jnp.sum(value * value, 0, keepdims=True), 1, keepdims=True))
        return value / (norm + 1e-07)

    def iterate(refs, first, last):
        for i in range(first, last):
            for ref in refs:
                value = ref[...]
                pair = split(value)
                gram = dot_three(pair, pair, NT)
                gram_high, gram_rest = split(gram)
                cross = dot(gram_high, gram_rest)
                square = dot(gram_high, gram_high) + cross + cross.T
                poly = split(poly_second * gram + poly_third * square)
                ref[...] = poly_first * value + dot_three(poly, pair)

    factor_conv = 0.2 * float(wide) ** 0.5
    factor_in = 0.2 * float(max(width, hidden)) ** 0.5

    def conv_out(l):
        o_conv_m[l] = mf[l, g].reshape(shard, wide)
        ortho = y_conv[l, own_rows, :]
        weight = w_conv[l]
        o_conv[l] = weight - muon_rate * (factor_conv * ortho + decay_rate * weight)

    mf[1, :, chip, :, core_lanes] = muon_beta * mpc[1] + over_z(9, zc.at[1])
    spread(0, conv_view(1), conv_some(1))
    hf[chip, :, head_lanes] = over_z(10, zh)
    spread(1, head_view, head_some)
    zc[0, g] = lowered(pieces_sum(2, None, rsc.at[0], conv_piece(gbc.at[0], me)[...]))
    z_send(11, zc.at[0, g], zc.at[0, others])
    zi[g] = lowered(pieces_sum(3, None, rsi, gbi[me]))
    z_send(12, zi.at[g], zi.at[others])
    spread_forward(0, conv_view(1), conv_some(1))
    spread_forward(1, head_view, head_some)
    spread_wait(0, conv_some(1))
    y_conv[1] = scaled(mf[1].reshape(hidden, wide))
    iterate([y_conv.at[1]], 0, EARLY_STEPS)
    mf[0, :, chip, :, core_lanes] = muon_beta * mpc[0] + over_z(11, zc.at[0])
    spread(2, conv_view(0), conv_some(0))
    mfi[me] = muon_beta * mi[me] + over_z(12, zi)
    spread(3, in_view, in_some)
    iterate([y_conv.at[1]], EARLY_STEPS, NS_STEPS)
    spread_forward(2, conv_view(0), conv_some(0))
    spread_forward(3, in_view, in_some)
    conv_out(1)

    spread_wait(1, head_some)
    grad = hf[...].reshape(64, hidden)[:classes]
    o_head[...], o_head_f[...], o_head_s[...] = adamw(w_head[...], grad, f_head[...], s_head[...])
    z_wait(4)
    z_wait(5)
    late = zs[1, 0]
    early = zs[2, 0]
    for i in range(1, groups):
        late = late + zs[1, i]
        early = early + zs[2, i]
    for l, rows_l in ((0, early), (1, late)):
        grad = jnp.concatenate([rows_l[1:2], rows_l[0:1]], 0)
        o_norm[l], o_norm_f[l], o_norm_s[l] = adamw(w_norm[l], grad, f_norm[l], s_norm[l])
    o_bias[...], o_bias_f[...], o_bias_s[...] = adamw(
        w_bias[...], late[2:3, :classes], f_bias[...], s_bias[...]
    )
    o_loss[...] = jnp.concatenate([late[3:4, 0:1], count], 1)

    spread_wait(2, conv_some(0))
    spread_wait(3, in_some)
    y_conv[0] = scaled(mf[0].reshape(hidden, wide))
    y_in[...] = scaled(mfi[...].reshape(128, hidden))
    iterate([y_conv.at[0], y_in], 0, NS_STEPS)
    conv_out(0)
    tall_in[...] = mfi[...].reshape(128, hidden).T
    o_in_m[...] = tall_in[own_rows, :][:, :width]
    tall_in[...] = y_in[...].T
    ortho = tall_in[own_rows, :][:, :width]
    weight = w_in[...]
    o_in[...] = weight - muon_rate * (factor_in * ortho + decay_rate * weight)
    for sem, view in sent:
        drain(sem, view)


def planned(mesh):
    groups = mesh.shape["grp"]

    def call(
        features,
        adjacency,
        labels,
        train_mask,
        input_weight,
        input_moment,
        conv_weight,
        conv_moment,
        head_weight,
        head_first,
        head_second,
        head_bias,
        bias_first,
        bias_second,
        norm_params,
        norm_first,
        norm_second,
    ):
        f32, bf16 = jnp.float32, jnp.bfloat16
        graphs, rows, width = features.shape
        total = adjacency.shape[2]
        hidden, classes = head_weight.shape
        wide = 2 * hidden
        shard = hidden // groups
        part = shard // 4
        span_in = 16 * ((width + 15) // 16)
        vm = pltpu.VMEM
        sem = pltpu.SemaphoreType.DMA
        shape = jax.ShapeDtypeStruct
        near = pl.BlockSpec(memory_space=pltpu.VMEM)
        anywhere = pl.BlockSpec(memory_space=pl.ANY)
        results = [
            shape((1, 2), f32),
            shape((shard, width), f32),
            shape((shard, width), f32),
            shape((2, shard, wide), f32),
            shape((2, shard, wide), f32),
            shape((classes, hidden), f32),
            shape((classes, hidden), f32),
            shape((classes, hidden), f32),
            shape((1, classes), f32),
            shape((1, classes), f32),
            shape((1, classes), f32),
            shape(norm_params.shape, f32),
            shape(norm_params.shape, f32),
            shape(norm_params.shape, f32),
        ]
        outs = pl.pallas_call(
            functools.partial(step_kernel, groups, classes),
            out_shape=results,
            in_specs=[anywhere] * 17,
            out_specs=[near] * 14,
            scratch_shapes=[
                vm((graphs, rows, total), bf16),
                vm((graphs, 8, span_in, rows), bf16),
                vm((graphs, 8, rows, hidden), bf16),
                vm((graphs, 8, rows, hidden), bf16),
                vm((128, 128), f32),
                vm((128, rows), f32),
                vm((hidden, wide + 128), bf16),
                vm((hidden, wide), bf16),
                vm((wide, hidden), bf16),
                vm((128, hidden), bf16),
                vm((graphs, rows, hidden), bf16),
                vm((2, graphs, rows, hidden), bf16),
                vm((2, graphs, rows, hidden), f32),
                vm((2, graphs, rows, hidden), f32),
                vm((2, graphs, 8, hidden), f32),
                vm((graphs, rows, span_in), bf16),
                vm((rows, span_in), f32),
                vm((rows, hidden), f32),
                vm((graphs, rows, hidden), bf16),
                vm((graphs, rows, hidden), f32),
                vm((2, graphs, rows, hidden), bf16),
                vm((2, hidden, wide), f32),
                vm((hidden, span_in), f32),
                vm((hidden, span_in), f32),
                vm((hidden, 128), f32),
                vm((64, hidden), f32),
                vm((ROUNDS, 8, 8, hidden // 2), f32),
                vm((3, groups, 8, hidden), f32),
                vm((2, 8, hidden), f32),
                vm((2, groups, part, hidden), f32),
                vm((hidden, 128), f32),
                vm((8, 16, hidden), f32),
                vm((2, groups, 4, part, wide), bf16),
                vm((8, 16, hidden), bf16),
                vm((4, 16, hidden), bf16),
                vm((2, 8, groups, part, hidden), bf16),
                vm((8, 16, hidden), bf16),
                vm((8, 16, hidden // 2), bf16),
                vm((2, groups, groups, part, hidden), bf16),
                vm((groups, 16, hidden), bf16),
                vm((groups, 16, hidden // 2), bf16),
                vm((2, groups, 4, part, wide), f32),
                vm((8, 16, hidden), f32),
                vm((4, 16, hidden), f32),
                vm((2, hidden, wide), f32),
                vm((128, hidden), f32),
                vm((width, graphs, rows), bf16),
                vm((shard, width), f32),
                vm((2, shard, wide), f32),
                vm((graphs, rows), jnp.int32),
                vm((graphs, rows), jnp.int32),
                vm((shard, width), f32),
                vm((classes, hidden), f32),
                vm((classes, hidden), f32),
                vm((classes, hidden), f32),
                vm((1, classes), f32),
                vm((1, classes), f32),
                vm((1, classes), f32),
                vm(norm_params.shape, f32),
                vm(norm_params.shape, f32),
                vm(norm_params.shape, f32),
                sem((graphs + 17,)),
                sem((6,)),
                sem((30,)),
                sem((ROUNDS,)),
                sem((ROUNDS,)),
                sem((13,)),
                sem((13,)),
                sem((2,)),
                sem((2,)),
                sem((4,)),
                sem((4,)),
                sem((8,)),
                sem((8,)),
            ],
            compiler_params=pltpu.CompilerParams(
                collective_id=0, has_side_effects=True, vmem_limit_bytes=VMEM_BYTES
            ),
            name="train_step",
        )(
            jnp.transpose(features, (2, 0, 1)),
            adjacency,
            labels,
            train_mask,
            input_weight.T,
            input_moment.T,
            jnp.swapaxes(conv_weight, 1, 2),
            jnp.swapaxes(conv_moment, 1, 2),
            head_weight.T,
            head_first.T,
            head_second.T,
            head_bias[None, :],
            bias_first[None, :],
            bias_second[None, :],
            norm_params,
            norm_first,
            norm_second,
        )
        outs = pl.pallas_call(
            hand_over,
            out_shape=results,
            in_specs=[near] * 14,
            out_specs=[near] * 14,
            name="hand_over",
        )(*outs)
        loss, in_new, in_m, conv_new, conv_m, h_new, h_f, h_s, b_new, b_f, b_s, *norms = outs
        return (
            loss[0],
            in_new.T,
            in_m.T,
            jnp.swapaxes(conv_new, 1, 2),
            jnp.swapaxes(conv_m, 1, 2),
            h_new.T,
            h_f.T,
            h_s.T,
            b_new[0],
            b_f[0],
            b_s[0],
            *norms,
        )

    return call


def hand_over(*refs):
    for source, target in zip(refs[:14], refs[14:]):
        target[...] = source[...]


def solution(mesh):
    placed = (
        P("grp", "node", None),
        P("grp", "node", None),
        P("grp", "node"),
        P("grp", "node"),
        P(None, "grp"),
        P(None, "grp"),
        P(None, None, "grp"),
        P(None, None, "grp"),
        P(),
        P(),
        P(),
        P(),
        P(),
        P(),
        P(),
        P(),
        P(),
    )
    small = mesh.shape["node"] == 8 and mesh.shape["grp"] == 4
    return jax.shard_map(
        planned(mesh) if small else per_device,
        mesh=mesh,
        in_specs=placed,
        out_specs=(
            P(),
            P(None, "grp"),
            P(None, "grp"),
            P(None, None, "grp"),
            P(None, None, "grp"),
            P(),
            P(),
            P(),
            P(),
            P(),
            P(),
            P(),
            P(),
            P(),
        ),
        check_vma=False,
    )
```
